256 devices in a mesh: front: 64 (over z, y, core), rhs: 4 (over x).
Axes of the slice: x: 4, y: 4, z: 8, core: 2. Of those that a mesh axis runs over, the one named last changes fastest.
Arguments:
- right_side: float32 [32, 4, 8192], P('rhs', None, 'front'), may hold values from -6 to 6
- inverse_top: float32 [8192, 8192], P('front'), as said below
- inverse_second: float32 [8192, 4096], P('front'), as said below
- inverse_third: float32 [8192, 2048], P('front'), as said below
- inverse_fourth: float32 [8192, 1024], P('front'), as said below
- panels: float32 [3, 1024, 8192], P(None, None, 'front'), may hold values from -0.09375 to 0.09375
- targets: int32 [3, 64, 8], P(None, 'front'), may hold values from -1 to 191, as said below
Outputs:
- forward_result: float32 [32, 4, 8192], P('rhs', None, 'front')
- solution: float32 [32, 4, 8192], P('rhs', None, 'front')
The draws below stay inside these ranges and needn't reach their ends.
Inputs may be any that keep to these rules, and one draw needn't show every extreme that they name: `targets`: for tier k + 1 the devices of one front hold the same list; its live entries are distinct blocks of that front's ancestors in the window (tiers 0 to k, the blocks inside the ancestor's devices), -1 marks an unused slot, each front has 1 to 8 live entries, and on every tier some front has exactly 8. `inverse_top`: within each front of D * 128 rows, with r the row's place in the front, the block is triangular in the elimination order o(r) = (r % 128) * D + r // 128: entry (i, j) is zero when o(j) > o(i); diagonal entries in 1 to 2. `inverse_second`: triangular in the same elimination order within each front, diagonal entries in 1 to 2. `inverse_third`: triangular in the same elimination order within each front, diagonal entries in 1 to 2. `inverse_fourth`: triangular in the same elimination order within each front, diagonal entries in 1 to 2.
All inputs are finite; a program needn't handle non-finite values.
Results may differ from the reference program's by a relative error of at most 0.0001.
Values sent between devices are 32-bit elements; how exact they have to be, the bound alone decides.
A program may use at most 64 MiB of HBM per device.

```python
import jax
import jax.numpy as jnp
from jax import lax

ROWS = 128
LEVELS = 4
UMAX = 8
NRHS = 32
POSITIONS = 8192
SEP_TOP = 8192
SEP_SECOND = 4096
SEP_THIRD = 2048
SEP_FOURTH = 1024
N_FRONT = 64


def elimination_order(place, width):
    devices_front = width // ROWS
    return place % ROWS * devices_front + place // ROWS


def lower_block(noise, diagonal, width):
    row_place = jnp.arange(POSITIONS, dtype=jnp.int32) % width
    column_place = jnp.arange(width, dtype=jnp.int32)
    row_order = elimination_order(row_place, width)[:, None]
    column_order = elimination_order(column_place, width)[None, :]
    below = (column_order < row_order).astype(jnp.float32)
    on_diagonal = (column_order == row_order).astype(jnp.float32)
    scaled = noise * (1.0 / width ** 0.5)
    return below * scaled + on_diagonal * diagonal


def inverse_noise(key, width):
    noise_key, diag_key = jax.random.split(key)
    noise = jax.random.normal(noise_key, (POSITIONS, width), jnp.float32)
    diagonal = jax.random.uniform(diag_key, (POSITIONS, 1), jnp.float32, 1.0, 2.0)
    return lower_block(noise, diagonal, width)


def draw_inverse_top(key, part):
    key = jax.random.fold_in(key, 3)
    return inverse_noise(key, SEP_TOP)


def draw_inverse_second(key, part):
    key = jax.random.fold_in(key, 5)
    return inverse_noise(key, SEP_SECOND)


def draw_inverse_third(key, part):
    key = jax.random.fold_in(key, 7)
    return inverse_noise(key, SEP_THIRD)


def draw_inverse_fourth(key, part):
    key = jax.random.fold_in(key, 9)
    return inverse_noise(key, SEP_FOURTH)


def draw_targets(key, part):
    key = jax.random.fold_in(key, 11)
    fronts_mesh = POSITIONS // ROWS
    tier_lists = []
    for height in range(1, LEVELS):
        group_size = fronts_mesh >> height
        front_count = 1 << height
        spans_above = [fronts_mesh >> tier for tier in range(height)]
        candidates = sum(spans_above)
        tier_key = jax.random.fold_in(key, height)

        def one_front(front_number, front_key):
            chosen = jax.random.permutation(front_key, candidates)[:UMAX].astype(jnp.int32)
            block_list = jnp.full((UMAX,), -1, jnp.int32)
            lowest = 0
            for tier in range(height):
                width_here = spans_above[tier]
                within = (chosen >= lowest) & (chosen < lowest + width_here)
                first_block = (front_number >> height - tier) * width_here
                block_list = jnp.where(within, tier * fronts_mesh + first_block + chosen - lowest, block_list)
                lowest = lowest + width_here
            return block_list
        front_keys = jax.random.split(tier_key, front_count)
        front_numbers = jnp.arange(front_count, dtype=jnp.int32)
        block_lists = jax.vmap(one_front)(front_numbers, front_keys)
        live_counts = jax.random.randint(jax.random.fold_in(tier_key, 99), (front_count,), 1, UMAX + 1)
        full_front = jax.random.randint(jax.random.fold_in(tier_key, 98), (), 0, front_count)
        live_counts = jnp.where(front_numbers == full_front, UMAX, live_counts)
        slot_index = jnp.arange(UMAX, dtype=jnp.int32)[None, :]
        block_lists = jnp.where(slot_index < live_counts[:, None], block_lists, -1)
        tier_lists.append(jnp.repeat(block_lists, group_size, axis=0))
    return jnp.stack(tier_lists).astype(jnp.int32)


def block_levels(rng, shape, cuts, smallest, high):
    gain, own = 1.0, jax.random.fold_in(rng, 6)
    for dim, blocks in cuts:
        steps = jnp.exp(jax.random.uniform(jax.random.fold_in(own, dim), (blocks,), jnp.float32, smallest / len(cuts), high / len(cuts)))
        gain = gain * jnp.repeat(steps, shape[dim] // blocks).reshape([-1 if axis == dim else 1 for axis in range(len(shape))])
    return gain


def scatter_about(own_key, shape, scale, most, cuts=(), held_as=jnp.bfloat16):
    array = scale * jax.random.normal(own_key, shape, jnp.float32)
    if cuts:
        array = array * block_levels(own_key, shape, cuts, -0.22, 0.18)
    return jnp.clip(array, -most, most).astype(held_as)


def setup_inputs(seed: int = 0) -> dict:
    arg_keys = jax.random.split(jax.random.key(seed), 8)
    right_side = scatter_about(arg_keys[0], (NRHS, LEVELS, POSITIONS), 1.0, 6.0, ((0, 4), (2, 64)), jnp.float32)
    inverse_top = draw_inverse_top(jax.random.fold_in(arg_keys[7], 71), 0)
    inverse_second = draw_inverse_second(jax.random.fold_in(arg_keys[7], 71), 0)
    inverse_third = draw_inverse_third(jax.random.fold_in(arg_keys[7], 71), 0)
    inverse_fourth = draw_inverse_fourth(jax.random.fold_in(arg_keys[7], 71), 0)
    panels = scatter_about(arg_keys[5], (LEVELS - 1, UMAX * ROWS, POSITIONS), (4 * SEP_FOURTH) ** -0.5, 0.09375, ((2, 64),), jnp.float32)
    targets = draw_targets(jax.random.fold_in(arg_keys[7], 71), 0)
    return {"right_side": right_side, "inverse_top": inverse_top, "inverse_second": inverse_second, "inverse_third": inverse_third, "inverse_fourth": inverse_fourth, "panels": panels, "targets": targets}


def reference(right_side, inverse_top, inverse_second, inverse_third, inverse_fourth, panels, targets):
    highest = lax.Precision.HIGHEST
    inverses = [inverse_top, inverse_second, inverse_third, inverse_fourth]
    positions = ROWS * N_FRONT
    count_rhs = right_side.shape[0]
    blocks_all = (LEVELS - 1) * N_FRONT
    block_ids = jnp.arange(blocks_all, dtype=jnp.int32)
    incoming = [jnp.zeros((count_rhs, positions), jnp.float32) for height in range(LEVELS)]
    forward_list = [None] * LEVELS
    hit_tables = [None] * LEVELS
    for height in range(LEVELS - 1, -1, -1):
        front_count = 1 << height
        span_rows = positions // front_count
        group_size = N_FRONT >> height
        grouped = (right_side[:, height, :] - incoming[height]).reshape(count_rhs, front_count, span_rows)
        inverse_blocks = inverses[height].reshape(front_count, span_rows, span_rows)
        forward_part = jnp.einsum('nfj,fij->nfi', grouped, inverse_blocks, precision=highest)
        forward_list[height] = forward_part.reshape(count_rhs, positions)
        if height > 0:
            panel_blocks = panels[height - 1].reshape(UMAX * ROWS, front_count, span_rows)
            update_terms = jnp.einsum('nfj,afj->nfa', forward_part, panel_blocks, precision=highest)
            update_terms = update_terms.reshape(count_rhs, front_count, UMAX, ROWS)
            front_targets = targets[height - 1].reshape(front_count, group_size, UMAX)[:, 0, :]
            hit_table = (front_targets[:, :, None] == block_ids[None, None, :]).astype(jnp.float32)
            hit_tables[height] = hit_table
            landed = jnp.einsum('fub,nfur->nbr', hit_table, update_terms, precision=highest)
            landed = landed.reshape(count_rhs, LEVELS - 1, positions)
            for ancestor in range(LEVELS - 1):
                incoming[ancestor] = incoming[ancestor] + landed[:, ancestor, :]
    solution_list = [None] * LEVELS
    for height in range(LEVELS):
        front_count = 1 << height
        span_rows = positions // front_count
        reduced = forward_list[height].reshape(count_rhs, front_count, span_rows)
        if height > 0:
            known = jnp.stack(solution_list[:LEVELS - 1] if height == LEVELS else
                              [solution_list[tier] if tier < height else jnp.zeros((count_rhs, positions), jnp.float32)
                               for tier in range(LEVELS - 1)], axis=1)
            known = known.reshape(count_rhs, blocks_all, ROWS)
            picked = jnp.einsum('fub,nbr->nfur', hit_tables[height], known, precision=highest)
            picked = picked.reshape(count_rhs, front_count, UMAX * ROWS)
            panel_blocks = panels[height - 1].reshape(UMAX * ROWS, front_count, span_rows)
            back_terms = jnp.einsum('nfa,afj->nfj', picked, panel_blocks, precision=highest)
            reduced = reduced - back_terms
        inverse_blocks = inverses[height].reshape(front_count, span_rows, span_rows)
        solved = jnp.einsum('nfi,fij->nfj', reduced, inverse_blocks, precision=highest)
        solution_list[height] = solved.reshape(count_rhs, positions)
    return jnp.stack(forward_list, axis=1), jnp.stack(solution_list, axis=1)
```

```python
import functools

import jax
import jax.numpy as jnp
from jax import lax
from jax.experimental import pallas as pl
from jax.experimental.pallas import tpu as pltpu
from jax.sharding import PartitionSpec as P

F32 = jnp.float32
BF16 = jnp.bfloat16
I32 = jnp.int32
MESH = pl.DeviceIdType.MESH
TIERS = 4
SLOTS = 8
BLOCKS = (64, 32, 16, 8)
PLANES = (8, 4, 2, 1)
TRANSPOSED = (((1,), (1,)), ((), ()))
NATURAL = (((1,), (0,)), ((), ()))


def split_rows(value):
    high = value.astype(BF16).astype(F32)
    return jnp.concatenate([high, value - high], axis=0).astype(BF16)


def fold_rows(value):
    return value[:8] + value[8:]


def fold_all(value):
    rows = fold_rows(value)
    return rows[:, :128] + rows[:, 128:]


def doubled(value):
    halves = split_rows(value)
    return jnp.concatenate([halves, halves], axis=1)


def matmul(left, right, dims):
    return lax.dot_general(left, right, dims, preferred_element_type=F32)


class Stage:
    def __init__(self):
        self.count = 0

    def take(self):
        self.count += 1
        return self.count - 1


STAGE_COUNT = 48

SCRATCH = dict(
    v0=((128, 8192), F32), v1=((128, 4096), F32), v2=((128, 2048), F32), v3=((128, 1024), F32),
    vp=((3, 1024, 128), F32),
    c0=((64, 256, 128), BF16), c1=((32, 256, 128), BF16), c2=((16, 256, 128), BF16), c3=((8, 256, 128), BF16),
    pc=((3, 1024, 256), BF16),
    rb0=((8, 8, 8, 128), F32), rb1=((4, 8, 8, 128), F32), rb2=((2, 8, 8, 128), F32), rb3=((1, 8, 8, 128), F32),
    tgv=((8, 8, 128), I32),
    up3=((4, 2, 8, 128), F32), up2=((4, 2, 8, 128), F32), up1=((4, 2, 8, 128), F32),
    ur3=((8, 2, 8, 128), F32), ur2=((8, 2, 8, 128), F32), ur1=((8, 2, 8, 128), F32),
    us3=((2, 8, 128), F32), us2=((2, 8, 128), F32), us1=((2, 8, 128), F32),
    uz3=((8, 2, 8, 128), F32), uz2=((8, 2, 8, 128), F32), uz2b=((4, 2, 8, 128), F32), uz1=((8, 2, 8, 128), F32),
    s3p=((2, 8, 8, 128), F32), s3q=((6, 8, 8, 128), F32),
    s2p=((2, 8, 8, 128), F32), s2q=((2, 8, 8, 128), F32), s1p=((2, 8, 8, 128), F32),
    st2=((2, 2, 8, 128), F32), st2b=((2, 2, 8, 128), F32), st1=((2, 2, 8, 128), F32),
    a1=((4, 2, 2, 8, 128), F32), a2=((4, 2, 2, 8, 128), F32), a3=((4, 2, 2, 8, 128), F32),
    ar1=((8, 2, 2, 8, 128), F32), ar2=((8, 2, 2, 8, 128), F32), ar3=((8, 2, 2, 8, 128), F32),
    as1=((2, 2, 8, 128), F32), as2=((2, 2, 8, 128), F32), as3=((2, 2, 8, 128), F32),
    az1=((8, 2, 8, 128), F32), az2=((4, 2, 8, 128), F32), az3=((2, 2, 8, 128), F32),
    pt1=((2, 8, 128), F32), pt2=((2, 8, 128), F32), pt3=((2, 8, 128), F32),
    pk1=((8, 8, 128), F32), pk2=((8, 8, 128), F32), pk3=((8, 8, 128), F32),
    n0=((4, 12, 2, 8, 128), F32), nr0=((8, 12, 2, 8, 128), F32), ns0=((8, 2, 2, 8, 128), F32), nz0=((8, 2, 2, 8, 128), F32),
    n1=((4, 4, 2, 8, 128), F32), nr1=((8, 4, 2, 8, 128), F32), ns1=((4, 2, 8, 128), F32), nz1=((4, 2, 8, 128), F32),
    t0p=((2, 2, 8, 128), F32), t1p=((2, 8, 128), F32),
    sd0=((8, 8, 8, 128), F32), sd1=((8, 4, 8, 128), F32), sd2=((8, 2, 8, 128), F32), sd3=((8, 1, 8, 128), F32),
    dr0=((8, 8, 8, 128), F32), dr1=((8, 4, 8, 128), F32), dr2=((8, 2, 8, 128), F32), dr3=((8, 1, 8, 128), F32),
    ds0=((8, 8, 128), F32), ds1=((4, 8, 128), F32), ds2=((2, 8, 128), F32),
    dz0=((8, 8, 128), F32), dz1=((4, 8, 128), F32), dz2=((2, 8, 128), F32),
    fk=((4, 8, 128), F32),
    dummy=((168, 8, 128), F32),
)


def kernel(rs_ref, i0_ref, i1_ref, i2_ref, i3_ref, pn_ref, tg_ref, fo_ref, so_ref, *scratch):
    names = list(SCRATCH)
    ref = dict(zip(names, scratch[: len(names)]))
    tgs, send_sem, recv_sem, load_sem = scratch[len(names) :]
    front = lax.axis_index("front")
    core = front % 2
    chip_y = (front // 2) % 4
    d = front % 8
    z = front // 8
    is_one = core == 1
    stage = Stage()
    drains = []

    def put(src, dst, st, to):
        pltpu.make_async_remote_copy(
            src_ref=src, dst_ref=dst, send_sem=send_sem.at[st], recv_sem=recv_sem.at[st],
            device_id={"front": to}, device_id_type=MESH,
        ).start()

    def drain(sem, blocks):
        piece = ref["dummy"].at[pl.ds(0, blocks)]
        pltpu.make_async_copy(piece, piece, sem).wait()

    def arrived(st, blocks):
        drain(recv_sem.at[st], blocks)

    def arrived_by_core(st, blocks_zero, blocks_one):
        @pl.when(is_one)
        def _():
            arrived(st, blocks_one)

        @pl.when(jnp.logical_not(is_one))
        def _():
            arrived(st, blocks_zero)

    loads = {}
    for number, (name, src) in enumerate(
        (("v3", i3_ref), ("p3", pn_ref.at[2]), ("v2", i2_ref), ("p2", pn_ref.at[1]),
         ("v1", i1_ref), ("p1", pn_ref.at[0]), ("v0", i0_ref))
    ):
        dst = ref["vp"].at[int(name[1]) - 1] if name[0] == "p" else ref[name]
        loads[name] = pltpu.make_async_copy(src, dst, load_sem.at[number])
        loads[name].start()

    barrier = pltpu.get_barrier_semaphore()
    masks = list(range(1, 16)) + [8 * m for m in range(2, 8)]
    for mask in masks:
        pl.semaphore_signal(barrier, inc=1, device_id={"front": front ^ mask}, device_id_type=MESH)

    rb = [ref["rb0"], ref["rb1"], ref["rb2"], ref["rb3"]]
    zz = [z, z % 4, z % 2, 0]
    for t in range(TIERS):
        rb[t][zz[t], d] = rs_ref[:, t, :]
    lanes = lax.broadcasted_iota(I32, (8, 128), 1)
    own_targets = jnp.full((8, 128), -1, I32)
    for k in range(3):
        for u in range(SLOTS):
            own_targets = jnp.where(lanes == k * 8 + u, tg_ref[k, 0, u], own_targets)
    ref["tgv"][z] = own_targets

    pl.semaphore_wait(barrier, len(masks))

    st_r3 = stage.take()
    for mask in (4, 5, 2, 3, 6, 7, 1):
        put(rb[3].at[0, d], rb[3].at[0, d], st_r3, front ^ mask)
    drains.append((st_r3, 7, 7))
    st_tg = stage.take()
    st_rz = [stage.take() for t in range(3)]
    put(rb[2].at[z % 2, d], rb[2].at[z % 2, d], st_rz[2], front ^ 8)
    drains.append((st_rz[2], 1, 1))
    for m in range(1, 8):
        put(ref["tgv"].at[z], ref["tgv"].at[z], st_tg, front ^ (8 * m))
    drains.append((st_tg, 7, 7))
    for t, count in ((1, 4), (0, 8)):
        for m in range(1, count):
            put(rb[t].at[zz[t], d], rb[t].at[zz[t], d], st_rz[t], front ^ (8 * m))
        drains.append((st_rz[t], count - 1, count - 1))

    cc = [ref["c0"], ref["c1"], ref["c2"], ref["c3"]]
    vv = [ref["v0"], ref["v1"], ref["v2"], ref["v3"]]

    def prepare_inverse(t):
        loads["v" + str(t)].wait()

        def body(e, carry):
            block = vv[t][:, pl.ds(pl.multiple_of(e * 128, 128), 128)]
            high = block.astype(BF16)
            cc[t][e, 0:128, :] = high
            cc[t][e, 128:256, :] = (block - high.astype(F32)).astype(BF16)
            return carry

        lax.fori_loop(0, BLOCKS[t], body, 0)

    def prepare_panel(t):
        loads["p" + str(t)].wait()

        def body(u, carry):
            rows = pl.ds(pl.multiple_of(u * 128, 128), 128)
            block = ref["vp"][t - 1, rows, :]
            high = block.astype(BF16)
            ref["pc"][t - 1, rows, 0:128] = high
            ref["pc"][t - 1, rows, 128:256] = (block - high.astype(F32)).astype(BF16)
            return carry

        lax.fori_loop(0, SLOTS, body, 0)

    def target(m, k, u):
        return tgs[z ^ m, 0, k * 8 + u]

    def dense_forward(t):
        def chunk(index):
            x = jnp.concatenate([rb[t][index, j] for j in range(8)], axis=1)
            w = jnp.concatenate([cc[t][index * 8 + j] for j in range(8)], axis=1)
            return fold_all(matmul(split_rows(x), w, TRANSPOSED))

        if PLANES[t] == 1:
            return chunk(0)
        return lax.fori_loop(0, PLANES[t], lambda i, total: total + chunk(i), jnp.zeros((8, 128), F32))

    def slots_forward(t, k, m, block_of):
        parts, weights = [], []
        for u in range(SLOTS):
            tag = target(m, k, u)
            live = jnp.where((tag >> 6) == t, 1.0, 0.0).astype(F32)
            parts.append(block_of(u) * live)
            weights.append(cc[t][tag & (BLOCKS[t] - 1)])
        x = jnp.concatenate(parts, axis=1)
        w = jnp.concatenate(weights, axis=1)
        return fold_all(matmul(split_rows(x), w, TRANSPOSED))

    def panel_forward(t, value, out):
        terms = fold_rows(matmul(doubled(value), ref["pc"][t - 1], TRANSPOSED))
        for u in range(SLOTS):
            out[u // 2, u % 2] = terms[:, u * 128 : (u + 1) * 128]

    def panel_backward(t, picked):
        x = jnp.concatenate([picked[u] for u in range(SLOTS)], axis=1)
        return fold_all(matmul(split_rows(x), ref["pc"][t - 1], NATURAL))

    def dense_backward(t, value2, out):
        def chunk(index, carry):
            w = jnp.concatenate([cc[t][index * 8 + j] for j in range(8)], axis=1)
            terms = fold_rows(matmul(value2, w, NATURAL))
            for j in range(8):
                out[j, index] = terms[:, j * 128 : (j + 1) * 128]
            return carry

        if PLANES[t] == 1:
            chunk(0, 0)
        else:
            lax.fori_loop(0, PLANES[t], chunk, 0)

    def slots_backward(t, k, m, value2, out, place):
        weights, lives = [], []
        for u in range(SLOTS):
            tag = target(m, k, u)
            lives.append(jnp.where((tag >> 6) == t, 1.0, 0.0).astype(F32))
            weights.append(cc[t][tag & (BLOCKS[t] - 1)])
        w = jnp.concatenate(weights, axis=1)
        terms = fold_rows(matmul(value2, w, NATURAL))
        for u in range(SLOTS):
            out[u // 2, place, u % 2] = terms[:, u * 128 : (u + 1) * 128] * lives[u]

    def reduce_send(out, into, blocks):
        st = stage.take()
        for k in (2, 1, 3):
            put(out.at[chip_y ^ k], into.at[d], st, (front ^ (2 * k)) | 1)

        @pl.when(jnp.logical_not(is_one))
        def _():
            put(out.at[chip_y], into.at[d], st, front ^ 1)

        drains.append((st, 4 * blocks, 3 * blocks))
        return st

    def reduced(st, out, into, blocks, index):
        total = out[(chip_y,) + index]
        for k in range(1, 8):
            total = total + into[(d ^ k,) + index]
        return total

    def spread(src, dst, blocks):
        st = stage.take()
        for mask in (4, 5, 2, 3, 6, 7, 1):
            put(src, dst, st, front ^ mask)
        drains.append((st, 0, 7 * blocks))
        return st

    def on_one(body):
        pl.when(is_one)(body)

    pair = pl.ds(2 * chip_y, 2)

    prepare_inverse(3)
    prepare_panel(3)
    arrived(st_r3, 7)
    forward3 = dense_forward(3)
    panel_forward(3, forward3, ref["up3"])
    st = reduce_send(ref["up3"], ref["ur3"], 2)
    fo_ref[:, 3, :] = forward3
    ref["fk"][3] = forward3
    arrived(st_tg, 7)
    targets_copy = pltpu.make_async_copy(ref["tgv"], tgs, load_sem.at[7])
    targets_copy.start()
    arrived(st_rz[2], 1)
    st_rp = [None] * 3

    def plane_gather(t):
        st_rp[t] = stage.take()
        for mask in (4, 5, 2, 3, 6, 7, 1):
            put(rb[t].at[:, d], rb[t].at[:, d], st_rp[t], front ^ mask)
        drains.append((st_rp[t], 7 * PLANES[t], 7 * PLANES[t]))

    plane_gather(2)
    prepare_inverse(2)
    targets_copy.wait()
    st_s3 = stage.take()
    st_z3 = stage.take()

    @on_one
    def _():
        arrived(st, 14)
        for i in range(2):
            total = reduced(st, ref["up3"], ref["ur3"], 2, (i,))
            ref["us3"][i] = total
            ref["s3p"][0, 2 * chip_y + i] = total
        for mask in (12, 13, 10, 11, 14, 15, 8, 9):
            put(ref["us3"], ref["s3p"].at[1, pair], st_s3, front ^ mask)
        for mask in (4, 5, 2, 3, 6, 7, 1):
            put(ref["us3"], ref["s3p"].at[0, pair], st_s3, front ^ mask)
        for m in range(2, 8):
            put(ref["us3"], ref["uz3"].at[m], st_z3, front ^ (8 * m))

    drains.append((st_s3, 0, 30))
    drains.append((st_z3, 0, 12))
    prepare_panel(2)
    arrived(st_rp[2], 14)
    base2 = dense_forward(2)
    arrived_by_core(st_s3, 16, 14)

    forward2 = base2
    for m in range(2):
        forward2 = forward2 - slots_forward(2, 2, m, lambda u, m=m: ref["s3p"][m, u])
    panel_forward(2, forward2, ref["up2"])
    st = reduce_send(ref["up2"], ref["ur2"], 2)
    fo_ref[:, 2, :] = forward2
    ref["fk"][2] = forward2
    arrived(st_rz[1], 3)
    plane_gather(1)
    prepare_inverse(1)
    st_q3 = stage.take()

    @on_one
    def _():
        arrived(st_z3, 12)
        for m in range(2, 8):
            for i in range(2):
                ref["s3q"][m - 2, 2 * chip_y + i] = ref["uz3"][m, i]
        for mask in (4, 5, 2, 3, 6, 7, 1):
            put(ref["uz3"].at[pl.ds(2, 6)], ref["s3q"].at[:, pair], st_q3, front ^ mask)

    drains.append((st_q3, 0, 84))
    st_z2 = stage.take()
    st_z2b = stage.take()

    @on_one
    def _():
        arrived(st, 14)
        for i in range(2):
            ref["us2"][i] = reduced(st, ref["up2"], ref["ur2"], 2, (i,))
        for m in (2, 3, 1):
            put(ref["us2"], ref["uz2"].at[m], st_z2, front ^ (8 * m))
        for m in range(4, 8):
            put(ref["us2"], ref["uz2b"].at[m - 4], st_z2b, front ^ (8 * m))

    drains.append((st_z2, 0, 6))
    drains.append((st_z2b, 0, 8))
    prepare_panel(1)
    arrived(st_rp[1], 28)
    base1 = dense_forward(1)
    arrived(st_rz[0], 7)
    plane_gather(0)
    st_s2 = stage.take()

    @on_one
    def _():
        arrived(st_z2, 6)
        for i in range(2):
            own = ref["us2"][i] + ref["uz2"][1, i]
            other = ref["uz2"][2, i] + ref["uz2"][3, i]
            for h, total in ((0, own), (1, other)):
                ref["st2"][h, i] = total
                ref["s2p"][h, 2 * chip_y + i] = total
        for mask in (4, 5, 2, 3, 6, 7, 1):
            put(ref["st2"], ref["s2p"].at[:, pair], st_s2, front ^ mask)

    drains.append((st_s2, 0, 28))
    arrived_by_core(st_q3, 48, 36)
    for m in range(4):
        src = ref["s3p"].at[m] if m < 2 else ref["s3q"].at[m - 2]
        base1 = base1 - slots_forward(1, 2, m, lambda u, src=src: src[u])
    arrived_by_core(st_s2, 16, 12)

    forward1 = base1
    for h in range(2):
        forward1 = forward1 - slots_forward(1, 1, 2 * h, lambda u, h=h: ref["s2p"][h, u])
    panel_forward(1, forward1, ref["up1"])
    st = reduce_send(ref["up1"], ref["ur1"], 2)
    fo_ref[:, 1, :] = forward1
    ref["fk"][1] = forward1
    prepare_inverse(0)
    st_z1 = stage.take()

    @on_one
    def _():
        arrived(st, 14)
        for i in range(2):
            ref["us1"][i] = reduced(st, ref["up1"], ref["ur1"], 2, (i,))
        for m in (4, 5, 3, 6, 2, 7, 1):
            put(ref["us1"], ref["uz1"].at[m], st_z1, front ^ (8 * m))

    drains.append((st_z1, 0, 14))
    st_q2 = stage.take()

    @on_one
    def _():
        arrived(st_z2b, 8)
        for i in range(2):
            for h in range(2):
                total = ref["uz2b"][2 * h, i] + ref["uz2b"][2 * h + 1, i]
                ref["st2b"][h, i] = total
                ref["s2q"][h, 2 * chip_y + i] = total
        for mask in (4, 5, 2, 3, 6, 7, 1):
            put(ref["st2b"], ref["s2q"].at[:, pair], st_q2, front ^ mask)

    drains.append((st_q2, 0, 28))
    arrived(st_rp[0], 56)
    base0 = dense_forward(0)
    for h in range(2):
        base0 = base0 - slots_forward(0, 1, 2 * h, lambda u, h=h: ref["s2p"][h, u])
    st_s1 = stage.take()

    @on_one
    def _():
        arrived(st_z1, 14)
        for i in range(2):
            own = ref["us1"][i]
            for m in range(1, 4):
                own = own + ref["uz1"][m, i]
            other = ref["uz1"][4, i]
            for m in range(5, 8):
                other = other + ref["uz1"][m, i]
            for h, total in ((0, own), (1, other)):
                ref["st1"][h, i] = total
                ref["s1p"][h, 2 * chip_y + i] = total
        for mask in (4, 5, 2, 3, 6, 7, 1):
            put(ref["st1"], ref["s1p"].at[:, pair], st_s1, front ^ mask)

    drains.append((st_s1, 0, 28))
    for m in range(2):
        base0 = base0 - slots_forward(0, 2, m, lambda u, m=m: ref["s3p"][m, u])
    base0 = lax.fori_loop(
        0, 6, lambda m, total: total - slots_forward(0, 2, m + 2, lambda u: ref["s3q"][m, u]), base0
    )
    arrived_by_core(st_q2, 16, 12)
    for h in range(2):
        base0 = base0 - slots_forward(0, 1, 4 + 2 * h, lambda u, h=h: ref["s2q"][h, u])
    arrived_by_core(st_s1, 16, 12)

    forward0 = base0
    for h in range(2):
        forward0 = forward0 - slots_forward(0, 0, 4 * h, lambda u, h=h: ref["s1p"][h, u])

    value2 = doubled(forward0)
    for h in range(2):
        slots_backward(0, 0, 4 * h, value2, ref["a1"], h)
    st = reduce_send(ref["a1"], ref["ar1"], 4)
    fo_ref[:, 0, :] = forward0
    dense_backward(0, value2, ref["sd0"])
    for j in range(12):
        k = 1 if j < 4 else 2
        m = 2 * j if j < 4 else j - 4
        for u in range(SLOTS):
            tag = target(m, k, u)
            live = jnp.where((tag >> 6) == 0, 1.0, 0.0).astype(F32)
            ref["n0"][u // 2, j, u % 2] = ref["sd0"][tag & 7, (tag >> 3) & 7] * live
    st_n0 = reduce_send(ref["n0"], ref["nr0"], 24)

    def dense_send(out, into, blocks):
        st_d = stage.take()
        for mask in (4, 5, 2, 3, 6, 7, 1):
            put(out.at[d ^ mask], into.at[mask], st_d, front ^ mask)
        drains.append((st_d, 7 * blocks, 7 * blocks))
        return st_d

    def dense_total(out, into, index):
        total = out[d, index]
        for mask in range(1, 8):
            total = total + into[mask, index]
        return total

    st_d0 = dense_send(ref["sd0"], ref["dr0"], 8)
    st_z = stage.take()

    @on_one
    def _():
        arrived(st, 28)
        for h in range(2):
            for i in range(2):
                ref["as1"][h, i] = reduced(st, ref["a1"], ref["ar1"], 4, (h, i))
        for m in (4, 5, 3, 6, 2, 7, 1):
            put(ref["as1"].at[m >> 2], ref["az1"].at[m], st_z, front ^ (8 * m))

    drains.append((st_z, 0, 14))
    st_p = stage.take()

    @on_one
    def _():
        arrived(st_z, 14)
        for i in range(2):
            total = ref["as1"][0, i]
            for m in range(1, 8):
                total = total + ref["az1"][m, i]
            ref["pt1"][i] = total
            ref["pk1"][2 * chip_y + i] = total
        for mask in (4, 5, 2, 3, 6, 7, 1):
            put(ref["pt1"], ref["pk1"].at[pair], st_p, front ^ mask)

    drains.append((st_p, 0, 14))
    st_nz0 = stage.take()

    @on_one
    def _():
        arrived(st_n0, 168)

        def body(m, carry):
            for i in range(2):
                ref["ns0"][m, 0, i] = reduced(st_n0, ref["n0"], ref["nr0"], 24, (m // 2, i))
                ref["ns0"][m, 1, i] = reduced(st_n0, ref["n0"], ref["nr0"], 24, (4 + m, i))
            return carry

        lax.fori_loop(0, 8, body, 0)
        for m in range(1, 8):
            put(ref["ns0"].at[m], ref["nz0"].at[m], st_nz0, front ^ (8 * m))

    drains.append((st_nz0, 0, 28))
    arrived_by_core(st_p, 8, 6)

    value2 = doubled(ref["fk"][1] - panel_backward(1, ref["pk1"]))
    for h in range(2):
        slots_backward(1, 1, 2 * h, value2, ref["a2"], h)
    st = reduce_send(ref["a2"], ref["ar2"], 4)
    dense_backward(1, value2, ref["sd1"])
    for m in range(4):
        for u in range(SLOTS):
            tag = target(m, 2, u)
            live = jnp.where((tag >> 6) == 1, 1.0, 0.0).astype(F32)
            ref["n1"][u // 2, m, u % 2] = ref["sd1"][tag & 7, (tag >> 3) & 3] * live
    st_n1 = reduce_send(ref["n1"], ref["nr1"], 8)
    st_d1 = dense_send(ref["sd1"], ref["dr1"], 4)

    st_z = stage.take()

    @on_one
    def _():
        arrived(st, 28)
        for h in range(2):
            for i in range(2):
                ref["as2"][h, i] = reduced(st, ref["a2"], ref["ar2"], 4, (h, i))
        for m in (2, 3, 1):
            put(ref["as2"].at[m >> 1], ref["az2"].at[m], st_z, front ^ (8 * m))

    drains.append((st_z, 0, 6))

    @on_one
    def _():
        arrived(st_nz0, 28)
        for q in range(2):
            for i in range(2):
                total = ref["ns0"][0, q, i]
                for m in range(1, 8):
                    total = total + ref["nz0"][m, q, i]
                ref["t0p"][q, i] = total

    st_p = stage.take()

    @on_one
    def _():
        arrived(st_z, 6)
        for i in range(2):
            total = ref["as2"][0, i] + ref["t0p"][0, i]
            for m in range(1, 4):
                total = total + ref["az2"][m, i]
            ref["pt2"][i] = total
            ref["pk2"][2 * chip_y + i] = total
        for mask in (4, 5, 2, 3, 6, 7, 1):
            put(ref["pt2"], ref["pk2"].at[pair], st_p, front ^ mask)

    drains.append((st_p, 0, 14))
    st_nz1 = stage.take()

    @on_one
    def _():
        arrived(st_n1, 56)
        for m in range(4):
            for i in range(2):
                ref["ns1"][m, i] = reduced(st_n1, ref["n1"], ref["nr1"], 8, (m, i))
        for m in range(1, 4):
            put(ref["ns1"].at[m], ref["nz1"].at[m], st_nz1, front ^ (8 * m))

    drains.append((st_nz1, 0, 6))

    st_dz0 = stage.take()
    arrived(st_d0, 56)
    for w in range(8):
        ref["ds0"][w] = dense_total(ref["sd0"], ref["dr0"], w)
    for m in range(1, 8):
        put(ref["ds0"].at[z ^ m], ref["dz0"].at[m], st_dz0, front ^ (8 * m))
    drains.append((st_dz0, 7, 7))
    arrived_by_core(st_p, 8, 6)

    value2 = doubled(ref["fk"][2] - panel_backward(2, ref["pk2"]))
    for h in range(2):
        slots_backward(2, 2, h, value2, ref["a3"], h)
    st = reduce_send(ref["a3"], ref["ar3"], 4)
    dense_backward(2, value2, ref["sd2"])
    st_d2 = dense_send(ref["sd2"], ref["dr2"], 2)

    st_z = stage.take()

    @on_one
    def _():
        arrived(st, 28)
        for h in range(2):
            for i in range(2):
                ref["as3"][h, i] = reduced(st, ref["a3"], ref["ar3"], 4, (h, i))
        put(ref["as3"].at[1], ref["az3"].at[1], st_z, front ^ 8)

    drains.append((st_z, 0, 2))

    @on_one
    def _():
        arrived(st_nz1, 6)
        for i in range(2):
            total = ref["ns1"][0, i] + ref["t0p"][1, i]
            for m in range(1, 4):
                total = total + ref["nz1"][m, i]
            ref["t1p"][i] = total

    st_p = stage.take()

    @on_one
    def _():
        arrived(st_z, 2)
        for i in range(2):
            total = ref["as3"][0, i] + ref["t1p"][i] + ref["az3"][1, i]
            ref["pt3"][i] = total
            ref["pk3"][2 * chip_y + i] = total
        for mask in (4, 5, 2, 3, 6, 7, 1):
            put(ref["pt3"], ref["pk3"].at[pair], st_p, front ^ mask)

    drains.append((st_p, 0, 14))
    st_dz1 = stage.take()
    arrived(st_d1, 28)
    for w in range(4):
        ref["ds1"][w] = dense_total(ref["sd1"], ref["dr1"], w)
    for m in range(1, 4):
        put(ref["ds1"].at[(z ^ m) % 4], ref["dz1"].at[m], st_dz1, front ^ (8 * m))
    drains.append((st_dz1, 3, 3))
    st_dz2 = stage.take()
    arrived(st_d2, 14)
    for w in range(2):
        ref["ds2"][w] = dense_total(ref["sd2"], ref["dr2"], w)
    put(ref["ds2"].at[(z ^ 1) % 2], ref["dz2"].at[1], st_dz2, front ^ 8)
    drains.append((st_dz2, 1, 1))
    arrived(st_dz0, 7)
    total = ref["ds0"][z]
    for m in range(1, 8):
        total = total + ref["dz0"][m]
    so_ref[:, 0, :] = total
    arrived_by_core(st_p, 8, 6)

    value2 = doubled(ref["fk"][3] - panel_backward(3, ref["pk3"]))
    dense_backward(3, value2, ref["sd3"])
    st_d3 = dense_send(ref["sd3"], ref["dr3"], 1)
    arrived(st_dz1, 3)
    total = ref["ds1"][z % 4]
    for m in range(1, 4):
        total = total + ref["dz1"][m]
    so_ref[:, 1, :] = total
    arrived(st_dz2, 1)
    so_ref[:, 2, :] = ref["ds2"][z % 2] + ref["dz2"][1]

    @on_one
    def _():
        for st_x, _zero, one in drains:
            left = one
            while left:
                drain(send_sem.at[st_x], min(left, 168))
                left -= min(left, 168)

    @pl.when(jnp.logical_not(is_one))
    def _():
        for st_x, zero, _one in drains:
            left = zero
            while left:
                drain(send_sem.at[st_x], min(left, 168))
                left -= min(left, 168)

    arrived(st_d3, 7)
    so_ref[:, 3, :] = dense_total(ref["sd3"], ref["dr3"], 0)
    assert stage.count <= STAGE_COUNT


def shards(right_side, inverse_top, inverse_second, inverse_third, inverse_fourth, panels, targets):
    vmem = pl.BlockSpec(memory_space=pltpu.VMEM)
    anywhere = pl.BlockSpec(memory_space=pl.ANY)
    smem = pl.BlockSpec(memory_space=pltpu.SMEM)
    out = jax.ShapeDtypeStruct(right_side.shape, F32)
    return pl.pallas_call(
        kernel,
        out_shape=(out, out),
        in_specs=[vmem, anywhere, anywhere, anywhere, anywhere, anywhere, smem],
        out_specs=(vmem, vmem),
        scratch_shapes=[pltpu.VMEM(shape, dtype) for shape, dtype in SCRATCH.values()]
        + [
            pltpu.SMEM((8, 8, 128), I32),
            pltpu.SemaphoreType.DMA((STAGE_COUNT,)),
            pltpu.SemaphoreType.DMA((STAGE_COUNT,)),
            pltpu.SemaphoreType.DMA((8,)),
        ],
        compiler_params=pltpu.CompilerParams(
            collective_id=0, has_side_effects=True, vmem_limit_bytes=56 * 2**20
        ),
        name="tiers",
    )(right_side, inverse_top, inverse_second, inverse_third, inverse_fourth, panels, targets)


def solution(mesh):
    placed = (
        P("rhs", None, "front"),
        P("front", None),
        P("front", None),
        P("front", None),
        P("front", None),
        P(None, None, "front"),
        P(None, "front", None),
    )
    return jax.shard_map(
        shards,
        mesh=mesh,
        in_specs=placed,
        out_specs=(P("rhs", None, "front"), P("rhs", None, "front")),
        check_vma=False,
    )
```

```python
import functools

import jax
import jax.numpy as jnp
from jax import lax
from jax.experimental import pallas as pl
from jax.experimental.pallas import tpu as pltpu
from jax.sharding import PartitionSpec as P

F32 = jnp.float32
BF16 = jnp.bfloat16
I32 = jnp.int32
MESH = pl.DeviceIdType.MESH
TIERS = 4
SLOTS = 8
BLOCKS = (64, 32, 16, 8)
PLANES = (8, 4, 2, 1)
TRANSPOSED = (((1,), (1,)), ((), ()))
NATURAL = (((1,), (0,)), ((), ()))


def split_rows(value):
    high = value.astype(BF16).astype(F32)
    return jnp.concatenate([high, value - high], axis=0).astype(BF16)


def fold_rows(value):
    return value[:8] + value[8:]


def fold_all(value):
    rows = fold_rows(value)
    return rows[:, :128] + rows[:, 128:]


def doubled(value):
    halves = split_rows(value)
    return jnp.concatenate([halves, halves], axis=1)


def matmul(left, right, dims):
    return lax.dot_general(left, right, dims, preferred_element_type=F32)


class Stage:
    def __init__(self):
        self.count = 0

    def take(self):
        self.count += 1
        return self.count - 1


STAGE_COUNT = 48

SCRATCH = dict(
    v0=((128, 8192), F32), v1=((128, 4096), F32), v2=((128, 2048), F32), v3=((128, 1024), F32),
    vp=((3, 1024, 128), F32),
    c0=((64, 256, 128), BF16), c1=((32, 256, 128), BF16), c2=((16, 256, 128), BF16), c3=((8, 256, 128), BF16),
    pc=((3, 1024, 256), BF16),
    rb0=((8, 2, 4, 8, 128), F32), rb1=((4, 2, 4, 8, 128), F32), rb2=((2, 2, 4, 8, 128), F32), rb3=((1, 2, 4, 8, 128), F32),
    tgv=((8, 8, 128), I32),
    up3=((4, 2, 8, 128), F32), up2=((4, 2, 8, 128), F32), up1=((4, 2, 8, 128), F32),
    ur3=((8, 2, 8, 128), F32), ur2=((8, 2, 8, 128), F32), ur1=((8, 2, 8, 128), F32),
    us3=((2, 8, 128), F32), us2=((2, 8, 128), F32), us1=((2, 8, 128), F32),
    uz3=((8, 2, 8, 128), F32), uz2=((8, 2, 8, 128), F32), uz2b=((4, 2, 8, 128), F32), uz1=((8, 2, 8, 128), F32),
    s3p=((2, 8, 8, 128), F32), s3q=((2, 8, 8, 128), F32), s3r=((4, 8, 8, 128), F32),
    s2p=((2, 8, 8, 128), F32), s2q=((2, 8, 8, 128), F32), s1p=((2, 8, 8, 128), F32),
    st2=((2, 2, 8, 128), F32), st2b=((2, 2, 8, 128), F32), st1=((2, 2, 8, 128), F32),
    a1=((4, 2, 2, 8, 128), F32), a2=((4, 2, 2, 8, 128), F32), a3=((4, 2, 2, 8, 128), F32),
    ar1=((8, 2, 2, 8, 128), F32), ar2=((8, 2, 2, 8, 128), F32), ar3=((8, 2, 2, 8, 128), F32),
    as1=((2, 2, 8, 128), F32), as2=((2, 2, 8, 128), F32), as3=((2, 2, 8, 128), F32),
    az1=((8, 2, 8, 128), F32), az2=((4, 2, 8, 128), F32),
    pt1=((2, 8, 128), F32), pt2=((2, 8, 128), F32), pt3=((2, 8, 128), F32),
    pk1=((8, 8, 128), F32), pk2=((8, 8, 128), F32), pk3=((2, 8, 8, 128), F32),
    n0=((4, 12, 2, 8, 128), F32), nx0=((4, 12, 2, 8, 128), F32), ne0=((4, 12, 2, 8, 128), F32), nr0=((4, 12, 2, 8, 128), F32), ns0=((8, 2, 2, 8, 128), F32), nz0=((8, 2, 2, 8, 128), F32),
    n1=((4, 4, 2, 8, 128), F32), nr1=((8, 4, 2, 8, 128), F32), ns1=((4, 2, 8, 128), F32), nz1=((4, 2, 8, 128), F32),
    t0p=((2, 2, 8, 128), F32), t1p=((2, 8, 128), F32),
    sd0=((2, 4, 8, 8, 128), F32), sd1=((2, 4, 4, 8, 128), F32), sd2=((2, 4, 2, 8, 128), F32), sd3=((2, 4, 1, 8, 128), F32),
    dx0=((4, 8, 8, 128), F32), dx1=((4, 4, 8, 128), F32), de0=((4, 8, 8, 128), F32), de1=((4, 4, 8, 128), F32),
    dr0=((4, 8, 8, 128), F32), dr1=((4, 4, 8, 128), F32), dr2=((8, 2, 8, 128), F32), dr3=((8, 1, 8, 128), F32),
    ds0=((8, 8, 128), F32), ds1=((4, 8, 128), F32), ds2=((2, 8, 128), F32),
    dz0=((8, 8, 128), F32), dz1=((4, 8, 128), F32), dz2=((2, 8, 128), F32),
    fk=((4, 8, 128), F32),
    rs=((8, 4, 128), F32),
    dummy=((168, 8, 128), F32),
)


def kernel(rs_hbm, i0_ref, i1_ref, i2_ref, i3_ref, pn_ref, tg_hbm, out_ref, *scratch):
    names = list(SCRATCH)
    ref = dict(zip(names, scratch[: len(names)]))
    tgs, tg_ref, send_sem, recv_sem, load_sem = scratch[len(names) :]
    rs_ref, fo_ref, so_ref = ref["rs"], out_ref.at[0], out_ref.at[1]
    front = lax.axis_index("front")
    core = front % 2
    chip_y = (front // 2) % 4
    d = front % 8
    z = front // 8
    is_one = core == 1
    stage = Stage()
    drains = []

    def put(src, dst, st, to):
        pltpu.make_async_remote_copy(
            src_ref=src, dst_ref=dst, send_sem=send_sem.at[st], recv_sem=recv_sem.at[st],
            device_id={"front": to}, device_id_type=MESH,
        ).start()

    def drain(sem, blocks):
        piece = ref["dummy"].at[pl.ds(0, blocks)]
        pltpu.make_async_copy(piece, piece, sem).wait()

    def arrived(st, blocks):
        drain(recv_sem.at[st], blocks)

    def arrived_by_core(st, blocks_zero, blocks_one):
        @pl.when(is_one)
        def _():
            arrived(st, blocks_one)

        @pl.when(jnp.logical_not(is_one))
        def _():
            arrived(st, blocks_zero)

    barrier = pltpu.get_barrier_semaphore()
    masks = list(range(1, 16)) + [8 * m for m in range(2, 8)]
    for mask in masks:
        pl.semaphore_signal(barrier, inc=1, device_id={"front": front ^ mask}, device_id_type=MESH)

    loads = {}
    rs_copy = pltpu.make_async_copy(rs_hbm, rs_ref, load_sem.at[8])
    rs_copy.start()
    tg_copy = pltpu.make_async_copy(tg_hbm, tg_ref, load_sem.at[9])
    tg_copy.start()
    for number, (name, src) in enumerate(
        (("v3", i3_ref), ("p3", pn_ref.at[2]), ("v2", i2_ref), ("p2", pn_ref.at[1]),
         ("v1", i1_ref), ("p1", pn_ref.at[0]), ("v0", i0_ref))
    ):
        dst = ref["vp"].at[int(name[1]) - 1] if name[0] == "p" else ref[name]
        loads[name] = pltpu.make_async_copy(src, dst, load_sem.at[number])
        loads[name].start()

    rs_copy.wait()
    tg_copy.wait()
    rb = [ref["rb0"], ref["rb1"], ref["rb2"], ref["rb3"]]
    zz = [z, z % 4, z % 2, 0]
    for t in range(TIERS):
        rb[t][zz[t], core, chip_y] = rs_ref[:, t, :]
    lanes = lax.broadcasted_iota(I32, (8, 128), 1)
    own_targets = jnp.full((8, 128), -1, I32)
    for k in range(3):
        for u in range(SLOTS):
            own_targets = jnp.where(lanes == k * 8 + u, tg_ref[k, 0, u], own_targets)
    ref["tgv"][z] = own_targets

    pl.semaphore_wait(barrier, len(masks))

    st_r3 = stage.take()
    for mask in (4, 5, 2, 3, 6, 7, 1):
        put(rb[3].at[0, core, chip_y], rb[3].at[0, core, chip_y], st_r3, front ^ mask)
    drains.append((st_r3, 7, 7))
    st_tg = stage.take()
    st_rz = [stage.take() for t in range(3)]
    put(rb[2].at[z % 2, core, chip_y], rb[2].at[z % 2, core, chip_y], st_rz[2], front ^ 8)
    drains.append((st_rz[2], 1, 1))
    for m in range(1, 8):
        put(ref["tgv"].at[z], ref["tgv"].at[z], st_tg, front ^ (8 * m))
    drains.append((st_tg, 7, 7))
    for t, count in ((1, 4), (0, 8)):
        for m in range(1, count):
            put(rb[t].at[zz[t], core, chip_y], rb[t].at[zz[t], core, chip_y], st_rz[t], front ^ (8 * m))
        drains.append((st_rz[t], count - 1, count - 1))

    cc = [ref["c0"], ref["c1"], ref["c2"], ref["c3"]]
    vv = [ref["v0"], ref["v1"], ref["v2"], ref["v3"]]

    def prepare_inverse(t):
        loads["v" + str(t)].wait()

        def body(e, carry):
            block = vv[t][:, pl.ds(pl.multiple_of(e * 128, 128), 128)]
            high = block.astype(BF16)
            cc[t][e, 0:128, :] = high
            cc[t][e, 128:256, :] = (block - high.astype(F32)).astype(BF16)
            return carry

        lax.fori_loop(0, BLOCKS[t], body, 0)

    def prepare_panel(t):
        loads["p" + str(t)].wait()

        def body(u, carry):
            rows = pl.ds(pl.multiple_of(u * 128, 128), 128)
            block = ref["vp"][t - 1, rows, :]
            high = block.astype(BF16)
            ref["pc"][t - 1, rows, 0:128] = high
            ref["pc"][t - 1, rows, 128:256] = (block - high.astype(F32)).astype(BF16)
            return carry

        lax.fori_loop(0, SLOTS, body, 0)

    def target(m, k, u):
        return tgs[z ^ m, 0, k * 8 + u]

    def dense_forward(t):
        def chunk(index):
            x = jnp.concatenate([rb[t][index, j % 2, j // 2] for j in range(8)], axis=1)
            w = jnp.concatenate([cc[t][index * 8 + j] for j in range(8)], axis=1)
            return fold_all(matmul(split_rows(x), w, TRANSPOSED))

        if PLANES[t] == 1:
            return chunk(0)
        return lax.fori_loop(0, PLANES[t], lambda i, total: total + chunk(i), jnp.zeros((8, 128), F32))

    def slots_forward(t, k, m, block_of):
        parts, weights = [], []
        for u in range(SLOTS):
            tag = target(m, k, u)
            live = jnp.where((tag >> 6) == t, 1.0, 0.0).astype(F32)
            parts.append(block_of(u) * live)
            weights.append(cc[t][tag & (BLOCKS[t] - 1)])
        x = jnp.concatenate(parts, axis=1)
        w = jnp.concatenate(weights, axis=1)
        return fold_all(matmul(split_rows(x), w, TRANSPOSED))

    def panel_forward(t, value, out):
        terms = fold_rows(matmul(doubled(value), ref["pc"][t - 1], TRANSPOSED))
        for u in range(SLOTS):
            out[u // 2, u % 2] = terms[:, u * 128 : (u + 1) * 128]

    def panel_backward(t, picked):
        x = jnp.concatenate([picked[u] for u in range(SLOTS)], axis=1)
        return fold_all(matmul(split_rows(x), ref["pc"][t - 1], NATURAL))

    def dense_backward(t, value2, out):
        def chunk(index, carry):
            w = jnp.concatenate([cc[t][index * 8 + j] for j in range(8)], axis=1)
            terms = fold_rows(matmul(value2, w, NATURAL))
            for j in range(8):
                out[j % 2, j // 2, index] = terms[:, j * 128 : (j + 1) * 128]
            return carry

        if PLANES[t] == 1:
            chunk(0, 0)
        else:
            lax.fori_loop(0, PLANES[t], chunk, 0)

    def slots_backward(t, k, m, value2, out, place):
        weights, lives = [], []
        for u in range(SLOTS):
            tag = target(m, k, u)
            lives.append(jnp.where((tag >> 6) == t, 1.0, 0.0).astype(F32))
            weights.append(cc[t][tag & (BLOCKS[t] - 1)])
        w = jnp.concatenate(weights, axis=1)
        terms = fold_rows(matmul(value2, w, NATURAL))
        for u in range(SLOTS):
            out[u // 2, place, u % 2] = terms[:, u * 128 : (u + 1) * 128] * lives[u]

    def reduce_send(out, into, blocks):
        st = stage.take()
        for k in (2, 1, 3):
            put(out.at[chip_y ^ k], into.at[d], st, (front ^ (2 * k)) | 1)

        @pl.when(jnp.logical_not(is_one))
        def _():
            put(out.at[chip_y], into.at[d], st, front ^ 1)

        drains.append((st, 4 * blocks, 3 * blocks))
        return st

    def reduced(st, out, into, blocks, index):
        total = out[(chip_y,) + index]
        for k in range(1, 8):
            total = total + into[(d ^ k,) + index]
        return total

    def spread(src, dst, blocks):
        st = stage.take()
        for mask in (4, 5, 2, 3, 6, 7, 1):
            put(src, dst, st, front ^ mask)
        drains.append((st, 0, 7 * blocks))
        return st

    def on_one(body):
        pl.when(is_one)(body)

    pair = pl.ds(2 * chip_y, 2)

    prepare_inverse(3)
    prepare_panel(3)
    arrived(st_r3, 7)
    forward3 = dense_forward(3)
    panel_forward(3, forward3, ref["up3"])
    st = reduce_send(ref["up3"], ref["ur3"], 2)
    fo_ref[:, 3, :] = forward3
    ref["fk"][3] = forward3
    arrived(st_tg, 7)
    targets_copy = pltpu.make_async_copy(ref["tgv"], tgs, load_sem.at[7])
    targets_copy.start()
    arrived(st_rz[2], 1)
    st_rp = [None] * 3
    st_rc = [None] * 3

    def plane_gather(t):
        st_rp[t] = stage.take()
        for mask in (4, 2, 6):
            put(rb[t].at[:, core, chip_y], rb[t].at[:, core, chip_y], st_rp[t], front ^ mask)
        drains.append((st_rp[t], 3 * PLANES[t], 3 * PLANES[t]))

    def core_gather(t):
        arrived(st_rp[t], 3 * PLANES[t])
        st_rc[t] = stage.take()
        put(rb[t].at[:, core], rb[t].at[:, core], st_rc[t], front ^ 1)
        drains.append((st_rc[t], 4 * PLANES[t], 4 * PLANES[t]))

    plane_gather(2)
    prepare_inverse(2)
    targets_copy.wait()
    st_s3 = stage.take()
    st_z3 = stage.take()

    @on_one
    def _():
        arrived(st, 14)
        for i in range(2):
            total = reduced(st, ref["up3"], ref["ur3"], 2, (i,))
            ref["us3"][i] = total
            ref["s3p"][0, 2 * chip_y + i] = total
        for mask in (12, 13, 10, 11, 14, 15, 8, 9):
            put(ref["us3"], ref["s3p"].at[1, pair], st_s3, front ^ mask)
        for mask in (4, 5, 2, 3, 6, 7, 1):
            put(ref["us3"], ref["s3p"].at[0, pair], st_s3, front ^ mask)
        for m in range(2, 8):
            put(ref["us3"], ref["uz3"].at[m], st_z3, front ^ (8 * m))

    drains.append((st_s3, 0, 30))
    drains.append((st_z3, 0, 12))
    core_gather(2)
    prepare_panel(2)
    arrived(st_rc[2], 8)
    base2 = dense_forward(2)
    arrived_by_core(st_s3, 16, 14)

    forward2 = base2
    for m in range(2):
        forward2 = forward2 - slots_forward(2, 2, m, lambda u, m=m: ref["s3p"][m, u])
    panel_forward(2, forward2, ref["up2"])
    st = reduce_send(ref["up2"], ref["ur2"], 2)
    fo_ref[:, 2, :] = forward2
    ref["fk"][2] = forward2
    arrived(st_rz[1], 3)
    plane_gather(1)
    prepare_inverse(1)
    st_q3 = stage.take()

    @on_one
    def _():
        arrived(st_z3, 12)
        for m in range(2, 8):
            into = ref["s3q"] if m < 4 else ref["s3r"]
            for i in range(2):
                into[m % 2 if m < 4 else m - 4, 2 * chip_y + i] = ref["uz3"][m, i]
        for mask in (4, 2, 6):
            put(ref["uz3"].at[pl.ds(2, 2)], ref["s3q"].at[:, pair], st_q3, front ^ mask)

    drains.append((st_q3, 0, 12))
    st_z2 = stage.take()
    st_z2b = stage.take()

    @on_one
    def _():
        arrived(st, 14)
        for i in range(2):
            ref["us2"][i] = reduced(st, ref["up2"], ref["ur2"], 2, (i,))
        for m in (2, 3, 1):
            put(ref["us2"], ref["uz2"].at[m], st_z2, front ^ (8 * m))
        for m in range(4, 8):
            put(ref["us2"], ref["uz2b"].at[m - 4], st_z2b, front ^ (8 * m))

    drains.append((st_z2, 0, 6))
    drains.append((st_z2b, 0, 8))
    core_gather(1)
    st_q3c = stage.take()

    @on_one
    def _():
        arrived(st_q3, 12)
        put(ref["s3q"], ref["s3q"], st_q3c, front ^ 1)

    drains.append((st_q3c, 0, 16))
    prepare_panel(1)
    arrived(st_rc[1], 16)
    base1 = dense_forward(1)
    st_s2 = stage.take()

    @on_one
    def _():
        arrived(st_z2, 6)
        for i in range(2):
            own = ref["us2"][i] + ref["uz2"][1, i]
            other = ref["uz2"][2, i] + ref["uz2"][3, i]
            for h, total in ((0, own), (1, other)):
                ref["st2"][h, i] = total
                ref["s2p"][h, 2 * chip_y + i] = total
        for mask in (4, 5, 2, 3, 6, 7, 1):
            put(ref["st2"], ref["s2p"].at[:, pair], st_s2, front ^ mask)

    drains.append((st_s2, 0, 28))

    @pl.when(jnp.logical_not(is_one))
    def _():
        arrived(st_q3c, 16)

    for m in range(4):
        src = ref["s3p"].at[m] if m < 2 else ref["s3q"].at[m - 2]
        base1 = base1 - slots_forward(1, 2, m, lambda u, src=src: src[u])
    arrived_by_core(st_s2, 16, 12)

    forward1 = base1
    for h in range(2):
        forward1 = forward1 - slots_forward(1, 1, 2 * h, lambda u, h=h: ref["s2p"][h, u])
    panel_forward(1, forward1, ref["up1"])
    st = reduce_send(ref["up1"], ref["ur1"], 2)
    fo_ref[:, 1, :] = forward1
    ref["fk"][1] = forward1
    st_q2 = stage.take()
    st_r3x = stage.take()

    @on_one
    def _():
        arrived(st_z2b, 8)
        for i in range(2):
            for h in range(2):
                total = ref["uz2b"][2 * h, i] + ref["uz2b"][2 * h + 1, i]
                ref["st2b"][h, i] = total
                ref["s2q"][h, 2 * chip_y + i] = total
        for mask in (4, 5, 2, 3, 6, 7, 1):
            put(ref["st2b"], ref["s2q"].at[:, pair], st_q2, front ^ mask)
        for mask in (4, 2, 6):
            put(ref["uz3"].at[pl.ds(4, 4)], ref["s3r"].at[:, pair], st_r3x, front ^ mask)

    drains.append((st_q2, 0, 28))
    drains.append((st_r3x, 0, 24))
    arrived(st_rz[0], 7)
    plane_gather(0)
    prepare_inverse(0)
    st_z1 = stage.take()

    @on_one
    def _():
        arrived(st, 14)
        for i in range(2):
            ref["us1"][i] = reduced(st, ref["up1"], ref["ur1"], 2, (i,))
        for m in (4, 5, 3, 6, 2, 7, 1):
            put(ref["us1"], ref["uz1"].at[m], st_z1, front ^ (8 * m))

    drains.append((st_z1, 0, 14))
    core_gather(0)
    st_r3c = stage.take()

    @on_one
    def _():
        arrived(st_r3x, 24)
        put(ref["s3r"], ref["s3r"], st_r3c, front ^ 1)

    drains.append((st_r3c, 0, 32))
    base0 = jnp.zeros((8, 128), F32)
    for h in range(2):
        base0 = base0 - slots_forward(0, 1, 2 * h, lambda u, h=h: ref["s2p"][h, u])
    for m in range(4):
        src = ref["s3p"].at[m] if m < 2 else ref["s3q"].at[m - 2]
        base0 = base0 - slots_forward(0, 2, m, lambda u, src=src: src[u])
    arrived(st_rc[0], 32)
    base0 = base0 + dense_forward(0)
    st_s1 = stage.take()

    @on_one
    def _():
        arrived(st_z1, 14)
        for i in range(2):
            own = ref["us1"][i]
            for m in range(1, 4):
                own = own + ref["uz1"][m, i]
            other = ref["uz1"][4, i]
            for m in range(5, 8):
                other = other + ref["uz1"][m, i]
            for h, total in ((0, own), (1, other)):
                ref["st1"][h, i] = total
                ref["s1p"][h, 2 * chip_y + i] = total
        for mask in (4, 5, 2, 3, 6, 7, 1):
            put(ref["st1"], ref["s1p"].at[:, pair], st_s1, front ^ mask)

    drains.append((st_s1, 0, 28))

    @pl.when(jnp.logical_not(is_one))
    def _():
        arrived(st_r3c, 32)

    base0 = lax.fori_loop(
        0, 4, lambda m, total: total - slots_forward(0, 2, m + 4, lambda u: ref["s3r"][m, u]), base0
    )
    arrived_by_core(st_q2, 16, 12)
    for h in range(2):
        base0 = base0 - slots_forward(0, 1, 4 + 2 * h, lambda u, h=h: ref["s2q"][h, u])
    arrived_by_core(st_s1, 16, 12)

    forward0 = base0
    for h in range(2):
        forward0 = forward0 - slots_forward(0, 0, 4 * h, lambda u, h=h: ref["s1p"][h, u])

    value2 = doubled(forward0)
    for h in range(2):
        slots_backward(0, 0, 4 * h, value2, ref["a1"], h)
    st = reduce_send(ref["a1"], ref["ar1"], 4)
    fo_ref[:, 0, :] = forward0
    dense_backward(0, value2, ref["sd0"])
    for j in range(12):
        k = 1 if j < 4 else 2
        m = 2 * j if j < 4 else j - 4
        for u in range(SLOTS):
            tag = target(m, k, u)
            live = jnp.where((tag >> 6) == 0, 1.0, 0.0).astype(F32)
            ref["n0"][u // 2, j, u % 2] = ref["sd0"][tag & 1, (tag >> 1) & 3, (tag >> 3) & 7] * live
    st_nx = stage.take()

    @pl.when(jnp.logical_not(is_one))
    def _():
        put(ref["n0"], ref["nx0"], st_nx, front ^ 1)

    drains.append((st_nx, 96, 0))

    def dense_send(out, into, blocks):
        st_d = stage.take()
        for mask in (4, 5, 2, 3, 6, 7, 1):
            put(out.at[core ^ (mask & 1), chip_y ^ (mask >> 1)], into.at[mask], st_d, front ^ mask)
        drains.append((st_d, 7 * blocks, 7 * blocks))
        return st_d

    def dense_total(out, into, index):
        total = out[core, chip_y, index]
        for mask in range(1, 8):
            total = total + into[mask, index]
        return total

    def chip_send(out, into, blocks):
        st_x = stage.take()
        put(out.at[1 - core], into, st_x, front ^ 1)
        drains.append((st_x, 4 * blocks, 4 * blocks))
        return st_x

    def chip_total_send(st_x, out, cross, summed, into, blocks):
        arrived(st_x, 4 * blocks)

        def body(w, carry):
            for y in range(4):
                summed[y, w] = out[core, y, w] + cross[y, w]
            return carry

        lax.fori_loop(0, blocks, body, 0)
        st_d = stage.take()
        for k in (2, 1, 3):
            put(summed.at[chip_y ^ k], into.at[k], st_d, front ^ (2 * k))
        drains.append((st_d, 3 * blocks, 3 * blocks))
        return st_d

    def plane_total(st_d, summed, into, final, blocks):
        arrived(st_d, 3 * blocks)
        for w in range(blocks):
            final[w] = (summed[chip_y, w] + into[1, w]) + (into[2, w] + into[3, w])

    st_dx0 = chip_send(ref["sd0"], ref["dx0"], 8)
    st_z = stage.take()

    @on_one
    def _():
        arrived(st, 28)
        for h in range(2):
            for i in range(2):
                ref["as1"][h, i] = reduced(st, ref["a1"], ref["ar1"], 4, (h, i))
        for m in (4, 5, 3, 6, 2, 7, 1):
            put(ref["as1"].at[m >> 2], ref["az1"].at[m], st_z, front ^ (8 * m))

    drains.append((st_z, 0, 14))
    st_n0 = stage.take()

    @on_one
    def _():
        arrived(st_nx, 96)

        def body(j, carry):
            for y in range(4):
                for i in range(2):
                    ref["ne0"][y, j, i] = ref["n0"][y, j, i] + ref["nx0"][y, j, i]
            return carry

        lax.fori_loop(0, 12, body, 0)
        for k in (2, 1, 3):
            put(ref["ne0"].at[chip_y ^ k], ref["nr0"].at[k], st_n0, front ^ (2 * k))

    drains.append((st_n0, 0, 72))
    st_d0 = chip_total_send(st_dx0, ref["sd0"], ref["dx0"], ref["de0"], ref["dr0"], 8)
    st_p = stage.take()

    @on_one
    def _():
        arrived(st_z, 14)
        for i in range(2):
            total = ref["as1"][0, i]
            for m in range(1, 8):
                total = total + ref["az1"][m, i]
            ref["pt1"][i] = total
            ref["pk1"][2 * chip_y + i] = total
        for mask in (4, 5, 2, 3, 6, 7, 1):
            put(ref["pt1"], ref["pk1"].at[pair], st_p, front ^ mask)

    drains.append((st_p, 0, 14))
    st_nz0 = stage.take()

    @on_one
    def _():
        arrived(st_n0, 72)

        def total_of(j, i):
            return (ref["ne0"][chip_y, j, i] + ref["nr0"][1, j, i]) + (ref["nr0"][2, j, i] + ref["nr0"][3, j, i])

        def body(m, carry):
            for i in range(2):
                ref["ns0"][m, 0, i] = total_of(m // 2, i)
                ref["ns0"][m, 1, i] = total_of(4 + m, i)
            return carry

        lax.fori_loop(0, 8, body, 0)
        for m in range(1, 8):
            put(ref["ns0"].at[m], ref["nz0"].at[m], st_nz0, front ^ (8 * m))

    drains.append((st_nz0, 0, 28))
    st_dz0 = stage.take()
    plane_total(st_d0, ref["de0"], ref["dr0"], ref["ds0"], 8)
    for m in range(1, 8):
        put(ref["ds0"].at[z ^ m], ref["dz0"].at[m], st_dz0, front ^ (8 * m))
    drains.append((st_dz0, 7, 7))
    arrived_by_core(st_p, 8, 6)

    value2 = doubled(ref["fk"][1] - panel_backward(1, ref["pk1"]))
    for h in range(2):
        slots_backward(1, 1, 2 * h, value2, ref["a2"], h)
    st = reduce_send(ref["a2"], ref["ar2"], 4)
    dense_backward(1, value2, ref["sd1"])
    for m in range(4):
        for u in range(SLOTS):
            tag = target(m, 2, u)
            live = jnp.where((tag >> 6) == 1, 1.0, 0.0).astype(F32)
            ref["n1"][u // 2, m, u % 2] = ref["sd1"][tag & 1, (tag >> 1) & 3, (tag >> 3) & 3] * live
    st_n1 = reduce_send(ref["n1"], ref["nr1"], 8)
    st_dx1 = chip_send(ref["sd1"], ref["dx1"], 4)

    st_z = stage.take()

    @on_one
    def _():
        arrived(st, 28)
        for h in range(2):
            for i in range(2):
                ref["as2"][h, i] = reduced(st, ref["a2"], ref["ar2"], 4, (h, i))
        for m in (2, 3, 1):
            put(ref["as2"].at[m >> 1], ref["az2"].at[m], st_z, front ^ (8 * m))

    drains.append((st_z, 0, 6))

    @on_one
    def _():
        arrived(st_nz0, 28)
        for q in range(2):
            for i in range(2):
                total = ref["ns0"][0, q, i]
                for m in range(1, 8):
                    total = total + ref["nz0"][m, q, i]
                ref["t0p"][q, i] = total

    st_d1 = chip_total_send(st_dx1, ref["sd1"], ref["dx1"], ref["de1"], ref["dr1"], 4)
    st_p = stage.take()

    @on_one
    def _():
        arrived(st_z, 6)
        for i in range(2):
            total = ref["as2"][0, i] + ref["t0p"][0, i]
            for m in range(1, 4):
                total = total + ref["az2"][m, i]
            ref["pt2"][i] = total
            ref["pk2"][2 * chip_y + i] = total
        for mask in (4, 5, 2, 3, 6, 7, 1):
            put(ref["pt2"], ref["pk2"].at[pair], st_p, front ^ mask)

    drains.append((st_p, 0, 14))
    st_nz1 = stage.take()

    @on_one
    def _():
        arrived(st_n1, 56)
        for m in range(4):
            for i in range(2):
                ref["ns1"][m, i] = reduced(st_n1, ref["n1"], ref["nr1"], 8, (m, i))
        for m in range(1, 4):
            put(ref["ns1"].at[m], ref["nz1"].at[m], st_nz1, front ^ (8 * m))

    drains.append((st_nz1, 0, 6))

    arrived(st_dz0, 7)
    total = ref["ds0"][z]
    for m in range(1, 8):
        total = total + ref["dz0"][m]
    so_ref[:, 0, :] = total
    arrived_by_core(st_p, 8, 6)

    value2 = doubled(ref["fk"][2] - panel_backward(2, ref["pk2"]))
    for h in range(2):
        slots_backward(2, 2, h, value2, ref["a3"], h)
    st = reduce_send(ref["a3"], ref["ar3"], 4)
    dense_backward(2, value2, ref["sd2"])
    st_d2 = dense_send(ref["sd2"], ref["dr2"], 2)

    st_dz1 = stage.take()
    plane_total(st_d1, ref["de1"], ref["dr1"], ref["ds1"], 4)
    for m in range(1, 4):
        put(ref["ds1"].at[(z ^ m) % 4], ref["dz1"].at[m], st_dz1, front ^ (8 * m))
    drains.append((st_dz1, 3, 3))
    st_p = stage.take()

    @on_one
    def _():
        arrived(st_nz1, 6)
        for i in range(2):
            total = ref["ns1"][0, i] + ref["t0p"][1, i]
            for m in range(1, 4):
                total = total + ref["nz1"][m, i]
            ref["t1p"][i] = total
        arrived(st, 28)
        for i in range(2):
            ref["as3"][1, i] = reduced(st, ref["a3"], ref["ar3"], 4, (1, i))
            total = ref["t1p"][i] + reduced(st, ref["a3"], ref["ar3"], 4, (0, i))
            ref["as3"][0, i] = total
            ref["pk3"][0, 2 * chip_y + i] = total
        for mask in (12, 13, 10, 11, 14, 15, 8, 9):
            put(ref["as3"].at[1], ref["pk3"].at[1, pair], st_p, front ^ mask)
        for mask in (4, 5, 2, 3, 6, 7, 1):
            put(ref["as3"].at[0], ref["pk3"].at[0, pair], st_p, front ^ mask)

    drains.append((st_p, 0, 30))
    st_dz2 = stage.take()
    arrived(st_d2, 14)
    for w in range(2):
        ref["ds2"][w] = dense_total(ref["sd2"], ref["dr2"], w)
    put(ref["ds2"].at[(z ^ 1) % 2], ref["dz2"].at[1], st_dz2, front ^ 8)
    drains.append((st_dz2, 1, 1))
    arrived(st_dz1, 3)
    total = ref["ds1"][z % 4]
    for m in range(1, 4):
        total = total + ref["dz1"][m]
    so_ref[:, 1, :] = total
    arrived_by_core(st_p, 16, 14)

    for u in range(SLOTS):
        ref["pk3"][0, u] = ref["pk3"][0, u] + ref["pk3"][1, u]
    value2 = doubled(ref["fk"][3] - panel_backward(3, ref["pk3"].at[0]))
    dense_backward(3, value2, ref["sd3"])
    st_d3 = dense_send(ref["sd3"], ref["dr3"], 1)
    arrived(st_dz2, 1)
    so_ref[:, 2, :] = ref["ds2"][z % 2] + ref["dz2"][1]

    @on_one
    def _():
        for st_x, _zero, one in drains:
            left = one
            while left:
                drain(send_sem.at[st_x], min(left, 168))
                left -= min(left, 168)

    @pl.when(jnp.logical_not(is_one))
    def _():
        for st_x, zero, _one in drains:
            left = zero
            while left:
                drain(send_sem.at[st_x], min(left, 168))
                left -= min(left, 168)

    arrived(st_d3, 7)
    so_ref[:, 3, :] = dense_total(ref["sd3"], ref["dr3"], 0)
    assert stage.count <= STAGE_COUNT


def shards(right_side, inverse_top, inverse_second, inverse_third, inverse_fourth, panels, targets):
    anywhere = pl.BlockSpec(memory_space=pl.ANY)
    results = pl.pallas_call(
        kernel,
        out_shape=pltpu.VMEM((2,) + right_side.shape, F32),
        in_specs=[anywhere] * 7,
        out_specs=pl.BlockSpec(memory_space=pltpu.VMEM),
        scratch_shapes=[pltpu.VMEM(shape, dtype) for shape, dtype in SCRATCH.values()]
        + [
            pltpu.SMEM((8, 8, 128), I32),
            pltpu.SMEM((3, 1, 8), I32),
            pltpu.SemaphoreType.DMA((STAGE_COUNT,)),
            pltpu.SemaphoreType.DMA((STAGE_COUNT,)),
            pltpu.SemaphoreType.DMA((12,)),
        ],
        compiler_params=pltpu.CompilerParams(
            collective_id=0, has_side_effects=True, vmem_limit_bytes=56 * 2**20
        ),
        name="tiers",
    )(right_side, inverse_top, inverse_second, inverse_third, inverse_fourth, panels, targets)
    return results[0], results[1]


def solution(mesh):
    placed = (
        P("rhs", None, "front"),
        P("front", None),
        P("front", None),
        P("front", None),
        P("front", None),
        P(None, None, "front"),
        P(None, "front", None),
    )
    return jax.shard_map(
        shards,
        mesh=mesh,
        in_specs=placed,
        out_specs=(P("rhs", None, "front"), P("rhs", None, "front")),
        check_vma=False,
    )
```

```python
import functools

import jax
import jax.numpy as jnp
from jax import lax
from jax.experimental import pallas as pl
from jax.experimental.pallas import tpu as pltpu
from jax.sharding import PartitionSpec as P

F32 = jnp.float32
BF16 = jnp.bfloat16
I32 = jnp.int32
MESH = pl.DeviceIdType.MESH
TIERS = 4
SLOTS = 8
BLOCKS = (64, 32, 16, 8)
PLANES = (8, 4, 2, 1)
TRANSPOSED = (((1,), (1,)), ((), ()))
NATURAL = (((1,), (0,)), ((), ()))


def split_rows(value):
    high = value.astype(BF16).astype(F32)
    return jnp.concatenate([high, value - high], axis=0).astype(BF16)


def fold_rows(value):
    return value[:8] + value[8:]


def fold_all(value):
    rows = fold_rows(value)
    return rows[:, :128] + rows[:, 128:]


def doubled(value):
    halves = split_rows(value)
    return jnp.concatenate([halves, halves], axis=1)


def matmul(left, right, dims):
    return lax.dot_general(left, right, dims, preferred_element_type=F32)


class Stage:
    def __init__(self):
        self.count = 0

    def take(self):
        self.count += 1
        return self.count - 1


STAGE_COUNT = 52

SCRATCH = dict(
    v0=((128, 8192), F32), v1=((128, 4096), F32), v2=((128, 2048), F32), v3=((128, 1024), F32),
    vp=((3, 1024, 128), F32),
    c0=((64, 256, 128), BF16), c1=((32, 256, 128), BF16), c2=((16, 256, 128), BF16), c3=((8, 256, 128), BF16),
    pc=((3, 1024, 256), BF16),
    rb0=((8, 2, 4, 8, 128), F32), rb1=((4, 2, 4, 8, 128), F32), rb2=((2, 2, 4, 8, 128), F32), rb3=((1, 2, 4, 8, 128), F32),
    tgv=((8, 8, 128), I32),
    up3=((4, 2, 8, 128), F32), up2=((4, 2, 8, 128), F32), up1=((4, 2, 8, 128), F32),
    ur3=((8, 2, 8, 128), F32), ur2=((8, 2, 8, 128), F32), ur1=((8, 2, 8, 128), F32),
    us3=((2, 8, 128), F32), us2=((2, 8, 128), F32), us1=((2, 8, 128), F32),
    uz3=((8, 2, 8, 128), F32), uz2=((8, 2, 8, 128), F32), uz2b=((4, 2, 8, 128), F32), uz1=((8, 2, 8, 128), F32),
    s3p=((2, 8, 8, 128), F32), s3q=((2, 8, 8, 128), F32), s3r=((4, 8, 8, 128), F32),
    s2p=((2, 8, 8, 128), F32), s2q=((2, 8, 8, 128), F32), s1p=((2, 8, 8, 128), F32),
    st2=((2, 2, 8, 128), F32), st2b=((2, 2, 8, 128), F32), st1=((2, 2, 8, 128), F32),
    a1=((4, 2, 2, 8, 128), F32), a2=((4, 2, 2, 8, 128), F32), a3=((4, 2, 2, 8, 128), F32),
    ar1=((8, 2, 2, 8, 128), F32), ar2=((8, 2, 2, 8, 128), F32), ar3=((8, 2, 2, 8, 128), F32),
    as1=((2, 2, 8, 128), F32), as2=((2, 2, 8, 128), F32), as3=((2, 2, 8, 128), F32),
    az1=((8, 2, 8, 128), F32), az2=((4, 2, 8, 128), F32),
    pt1=((2, 8, 128), F32), pt2=((2, 8, 128), F32), pt3=((2, 8, 128), F32),
    pk1=((8, 8, 128), F32), pk2=((8, 8, 128), F32), pk3=((2, 8, 8, 128), F32),
    n0=((4, 12, 2, 8, 128), F32), nx0=((4, 12, 2, 8, 128), F32), ne0=((4, 12, 2, 8, 128), F32), nr0=((4, 12, 2, 8, 128), F32), ns0=((8, 2, 2, 8, 128), F32), nz0=((8, 2, 2, 8, 128), F32),
    n1=((4, 4, 2, 8, 128), F32), nr1=((8, 4, 2, 8, 128), F32), ns1=((4, 2, 8, 128), F32), nz1=((4, 2, 8, 128), F32),
    t0p=((2, 2, 8, 128), F32), t1p=((2, 8, 128), F32),
    sd0=((2, 4, 8, 8, 128), F32), sd1=((2, 4, 4, 8, 128), F32), sd2=((2, 4, 2, 8, 128), F32), sd3=((2, 4, 1, 8, 128), F32),
    dx0=((4, 8, 8, 128), F32), dx1=((4, 4, 8, 128), F32), de0=((4, 8, 8, 128), F32), de1=((4, 4, 8, 128), F32),
    dr0=((4, 8, 8, 128), F32), dr1=((4, 4, 8, 128), F32), dr2=((16, 8, 128), F32), dr3=((8, 1, 8, 128), F32),
    ds0=((8, 8, 128), F32), ds1=((4, 8, 128), F32),
    dz0=((8, 8, 128), F32), dz1=((4, 8, 128), F32),
    fk=((4, 8, 128), F32),
    gp=((2, 4, 256, 128), F32), gx=((2, 4, 256, 128), F32), gs=((4, 2, 256, 128), F32), gr=((4, 2, 256, 128), F32),
    ga=((2, 4, 256, 128), F32), gc=((1024, 256), BF16),
    rs=((8, 4, 128), F32),
    dummy=((256, 8, 128), F32),
)


def kernel(rs_hbm, i0_ref, i1_ref, i2_ref, i3_ref, pn_ref, tg_hbm, out_ref, *scratch):
    names = list(SCRATCH)
    ref = dict(zip(names, scratch[: len(names)]))
    tgs, tg_ref, send_sem, recv_sem, load_sem = scratch[len(names) :]
    rs_ref, fo_ref, so_ref = ref["rs"], out_ref.at[0], out_ref.at[1]
    front = lax.axis_index("front")
    side = lax.axis_index("rhs")
    core = front % 2
    chip_y = (front // 2) % 4
    d = front % 8
    z = front // 8
    is_one = core == 1
    stage = Stage()
    drains = []

    def put(src, dst, st, to, axis="front"):
        pltpu.make_async_remote_copy(
            src_ref=src, dst_ref=dst, send_sem=send_sem.at[st], recv_sem=recv_sem.at[st],
            device_id={axis: to}, device_id_type=MESH,
        ).start()

    def drain(sem, blocks):
        piece = ref["dummy"].at[pl.ds(0, blocks)]
        pltpu.make_async_copy(piece, piece, sem).wait()

    def arrived(st, blocks):
        drain(recv_sem.at[st], blocks)

    def arrived_by_core(st, blocks_zero, blocks_one):
        @pl.when(is_one)
        def _():
            arrived(st, blocks_one)

        @pl.when(jnp.logical_not(is_one))
        def _():
            arrived(st, blocks_zero)

    barrier = pltpu.get_barrier_semaphore()
    masks = list(range(1, 16)) + [8 * m for m in range(2, 8)]
    for mask in masks:
        pl.semaphore_signal(barrier, inc=1, device_id={"front": front ^ mask}, device_id_type=MESH)
    for k in range(1, 4):
        pl.semaphore_signal(barrier, inc=1, device_id={"rhs": side ^ k}, device_id_type=MESH)

    loads = {}
    rs_copy = pltpu.make_async_copy(rs_hbm, rs_ref, load_sem.at[8])
    rs_copy.start()
    tg_copy = pltpu.make_async_copy(tg_hbm, tg_ref, load_sem.at[9])
    tg_copy.start()
    for number, (name, src) in enumerate(
        (("v3", i3_ref), ("p3", pn_ref.at[2]), ("v2", i2_ref), ("p2", pn_ref.at[1]),
         ("v1", i1_ref), ("p1", pn_ref.at[0]), ("v0", i0_ref))
    ):
        dst = ref["vp"].at[int(name[1]) - 1] if name[0] == "p" else ref[name]
        loads[name] = pltpu.make_async_copy(src, dst, load_sem.at[number])
        loads[name].start()

    rs_copy.wait()
    tg_copy.wait()
    rb = [ref["rb0"], ref["rb1"], ref["rb2"], ref["rb3"]]
    zz = [z, z % 4, z % 2, 0]
    for t in range(TIERS):
        rb[t][zz[t], core, chip_y] = rs_ref[:, t, :]
    lanes = lax.broadcasted_iota(I32, (8, 128), 1)
    own_targets = jnp.full((8, 128), -1, I32)
    for k in range(3):
        for u in range(SLOTS):
            own_targets = jnp.where(lanes == k * 8 + u, tg_ref[k, 0, u], own_targets)
    ref["tgv"][z] = own_targets

    pl.semaphore_wait(barrier, len(masks) + 3)

    st_r3 = stage.take()
    for mask in (4, 5, 2, 3, 6, 7, 1):
        put(rb[3].at[0, core, chip_y], rb[3].at[0, core, chip_y], st_r3, front ^ mask)
    drains.append((st_r3, 7, 7))
    st_tg = stage.take()
    st_rz = [stage.take() for t in range(3)]
    put(rb[2].at[z % 2, core, chip_y], rb[2].at[z % 2, core, chip_y], st_rz[2], front ^ 8)
    drains.append((st_rz[2], 1, 1))
    for m in range(1, 8):
        put(ref["tgv"].at[z], ref["tgv"].at[z], st_tg, front ^ (8 * m))
    drains.append((st_tg, 7, 7))
    for t, count in ((1, 4), (0, 8)):
        for m in range(1, count):
            put(rb[t].at[zz[t], core, chip_y], rb[t].at[zz[t], core, chip_y], st_rz[t], front ^ (8 * m))
        drains.append((st_rz[t], count - 1, count - 1))

    cc = [ref["c0"], ref["c1"], ref["c2"], ref["c3"]]
    vv = [ref["v0"], ref["v1"], ref["v2"], ref["v3"]]

    def prepare_inverse(t):
        loads["v" + str(t)].wait()

        def body(e, carry):
            block = vv[t][:, pl.ds(pl.multiple_of(e * 128, 128), 128)]
            high = block.astype(BF16)
            cc[t][e, 0:128, :] = high
            cc[t][e, 128:256, :] = (block - high.astype(F32)).astype(BF16)
            return carry

        lax.fori_loop(0, BLOCKS[t], body, 0)

    def prepare_panel(t):
        loads["p" + str(t)].wait()

        def body(u, carry):
            rows = pl.ds(pl.multiple_of(u * 128, 128), 128)
            block = ref["vp"][t - 1, rows, :]
            high = block.astype(BF16)
            ref["pc"][t - 1, rows, 0:128] = high
            ref["pc"][t - 1, rows, 128:256] = (block - high.astype(F32)).astype(BF16)
            return carry

        lax.fori_loop(0, SLOTS, body, 0)

    def target(m, k, u):
        return tgs[z ^ m, 0, k * 8 + u]

    def dense_forward(t):
        def chunk(index):
            x = jnp.concatenate([rb[t][index, j % 2, j // 2] for j in range(8)], axis=1)
            w = jnp.concatenate([cc[t][index * 8 + j] for j in range(8)], axis=1)
            return fold_all(matmul(split_rows(x), w, TRANSPOSED))

        if PLANES[t] == 1:
            return chunk(0)
        return lax.fori_loop(0, PLANES[t], lambda i, total: total + chunk(i), jnp.zeros((8, 128), F32))

    def slots_forward(t, k, m, block_of):
        parts, weights = [], []
        for u in range(SLOTS):
            tag = target(m, k, u)
            live = jnp.where((tag >> 6) == t, 1.0, 0.0).astype(F32)
            parts.append(block_of(u) * live)
            weights.append(cc[t][tag & (BLOCKS[t] - 1)])
        x = jnp.concatenate(parts, axis=1)
        w = jnp.concatenate(weights, axis=1)
        return fold_all(matmul(split_rows(x), w, TRANSPOSED))

    def panel_forward(t, value, out):
        terms = fold_rows(matmul(doubled(value), ref["pc"][t - 1], TRANSPOSED))
        for u in range(SLOTS):
            out[u // 2, u % 2] = terms[:, u * 128 : (u + 1) * 128]

    def panel_backward(t, picked):
        x = jnp.concatenate([picked[u] for u in range(SLOTS)], axis=1)
        return fold_all(matmul(split_rows(x), ref["pc"][t - 1], NATURAL))

    def dense_backward(t, value2, out):
        def chunk(index, carry):
            w = jnp.concatenate([cc[t][index * 8 + j] for j in range(8)], axis=1)
            terms = fold_rows(matmul(value2, w, NATURAL))
            for j in range(8):
                out[j % 2, j // 2, index] = terms[:, j * 128 : (j + 1) * 128]
            return carry

        if PLANES[t] == 1:
            chunk(0, 0)
        else:
            lax.fori_loop(0, PLANES[t], chunk, 0)

    def slots_backward(t, k, m, value2, out, place):
        weights, lives = [], []
        for u in range(SLOTS):
            tag = target(m, k, u)
            lives.append(jnp.where((tag >> 6) == t, 1.0, 0.0).astype(F32))
            weights.append(cc[t][tag & (BLOCKS[t] - 1)])
        w = jnp.concatenate(weights, axis=1)
        terms = fold_rows(matmul(value2, w, NATURAL))
        for u in range(SLOTS):
            out[u // 2, place, u % 2] = terms[:, u * 128 : (u + 1) * 128] * lives[u]

    def reduce_send(out, into, blocks):
        st = stage.take()
        for k in (2, 1, 3):
            put(out.at[chip_y ^ k], into.at[d], st, (front ^ (2 * k)) | 1)

        @pl.when(jnp.logical_not(is_one))
        def _():
            put(out.at[chip_y], into.at[d], st, front ^ 1)

        drains.append((st, 4 * blocks, 3 * blocks))
        return st

    def reduced(st, out, into, blocks, index):
        total = out[(chip_y,) + index]
        for k in range(1, 8):
            total = total + into[(d ^ k,) + index]
        return total

    def spread(src, dst, blocks):
        st = stage.take()
        for mask in (4, 5, 2, 3, 6, 7, 1):
            put(src, dst, st, front ^ mask)
        drains.append((st, 0, 7 * blocks))
        return st

    def on_one(body):
        pl.when(is_one)(body)

    def on_zero(body):
        pl.when(jnp.logical_not(is_one))(body)

    pair = pl.ds(2 * chip_y, 2)

    def dense_send(out, into, blocks):
        st_d = stage.take()
        for mask in (4, 5, 2, 3, 6, 7, 1):
            put(out.at[core ^ (mask & 1), chip_y ^ (mask >> 1)], into.at[mask], st_d, front ^ mask)
        drains.append((st_d, 7 * blocks, 7 * blocks))
        return st_d

    def dense_total(out, into, index):
        total = out[core, chip_y, index]
        for mask in range(1, 8):
            total = total + into[mask, index]
        return total


    st_rp = [None] * 3
    st_rc = [None] * 3

    def plane_gather(t):
        st_rp[t] = stage.take()
        for mask in (4, 2, 6):
            put(rb[t].at[:, core, chip_y], rb[t].at[:, core, chip_y], st_rp[t], front ^ mask)
        drains.append((st_rp[t], 3 * PLANES[t], 3 * PLANES[t]))

    def core_gather(t):
        arrived(st_rp[t], 3 * PLANES[t])
        st_rc[t] = stage.take()
        put(rb[t].at[:, core], rb[t].at[:, core], st_rc[t], front ^ 1)
        drains.append((st_rc[t], 4 * PLANES[t], 4 * PLANES[t]))

    prepare_inverse(3)
    prepare_panel(3)
    arrived(st_rz[2], 1)
    plane_gather(2)
    arrived(st_r3, 7)
    forward3 = dense_forward(3)
    panel_forward(3, forward3, ref["up3"])
    st = reduce_send(ref["up3"], ref["ur3"], 2)
    fo_ref[:, 3, :] = forward3
    ref["fk"][3] = forward3
    arrived(st_tg, 7)
    targets_copy = pltpu.make_async_copy(ref["tgv"], tgs, load_sem.at[7])
    targets_copy.start()
    dense_backward(3, doubled(forward3), ref["sd3"])
    st_d3 = dense_send(ref["sd3"], ref["dr3"], 1)
    prepare_inverse(2)
    targets_copy.wait()
    core_gather(2)
    st_s3 = stage.take()
    st_z3 = stage.take()

    @on_one
    def _():
        arrived(st, 14)
        for i in range(2):
            total = reduced(st, ref["up3"], ref["ur3"], 2, (i,))
            ref["us3"][i] = total
            ref["s3p"][0, 2 * chip_y + i] = total
        for mask in (12, 13, 10, 11, 14, 15, 8, 9):
            put(ref["us3"], ref["s3p"].at[1, pair], st_s3, front ^ mask)
        for mask in (4, 5, 2, 3, 6, 7, 1):
            put(ref["us3"], ref["s3p"].at[0, pair], st_s3, front ^ mask)
        for m in range(2, 8):
            put(ref["us3"], ref["uz3"].at[m], st_z3, front ^ (8 * m))

    drains.append((st_s3, 0, 30))
    drains.append((st_z3, 0, 12))
    arrived(st_rz[1], 3)
    plane_gather(1)
    prepare_panel(2)
    arrived(st_rc[2], 8)
    base2 = dense_forward(2)
    quarter = pl.ds(pl.multiple_of(side * 256, 256), 256)
    panel_rows = ref["pc"][2, quarter, :]
    swapped = jnp.concatenate([panel_rows[:, 128:], panel_rows[:, :128]], axis=1)
    for j in range(8):
        product = matmul(panel_rows, cc[3][j], NATURAL) + matmul(swapped, cc[3][j], NATURAL)
        ref["gp"][j % 2, j // 2] = product
    st_gx = stage.take()

    @on_one
    def _():
        put(ref["gp"], ref["gx"], st_gx, front ^ 1)

    drains.append((st_gx, 0, 256))
    arrived_by_core(st_s3, 16, 14)

    forward2 = base2
    for m in range(2):
        forward2 = forward2 - slots_forward(2, 2, m, lambda u, m=m: ref["s3p"][m, u])
    panel_forward(2, forward2, ref["up2"])
    st = reduce_send(ref["up2"], ref["ur2"], 2)
    fo_ref[:, 2, :] = forward2
    ref["fk"][2] = forward2
    core_gather(1)
    arrived(st_rz[0], 7)
    plane_gather(0)
    st_q3 = stage.take()

    @on_one
    def _():
        arrived(st_z3, 12)
        for m in range(2, 8):
            into = ref["s3q"] if m < 4 else ref["s3r"]
            for i in range(2):
                into[m % 2 if m < 4 else m - 4, 2 * chip_y + i] = ref["uz3"][m, i]
        for mask in (4, 2, 6):
            put(ref["uz3"].at[pl.ds(2, 2)], ref["s3q"].at[:, pair], st_q3, front ^ mask)

    drains.append((st_q3, 0, 12))
    st_gr = [stage.take(), stage.take()]

    def combined_send(half):
        rows = pl.ds(128 * half, 128)
        for k in (2, 1, 3):
            put(ref["gs"].at[chip_y ^ k, :, rows], ref["gr"].at[k, :, rows], st_gr[half], front ^ (2 * k))

    drains.append((st_gr[0], 96, 0))
    drains.append((st_gr[1], 96, 0))

    @on_zero
    def _():
        arrived(st_gx, 256)

        def add_cross(y, carry):
            for c in range(2):
                ref["gs"][y, c] = ref["gp"][c, y] + ref["gx"][c, y]
            return carry

        lax.fori_loop(0, 4, add_cross, 0)
        combined_send(0)

    prepare_inverse(1)
    st_z2 = stage.take()
    st_z2b = stage.take()

    @on_one
    def _():
        arrived(st, 14)
        for i in range(2):
            ref["us2"][i] = reduced(st, ref["up2"], ref["ur2"], 2, (i,))
        for m in (2, 3, 1):
            put(ref["us2"], ref["uz2"].at[m], st_z2, front ^ (8 * m))
        for m in range(4, 8):
            put(ref["us2"], ref["uz2b"].at[m - 4], st_z2b, front ^ (8 * m))

    drains.append((st_z2, 0, 6))
    drains.append((st_z2b, 0, 8))
    st_q3c = stage.take()

    @on_one
    def _():
        arrived(st_q3, 12)
        put(ref["s3q"], ref["s3q"], st_q3c, front ^ 1)

    drains.append((st_q3c, 0, 16))
    prepare_panel(1)
    arrived(st_rc[1], 16)
    base1 = dense_forward(1)
    st_s2 = stage.take()

    @on_one
    def _():
        arrived(st_z2, 6)
        for i in range(2):
            own = ref["us2"][i] + ref["uz2"][1, i]
            other = ref["uz2"][2, i] + ref["uz2"][3, i]
            for h, total in ((0, own), (1, other)):
                ref["st2"][h, i] = total
                ref["s2p"][h, 2 * chip_y + i] = total
        for mask in (4, 5, 2, 3, 6, 7, 1):
            put(ref["st2"], ref["s2p"].at[:, pair], st_s2, front ^ mask)

    drains.append((st_s2, 0, 28))

    core_gather(0)

    @on_zero
    def _():
        arrived(st_q3c, 16)

    for m in range(4):
        src = ref["s3p"].at[m] if m < 2 else ref["s3q"].at[m - 2]
        base1 = base1 - slots_forward(1, 2, m, lambda u, src=src: src[u])
    arrived_by_core(st_s2, 16, 12)

    forward1 = base1
    for h in range(2):
        forward1 = forward1 - slots_forward(1, 1, 2 * h, lambda u, h=h: ref["s2p"][h, u])
    panel_forward(1, forward1, ref["up1"])
    st = reduce_send(ref["up1"], ref["ur1"], 2)
    fo_ref[:, 1, :] = forward1
    ref["fk"][1] = forward1
    st_q2 = stage.take()
    st_r3x = stage.take()

    @on_one
    def _():
        arrived(st_z2b, 8)
        for i in range(2):
            for h in range(2):
                total = ref["uz2b"][2 * h, i] + ref["uz2b"][2 * h + 1, i]
                ref["st2b"][h, i] = total
                ref["s2q"][h, 2 * chip_y + i] = total
        for mask in (4, 5, 2, 3, 6, 7, 1):
            put(ref["st2b"], ref["s2q"].at[:, pair], st_q2, front ^ mask)
        for mask in (4, 2, 6):
            put(ref["uz3"].at[pl.ds(4, 4)], ref["s3r"].at[:, pair], st_r3x, front ^ mask)

    drains.append((st_q2, 0, 28))
    drains.append((st_r3x, 0, 24))

    @on_zero
    def _():
        combined_send(1)

    arrived(st_d3, 7)
    solved3 = dense_total(ref["sd3"], ref["dr3"], 0)
    prepare_inverse(0)
    st_z1 = stage.take()

    @on_one
    def _():
        arrived(st, 14)
        for i in range(2):
            ref["us1"][i] = reduced(st, ref["up1"], ref["ur1"], 2, (i,))
        for m in (4, 5, 3, 6, 2, 7, 1):
            put(ref["us1"], ref["uz1"].at[m], st_z1, front ^ (8 * m))

    drains.append((st_z1, 0, 14))
    st_r3c = stage.take()

    @on_one
    def _():
        arrived(st_r3x, 24)
        put(ref["s3r"], ref["s3r"], st_r3c, front ^ 1)

    drains.append((st_r3c, 0, 32))
    base0 = jnp.zeros((8, 128), F32)
    for h in range(2):
        base0 = base0 - slots_forward(0, 1, 2 * h, lambda u, h=h: ref["s2p"][h, u])
    for m in range(4):
        src = ref["s3p"].at[m] if m < 2 else ref["s3q"].at[m - 2]
        base0 = base0 - slots_forward(0, 2, m, lambda u, src=src: src[u])
    arrived(st_rc[0], 32)
    base0 = base0 + dense_forward(0)
    st_s1 = stage.take()

    @on_one
    def _():
        arrived(st_z1, 14)
        for i in range(2):
            own = ref["us1"][i]
            for m in range(1, 4):
                own = own + ref["uz1"][m, i]
            other = ref["uz1"][4, i]
            for m in range(5, 8):
                other = other + ref["uz1"][m, i]
            for h, total in ((0, own), (1, other)):
                ref["st1"][h, i] = total
                ref["s1p"][h, 2 * chip_y + i] = total
        for mask in (4, 5, 2, 3, 6, 7, 1):
            put(ref["st1"], ref["s1p"].at[:, pair], st_s1, front ^ mask)

    drains.append((st_s1, 0, 28))

    @pl.when(jnp.logical_not(is_one))
    def _():
        arrived(st_r3c, 32)

    base0 = lax.fori_loop(
        0, 4, lambda m, total: total - slots_forward(0, 2, m + 4, lambda u: ref["s3r"][m, u]), base0
    )
    arrived_by_core(st_q2, 16, 12)
    for h in range(2):
        base0 = base0 - slots_forward(0, 1, 4 + 2 * h, lambda u, h=h: ref["s2q"][h, u])
    arrived_by_core(st_s1, 16, 12)

    forward0 = base0
    for h in range(2):
        forward0 = forward0 - slots_forward(0, 0, 4 * h, lambda u, h=h: ref["s1p"][h, u])

    value2 = doubled(forward0)
    for h in range(2):
        slots_backward(0, 0, 4 * h, value2, ref["a1"], h)
    st = reduce_send(ref["a1"], ref["ar1"], 4)
    fo_ref[:, 0, :] = forward0
    dense_backward(0, value2, ref["sd0"])
    for j in range(12):
        k = 1 if j < 4 else 2
        m = 2 * j if j < 4 else j - 4
        for u in range(SLOTS):
            tag = target(m, k, u)
            live = jnp.where((tag >> 6) == 0, 1.0, 0.0).astype(F32)
            ref["n0"][u // 2, j, u % 2] = ref["sd0"][tag & 1, (tag >> 1) & 3, (tag >> 3) & 7] * live
    st_nx = stage.take()

    @pl.when(jnp.logical_not(is_one))
    def _():
        put(ref["n0"], ref["nx0"], st_nx, front ^ 1)

    drains.append((st_nx, 96, 0))

    def chip_send(out, into, blocks):
        st_x = stage.take()
        put(out.at[1 - core], into, st_x, front ^ 1)
        drains.append((st_x, 4 * blocks, 4 * blocks))
        return st_x

    def chip_total_send(st_x, out, cross, summed, into, blocks):
        arrived(st_x, 4 * blocks)

        def body(w, carry):
            for y in range(4):
                summed[y, w] = out[core, y, w] + cross[y, w]
            return carry

        lax.fori_loop(0, blocks, body, 0)
        st_d = stage.take()
        for k in (2, 1, 3):
            put(summed.at[chip_y ^ k], into.at[k], st_d, front ^ (2 * k))
        drains.append((st_d, 3 * blocks, 3 * blocks))
        return st_d

    def plane_total(st_d, summed, into, final, blocks):
        arrived(st_d, 3 * blocks)
        for w in range(blocks):
            final[w] = (summed[chip_y, w] + into[1, w]) + (into[2, w] + into[3, w])

    st_dx0 = chip_send(ref["sd0"], ref["dx0"], 8)
    st_z = stage.take()

    @on_one
    def _():
        arrived(st, 28)
        for h in range(2):
            for i in range(2):
                ref["as1"][h, i] = reduced(st, ref["a1"], ref["ar1"], 4, (h, i))
        for m in (4, 5, 3, 6, 2, 7, 1):
            put(ref["as1"].at[m >> 2], ref["az1"].at[m], st_z, front ^ (8 * m))

    drains.append((st_z, 0, 14))
    st_ga = stage.take()

    @on_zero
    def _():
        arrived(st_gr[0], 96)
        arrived(st_gr[1], 96)
        for c in range(2):
            ref["ga"][c, side] = (ref["gs"][chip_y, c] + ref["gr"][1, c]) + (ref["gr"][2, c] + ref["gr"][3, c])
        for k in (2, 1, 3):
            put(ref["ga"].at[:, side], ref["ga"].at[:, side], st_ga, side ^ k, "rhs")

    drains.append((st_ga, 192, 0))
    st_n0 = stage.take()

    @on_one
    def _():
        arrived(st_nx, 96)

        def body(j, carry):
            for y in range(4):
                for i in range(2):
                    ref["ne0"][y, j, i] = ref["n0"][y, j, i] + ref["nx0"][y, j, i]
            return carry

        lax.fori_loop(0, 12, body, 0)
        for k in (2, 1, 3):
            put(ref["ne0"].at[chip_y ^ k], ref["nr0"].at[k], st_n0, front ^ (2 * k))

    drains.append((st_n0, 0, 72))
    st_d0 = chip_total_send(st_dx0, ref["sd0"], ref["dx0"], ref["de0"], ref["dr0"], 8)
    st_p = stage.take()

    @on_one
    def _():
        arrived(st_z, 14)
        for i in range(2):
            total = ref["as1"][0, i]
            for m in range(1, 8):
                total = total + ref["az1"][m, i]
            ref["pt1"][i] = total
            ref["pk1"][2 * chip_y + i] = total
        for mask in (4, 5, 2, 3, 6, 7, 1):
            put(ref["pt1"], ref["pk1"].at[pair], st_p, front ^ mask)

    drains.append((st_p, 0, 14))
    st_nz0 = stage.take()

    @on_one
    def _():
        arrived(st_n0, 72)

        def total_of(j, i):
            return (ref["ne0"][chip_y, j, i] + ref["nr0"][1, j, i]) + (ref["nr0"][2, j, i] + ref["nr0"][3, j, i])

        def body(m, carry):
            for i in range(2):
                ref["ns0"][m, 0, i] = total_of(m // 2, i)
                ref["ns0"][m, 1, i] = total_of(4 + m, i)
            return carry

        lax.fori_loop(0, 8, body, 0)
        for m in range(1, 8):
            put(ref["ns0"].at[m], ref["nz0"].at[m], st_nz0, front ^ (8 * m))

    drains.append((st_nz0, 0, 28))
    st_dz0 = stage.take()
    plane_total(st_d0, ref["de0"], ref["dr0"], ref["ds0"], 8)
    for m in range(1, 8):
        put(ref["ds0"].at[z ^ m], ref["dz0"].at[m], st_dz0, front ^ (8 * m))
    drains.append((st_dz0, 7, 7))
    arrived_by_core(st_p, 8, 6)

    value2 = doubled(ref["fk"][1] - panel_backward(1, ref["pk1"]))
    for h in range(2):
        slots_backward(1, 1, 2 * h, value2, ref["a2"], h)
    st = reduce_send(ref["a2"], ref["ar2"], 4)
    dense_backward(1, value2, ref["sd1"])
    for m in range(4):
        for u in range(SLOTS):
            tag = target(m, 2, u)
            live = jnp.where((tag >> 6) == 1, 1.0, 0.0).astype(F32)
            ref["n1"][u // 2, m, u % 2] = ref["sd1"][tag & 1, (tag >> 1) & 3, (tag >> 3) & 3] * live
    st_n1 = reduce_send(ref["n1"], ref["nr1"], 8)
    st_dx1 = chip_send(ref["sd1"], ref["dx1"], 4)
    st_gd = stage.take()

    @on_zero
    def _():
        arrived(st_ga, 192)
        put(ref["ga"].at[1], ref["ga"].at[1], st_gd, front ^ 1)

    drains.append((st_gd, 128, 0))

    st_z = stage.take()

    @on_one
    def _():
        arrived(st, 28)
        for h in range(2):
            for i in range(2):
                ref["as2"][h, i] = reduced(st, ref["a2"], ref["ar2"], 4, (h, i))
        for m in (2, 3, 1):
            put(ref["as2"].at[m >> 1], ref["az2"].at[m], st_z, front ^ (8 * m))

    drains.append((st_z, 0, 6))

    @on_one
    def _():
        arrived(st_nz0, 28)
        for q in range(2):
            for i in range(2):
                total = ref["ns0"][0, q, i]
                for m in range(1, 8):
                    total = total + ref["nz0"][m, q, i]
                ref["t0p"][q, i] = total

    st_d1 = chip_total_send(st_dx1, ref["sd1"], ref["dx1"], ref["de1"], ref["dr1"], 4)
    st_p = stage.take()

    @on_one
    def _():
        arrived(st_z, 6)
        for i in range(2):
            total = ref["as2"][0, i] + ref["t0p"][0, i]
            for m in range(1, 4):
                total = total + ref["az2"][m, i]
            ref["pt2"][i] = total
            ref["pk2"][2 * chip_y + i] = total
        for mask in (4, 5, 2, 3, 6, 7, 1):
            put(ref["pt2"], ref["pk2"].at[pair], st_p, front ^ mask)

    drains.append((st_p, 0, 14))
    st_nz1 = stage.take()

    @on_one
    def _():
        arrived(st_n1, 56)
        for m in range(4):
            for i in range(2):
                ref["ns1"][m, i] = reduced(st_n1, ref["n1"], ref["nr1"], 8, (m, i))
        for m in range(1, 4):
            put(ref["ns1"].at[m], ref["nz1"].at[m], st_nz1, front ^ (8 * m))

    drains.append((st_nz1, 0, 6))

    arrived(st_dz0, 7)
    total = ref["ds0"][z]
    for m in range(1, 8):
        total = total + ref["dz0"][m]
    so_ref[:, 0, :] = total
    arrived_by_core(st_p, 8, 6)

    value2 = doubled(ref["fk"][2] - panel_backward(2, ref["pk2"]))
    for h in range(2):
        slots_backward(2, 2, h, value2, ref["a3"], h)
    st = reduce_send(ref["a3"], ref["ar3"], 4)
    dense_backward(2, value2, ref["sd2"])
    st_d2 = stage.take()
    for mask in (12, 13, 14, 15, 10, 11, 8, 9, 4, 5, 6, 7, 2, 3, 1):
        put(
            ref["sd2"].at[core ^ (mask & 1), chip_y ^ ((mask >> 1) & 3), (z ^ (mask >> 3)) % 2],
            ref["dr2"].at[mask], st_d2, front ^ mask,
        )
    drains.append((st_d2, 15, 15))

    st_dz1 = stage.take()
    plane_total(st_d1, ref["de1"], ref["dr1"], ref["ds1"], 4)
    for m in range(1, 4):
        put(ref["ds1"].at[(z ^ m) % 4], ref["dz1"].at[m], st_dz1, front ^ (8 * m))
    drains.append((st_dz1, 3, 3))
    st_p = stage.take()

    @on_one
    def _():
        arrived(st_nz1, 6)
        for i in range(2):
            total = ref["ns1"][0, i] + ref["t0p"][1, i]
            for m in range(1, 4):
                total = total + ref["nz1"][m, i]
            ref["t1p"][i] = total
        arrived(st, 28)
        for i in range(2):
            ref["as3"][1, i] = reduced(st, ref["a3"], ref["ar3"], 4, (1, i))
            total = ref["t1p"][i] + reduced(st, ref["a3"], ref["ar3"], 4, (0, i))
            ref["as3"][0, i] = total
            ref["pk3"][0, 2 * chip_y + i] = total
        for mask in (12, 13, 10, 11, 14, 15, 8, 9):
            put(ref["as3"].at[1], ref["pk3"].at[1, pair], st_p, front ^ mask)
        for mask in (4, 5, 2, 3, 6, 7, 1):
            put(ref["as3"].at[0], ref["pk3"].at[0, pair], st_p, front ^ mask)

    drains.append((st_p, 0, 30))

    @on_one
    def _():
        arrived(st_gd, 128)

    def split_combined(x, carry):
        block = ref["ga"][core, x]
        high = block.astype(BF16)
        rows = pl.ds(pl.multiple_of(x * 256, 256), 256)
        ref["gc"][rows, 0:128] = high
        ref["gc"][rows, 128:256] = (block - high.astype(F32)).astype(BF16)
        return carry

    lax.fori_loop(0, 4, split_combined, 0)
    arrived(st_d2, 15)
    total = ref["sd2"][core, chip_y, z % 2]
    for mask in range(1, 16):
        total = total + ref["dr2"][mask]
    so_ref[:, 2, :] = total
    arrived(st_dz1, 3)
    total = ref["ds1"][z % 4]
    for m in range(1, 4):
        total = total + ref["dz1"][m]
    so_ref[:, 1, :] = total
    arrived_by_core(st_p, 16, 14)

    for u in range(SLOTS):
        ref["pk3"][0, u] = ref["pk3"][0, u] + ref["pk3"][1, u]
    x = jnp.concatenate([ref["pk3"][0, u] for u in range(SLOTS)], axis=1)
    so_ref[:, 3, :] = solved3 - fold_all(matmul(split_rows(x), ref["gc"][...], NATURAL))

    @on_one
    def _():
        for st_x, _zero, one in drains:
            left = one
            while left:
                drain(send_sem.at[st_x], min(left, 256))
                left -= min(left, 256)

    @pl.when(jnp.logical_not(is_one))
    def _():
        for st_x, zero, _one in drains:
            left = zero
            while left:
                drain(send_sem.at[st_x], min(left, 256))
                left -= min(left, 256)

    assert stage.count <= STAGE_COUNT


def shards(right_side, inverse_top, inverse_second, inverse_third, inverse_fourth, panels, targets):
    anywhere = pl.BlockSpec(memory_space=pl.ANY)
    results = pl.pallas_call(
        kernel,
        out_shape=pltpu.VMEM((2,) + right_side.shape, F32),
        in_specs=[anywhere] * 7,
        out_specs=pl.BlockSpec(memory_space=pltpu.VMEM),
        scratch_shapes=[pltpu.VMEM(shape, dtype) for shape, dtype in SCRATCH.values()]
        + [
            pltpu.SMEM((8, 8, 128), I32),
            pltpu.SMEM((3, 1, 8), I32),
            pltpu.SemaphoreType.DMA((STAGE_COUNT,)),
            pltpu.SemaphoreType.DMA((STAGE_COUNT,)),
            pltpu.SemaphoreType.DMA((12,)),
        ],
        compiler_params=pltpu.CompilerParams(
            collective_id=0, has_side_effects=True, vmem_limit_bytes=56 * 2**20
        ),
        name="tiers",
    )(right_side, inverse_top, inverse_second, inverse_third, inverse_fourth, panels, targets)
    return results[0], results[1]


def solution(mesh):
    placed = (
        P("rhs", None, "front"),
        P("front", None),
        P("front", None),
        P("front", None),
        P("front", None),
        P(None, None, "front"),
        P(None, "front", None),
    )
    return jax.shard_map(
        shards,
        mesh=mesh,
        in_specs=placed,
        out_specs=(P("rhs", None, "front"), P("rhs", None, "front")),
        check_vma=False,
    )
```

```python
import functools

import jax
import jax.numpy as jnp
from jax import lax
from jax.experimental import pallas as pl
from jax.experimental.pallas import tpu as pltpu
from jax.sharding import PartitionSpec as P

F32 = jnp.float32
BF16 = jnp.bfloat16
I32 = jnp.int32
MESH = pl.DeviceIdType.MESH
TIERS = 4
SLOTS = 8
BLOCKS = (64, 32, 16, 8)
PLANES = (8, 4, 2, 1)
TRANSPOSED = (((1,), (1,)), ((), ()))
NATURAL = (((1,), (0,)), ((), ()))


def split_rows(value):
    high = value.astype(BF16).astype(F32)
    return jnp.concatenate([high, value - high], axis=0).astype(BF16)


def fold_rows(value):
    return value[:8] + value[8:]


def fold_all(value):
    rows = fold_rows(value)
    sums = [
        rows[:, i : i + 128] + rows[:, i + 128 : i + 256] for i in range(0, rows.shape[1], 256)
    ]
    return sums[0] if len(sums) == 1 else jnp.concatenate(sums, axis=1)


def doubled(value):
    halves = split_rows(value)
    parts = [halves[:, i : i + 128] for i in range(0, halves.shape[1], 128)]
    return jnp.concatenate([part for part in parts for _ in range(2)], axis=1)


def matmul(left, right, dims):
    return lax.dot_general(left, right, dims, preferred_element_type=F32)


class Stage:
    def __init__(self):
        self.count = 0

    def take(self):
        self.count += 1
        return self.count - 1


STAGE_COUNT = 56

SCRATCH = dict(
    v0=((128, 8192), F32), v1=((128, 4096), F32), v2=((128, 2048), F32), v3=((128, 1024), F32),
    vp=((3, 1024, 128), F32),
    w0=((128, 8192), F32), w1=((128, 4096), F32), w2=((128, 2048), F32), wp=((2, 1024, 128), F32),
    c0=((64, 512, 128), BF16), c1=((32, 512, 128), BF16), c2=((16, 512, 128), BF16), c3=((8, 256, 128), BF16),
    pc3=((1024, 256), BF16), pc2=((1024, 512), BF16), pc1=((1024, 512), BF16),
    rb0=((8, 4, 2, 8, 128), F32), rb1=((4, 4, 2, 8, 128), F32), rb2=((2, 4, 2, 8, 128), F32), rb3=((1, 4, 2, 8, 128), F32),
    tgv=((8, 8, 128), I32),
    up3=((4, 2, 8, 128), F32), up2=((4, 2, 8, 128), F32), up1=((4, 2, 8, 128), F32),
    ur3=((8, 2, 8, 128), F32), ur2=((4, 2, 8, 128), F32), ur1=((4, 2, 8, 128), F32),
    us3=((2, 8, 128), F32), us2=((2, 8, 128), F32), us1=((2, 8, 128), F32),
    uz3=((8, 2, 8, 128), F32), uz2=((4, 2, 8, 128), F32), uz2b=((4, 2, 8, 128), F32), uz1=((8, 2, 8, 128), F32),
    s3p=((2, 8, 8, 128), F32), s3q=((2, 8, 8, 128), F32), s3r=((4, 8, 8, 128), F32),
    s2p=((2, 8, 8, 128), F32), s2q=((2, 8, 8, 128), F32), s1p=((2, 8, 8, 128), F32),
    st2=((2, 2, 8, 128), F32), st2b=((2, 2, 8, 128), F32), st1=((2, 2, 8, 128), F32),
    a1=((4, 2, 2, 8, 128), F32), a2=((4, 2, 2, 8, 128), F32), a3=((4, 2, 2, 8, 128), F32),
    ar1=((4, 2, 2, 8, 128), F32), ar2=((4, 2, 2, 8, 128), F32), ar3=((4, 2, 2, 8, 128), F32),
    as1=((2, 2, 8, 128), F32), as2=((2, 2, 8, 128), F32), as3=((2, 2, 8, 128), F32),
    az1=((8, 2, 8, 128), F32), az2=((4, 2, 8, 128), F32),
    pt1=((2, 8, 128), F32), pt2=((2, 8, 128), F32),
    pk1=((8, 8, 128), F32), pk2=((8, 8, 128), F32), pk3=((2, 8, 8, 128), F32),
    n0=((4, 12, 2, 8, 128), F32), nr0=((4, 12, 2, 8, 128), F32), ns0=((8, 2, 2, 8, 128), F32), nz0=((8, 2, 2, 8, 128), F32),
    n1=((4, 4, 2, 8, 128), F32), nr1=((4, 4, 2, 8, 128), F32), ns1=((4, 2, 8, 128), F32), nz1=((4, 2, 8, 128), F32),
    t0p=((2, 2, 8, 128), F32), t1p=((2, 8, 128), F32),
    sd0=((4, 8, 2, 8, 128), F32), sd1=((4, 4, 2, 8, 128), F32), sd2=((4, 2, 2, 8, 128), F32), sd3=((4, 1, 2, 8, 128), F32),
    dr0=((4, 8, 2, 8, 128), F32), dr1=((4, 4, 2, 8, 128), F32), dr2=((8, 2, 8, 128), F32), dr3=((8, 8, 128), F32),
    ds0=((8, 2, 8, 128), F32), ds1=((4, 2, 8, 128), F32),
    dz0=((8, 2, 8, 128), F32), dz1=((4, 2, 8, 128), F32),
    fk=((3, 8, 256), F32), fout=((3, 8, 128), F32), fin=((3, 8, 128), F32), sout=((3, 8, 128), F32), sin=((3, 8, 128), F32),
    gp=((2, 4, 256, 128), F32), gx=((2, 4, 256, 128), F32), gs=((4, 2, 256, 128), F32), gr=((4, 2, 256, 128), F32),
    ga=((2, 4, 256, 128), F32), gc=((1024, 256), BF16),
    rs=((8, 4, 128), F32),
    dummy=((256, 8, 128), F32),
)


def kernel(rs_hbm, i0_ref, i1_ref, i2_ref, i3_ref, pn_ref, tg_hbm, out_ref, *scratch):
    names = list(SCRATCH)
    ref = dict(zip(names, scratch[: len(names)]))
    tgs, tg_ref, send_sem, recv_sem, load_sem = scratch[len(names) :]
    rs_ref, fo_ref, so_ref = ref["rs"], out_ref.at[0], out_ref.at[1]
    front = lax.axis_index("front")
    side = lax.axis_index("rhs")
    core = front % 2
    chip_y = (front // 2) % 4
    d = front % 8
    z = front // 8
    is_one = core == 1
    stage = Stage()
    drains = []
    cc = [ref["c0"], ref["c1"], ref["c2"], ref["c3"]]
    rb = [ref["rb0"], ref["rb1"], ref["rb2"], ref["rb3"]]
    sd = [ref["sd0"], ref["sd1"], ref["sd2"], ref["sd3"]]
    pc = [None, ref["pc1"], ref["pc2"], ref["pc3"]]
    zz = [z, z % 4, z % 2, 0]
    pair = pl.ds(2 * chip_y, 2)

    def on_one(body):
        pl.when(is_one)(body)

    def on_zero(body):
        pl.when(jnp.logical_not(is_one))(body)

    def put(src, dst, st, to, axis="front"):
        pltpu.make_async_remote_copy(
            src_ref=src, dst_ref=dst, send_sem=send_sem.at[st], recv_sem=recv_sem.at[st],
            device_id={axis: to}, device_id_type=MESH,
        ).start()

    def drain(sem, blocks):
        while blocks:
            some = min(blocks, 256)
            piece = ref["dummy"].at[pl.ds(0, some)]
            pltpu.make_async_copy(piece, piece, sem).wait()
            blocks -= some

    def arrived(st, blocks):
        drain(recv_sem.at[st], blocks)

    def finish_sends(core_number):
        for st_x, zero, one in drains:
            drain(send_sem.at[st_x], one if core_number else zero)

    barrier = pltpu.get_barrier_semaphore()
    masks = list(range(1, 16)) + [8 * m for m in range(2, 8)]
    for mask in masks:
        pl.semaphore_signal(barrier, inc=1, device_id={"front": front ^ mask}, device_id_type=MESH)
    for k in range(1, 4):
        pl.semaphore_signal(barrier, inc=1, device_id={"rhs": side ^ k}, device_id_type=MESH)

    inverse_refs = (i0_ref, i1_ref, i2_ref, i3_ref)

    def load(name):
        t = int(name[1])
        if name[0] == "p":
            return pltpu.make_async_copy(pn_ref.at[t - 1], ref["vp"].at[t - 1], load_sem.at[t + 3])
        return pltpu.make_async_copy(inverse_refs[t], ref[name], load_sem.at[t])

    rs_copy = pltpu.make_async_copy(rs_hbm, rs_ref, load_sem.at[8])
    rs_copy.start()
    tg_copy = pltpu.make_async_copy(tg_hbm, tg_ref, load_sem.at[9])
    tg_copy.start()
    load("v3").start()
    load("p3").start()

    @on_one
    def _():
        load("v2").start()
        load("p2").start()
        load("v1").start()
        load("p1").start()
        load("v0").start()

    rs_copy.wait()
    tg_copy.wait()
    for t in range(TIERS):
        rb[t][zz[t], chip_y, core] = rs_ref[:, t, :]
    lanes = lax.broadcasted_iota(I32, (8, 128), 1)
    own_targets = jnp.full((8, 128), -1, I32)
    for k in range(3):
        for u in range(SLOTS):
            own_targets = jnp.where(lanes == k * 8 + u, tg_ref[k, 0, u], own_targets)
    ref["tgv"][z] = own_targets

    pl.semaphore_wait(barrier, len(masks) + 3)

    st_r3 = stage.take()
    for mask in (4, 5, 2, 3, 6, 7, 1):
        put(rb[3].at[0, chip_y, core], rb[3].at[0, chip_y, core], st_r3, front ^ mask)
    drains.append((st_r3, 7, 7))
    st_tg = stage.take()
    st_rc = stage.take()
    st_rz = [stage.take() for t in range(3)]
    st_w = {name: stage.take() for name in ("w2", "p2", "w1", "p1", "w0")}

    @on_zero
    def _():
        for t in (2, 1, 0):
            put(rb[t].at[zz[t], chip_y, 0], rb[t].at[zz[t], chip_y, 0], st_rc, front ^ 1)
        put(i2_ref, ref["w2"], st_w["w2"], front ^ 1)
        put(pn_ref.at[1], ref["wp"].at[1], st_w["p2"], front ^ 1)
        put(i1_ref, ref["w1"], st_w["w1"], front ^ 1)
        put(pn_ref.at[0], ref["wp"].at[0], st_w["p1"], front ^ 1)
        put(i0_ref, ref["w0"], st_w["w0"], front ^ 1)

    drains.append((st_rc, 3, 0))
    drains.append((st_w["w2"], 256, 0))
    drains.append((st_w["p2"], 128, 0))
    drains.append((st_w["w1"], 512, 0))
    drains.append((st_w["p1"], 128, 0))
    drains.append((st_w["w0"], 1024, 0))

    def prepare_third():
        load("v3").wait()

        def body(e, carry):
            block = ref["v3"][:, pl.ds(pl.multiple_of(e * 128, 128), 128)]
            high = block.astype(BF16)
            cc[3][e, 0:128, :] = high
            cc[3][e, 128:256, :] = (block - high.astype(F32)).astype(BF16)
            return carry

        lax.fori_loop(0, 8, body, 0)
        load("p3").wait()

        def body_panel(u, carry):
            rows = pl.ds(pl.multiple_of(u * 128, 128), 128)
            block = ref["vp"][2, rows, :]
            high = block.astype(BF16)
            pc[3][rows, 0:128] = high
            pc[3][rows, 128:256] = (block - high.astype(F32)).astype(BF16)
            return carry

        lax.fori_loop(0, 8, body_panel, 0)

    def prepare_inverse(t, first, last):
        if first == 0:
            load("v" + str(t)).wait()
            arrived(st_w["w" + str(t)], 16 * BLOCKS[t])

        def body(e, carry):
            columns = pl.ds(pl.multiple_of(e * 128, 128), 128)
            for i, source in ((0, ref["w" + str(t)]), (1, ref["v" + str(t)])):
                block = source[:, columns]
                high = block.astype(BF16)
                cc[t][e, 256 * i : 256 * i + 128, :] = high
                cc[t][e, 256 * i + 128 : 256 * i + 256, :] = (block - high.astype(F32)).astype(BF16)
            return carry

        lax.fori_loop(first, last, body, 0)

    def prepare_panel(t):
        load("p" + str(t)).wait()
        arrived(st_w["p" + str(t)], 128)

        def body(u, carry):
            rows = pl.ds(pl.multiple_of(u * 128, 128), 128)
            for i, source in ((0, ref["wp"]), (1, ref["vp"])):
                block = source[t - 1, rows, :]
                high = block.astype(BF16)
                pc[t][rows, 256 * i : 256 * i + 128] = high
                pc[t][rows, 256 * i + 128 : 256 * i + 256] = (block - high.astype(F32)).astype(BF16)
            return carry

        lax.fori_loop(0, SLOTS, body, 0)

    def target(m, k, u):
        return tgs[z ^ m, 0, k * 8 + u]

    def dense_forward(t):
        def chunk(index):
            x = jnp.concatenate([rb[t][index, j // 2, j % 2] for j in range(8)], axis=1)
            w = jnp.concatenate([cc[t][index * 8 + j] for j in range(8)], axis=1)
            return fold_all(matmul(split_rows(x), w, TRANSPOSED))

        if PLANES[t] == 1:
            return chunk(0)
        return lax.fori_loop(0, PLANES[t], lambda i, total: total + chunk(i), jnp.zeros((8, 256), F32))

    def slots_forward(t, k, m, block_of):
        parts, weights = [], []
        for u in range(SLOTS):
            tag = target(m, k, u)
            live = jnp.where((tag >> 6) == t, 1.0, 0.0).astype(F32)
            parts.append(block_of(u) * live)
            weights.append(cc[t][tag & (BLOCKS[t] - 1)])
        x = jnp.concatenate(parts, axis=1)
        w = jnp.concatenate(weights, axis=1)
        return fold_all(matmul(split_rows(x), w, TRANSPOSED))

    def panel_forward(t, value, out):
        terms = fold_rows(matmul(doubled(value), pc[t][...], TRANSPOSED))
        for u in range(SLOTS):
            out[u // 2, u % 2] = terms[:, u * 128 : (u + 1) * 128]

    def panel_backward(t, picked):
        x = jnp.concatenate([picked[u] for u in range(SLOTS)], axis=1)
        return fold_all(matmul(split_rows(x), pc[t][...], NATURAL))

    def dense_backward(t, value2, first, last):
        def chunk(index, carry):
            w = jnp.concatenate([cc[t][index * 8 + j] for j in range(8)], axis=1)
            terms = fold_rows(matmul(value2, w, NATURAL))
            for j in range(8):
                sd[t][j // 2, index, j % 2] = terms[:, j * 128 : (j + 1) * 128]
            return carry

        if last - first == 1:
            chunk(first, 0)
        else:
            lax.fori_loop(first, last, chunk, 0)

    def slots_backward(t, k, m, value2, out, place):
        weights, lives = [], []
        for u in range(SLOTS):
            tag = target(m, k, u)
            lives.append(jnp.where((tag >> 6) == t, 1.0, 0.0).astype(F32))
            weights.append(cc[t][tag & (BLOCKS[t] - 1)])
        w = jnp.concatenate(weights, axis=1)
        terms = fold_rows(matmul(value2, w, NATURAL))
        for u in range(SLOTS):
            out[u // 2, place, u % 2] = terms[:, u * 128 : (u + 1) * 128] * lives[u]

    def reduce_send(out, into, blocks):
        st = stage.take()
        for k in (2, 1, 3):
            put(out.at[chip_y ^ k], into.at[k], st, front ^ (2 * k))
        drains.append((st, 0, 3 * blocks))
        return st

    def reduced(out, into, index):
        return (out[(chip_y,) + index] + into[(1,) + index]) + (into[(2,) + index] + into[(3,) + index])

    def spread(src, dst, blocks):
        st = stage.take()
        for mask in (4, 2, 6):
            put(src, dst, st, front ^ mask)
        drains.append((st, 0, 3 * blocks))
        return st

    def hand_over(kind, t, value):
        st = st_out[kind][t]
        out, into, own = (ref["fout"], ref["fin"], fo_ref) if kind == 0 else (ref["sout"], ref["sin"], so_ref)
        out[t] = value[0]
        put(out.at[t], into.at[t], st, front ^ 1)
        own[:, t, :] = value[1]

    st_out = [[stage.take() for t in range(3)] for kind in range(2)]
    for kind in range(2):
        for t in range(3):
            drains.append((st_out[kind][t], 0, 1))

    st_rp = [None] * 3

    def plane_gather(t):
        arrived(st_rz[t], 2 * PLANES[t] - 2)
        st_rp[t] = stage.take()
        for mask in (4, 2, 6):
            put(rb[t].at[:, chip_y], rb[t].at[:, chip_y], st_rp[t], front ^ mask)
        drains.append((st_rp[t], 0, 6 * PLANES[t]))

    @on_one
    def _():
        arrived(st_rc, 3)
        put(rb[2].at[z % 2, chip_y], rb[2].at[z % 2, chip_y], st_rz[2], front ^ 8)
        for m in range(1, 8):
            put(ref["tgv"].at[z], ref["tgv"].at[z], st_tg, front ^ (8 * m))
        for t, count in ((1, 4), (0, 8)):
            for m in range(1, count):
                put(rb[t].at[zz[t], chip_y], rb[t].at[zz[t], chip_y], st_rz[t], front ^ (8 * m))

    for t in range(3):
        drains.append((st_rz[t], 0, 2 * PLANES[t] - 2))
    drains.append((st_tg, 0, 7))
    prepare_third()

    @on_one
    def _():
        plane_gather(2)

    arrived(st_r3, 7)
    forward3 = dense_forward(3)
    panel_forward(3, forward3, ref["up3"])
    st_u3 = stage.take()
    for k in (2, 1, 3):
        put(ref["up3"].at[chip_y ^ k], ref["ur3"].at[d], st_u3, (front ^ (2 * k)) | 1)

    @on_zero
    def _():
        put(ref["up3"].at[chip_y], ref["ur3"].at[d], st_u3, front ^ 1)

    drains.append((st_u3, 8, 6))
    fo_ref[:, 3, :] = forward3
    dense_backward(3, doubled(forward3), 0, 1)
    st_d3 = stage.take()
    for mask in (4, 5, 2, 3, 6, 7, 1):
        put(sd[3].at[chip_y ^ (mask >> 1), 0, core ^ (mask & 1)], ref["dr3"].at[mask], st_d3, front ^ mask)
    drains.append((st_d3, 7, 7))

    def combined_partial():
        quarter = pl.ds(pl.multiple_of(side * 256, 256), 256)
        panel_rows = pc[3][quarter, :]
        swapped = jnp.concatenate([panel_rows[:, 128:], panel_rows[:, :128]], axis=1)
        for j in range(8):
            product = matmul(panel_rows, cc[3][j], NATURAL) + matmul(swapped, cc[3][j], NATURAL)
            ref["gp"][j % 2, j // 2] = product

    def split_combined():
        def body(x, carry):
            block = ref["ga"][core, x]
            high = block.astype(BF16)
            rows = pl.ds(pl.multiple_of(x * 256, 256), 256)
            ref["gc"][rows, 0:128] = high
            ref["gc"][rows, 128:256] = (block - high.astype(F32)).astype(BF16)
            return carry

        lax.fori_loop(0, 4, body, 0)

    def third_total():
        arrived(st_d3, 7)
        total = sd[3][chip_y, 0, core]
        for mask in range(1, 8):
            total = total + ref["dr3"][mask]
        return total

    def third_finish(solved3):
        x = jnp.concatenate([ref["pk3"][0, u] + ref["pk3"][1, u] for u in range(SLOTS)], axis=1)
        so_ref[:, 3, :] = solved3 - fold_all(matmul(split_rows(x), ref["gc"][...], NATURAL))

    st_gx = stage.take()
    drains.append((st_gx, 0, 256))
    st_gr = [stage.take(), stage.take()]
    drains.append((st_gr[0], 96, 0))
    drains.append((st_gr[1], 96, 0))
    st_ga = stage.take()
    drains.append((st_ga, 192, 0))
    st_gd = stage.take()
    drains.append((st_gd, 128, 0))
    st_p3 = stage.take()

    @on_zero
    def _():
        combined_partial()
        arrived(st_gx, 256)

        def add_cross(y, carry):
            for c in range(2):
                ref["gs"][y, c] = ref["gp"][c, y] + ref["gx"][c, y]
            return carry

        lax.fori_loop(0, 4, add_cross, 0)

        def combined_send(half):
            rows = pl.ds(128 * half, 128)
            for k in (2, 1, 3):
                put(ref["gs"].at[chip_y ^ k, :, rows], ref["gr"].at[k, :, rows], st_gr[half], front ^ (2 * k))

        arrived(st_out[0][2], 1)
        fo_ref[:, 2, :] = ref["fin"][2]
        combined_send(0)
        arrived(st_out[0][1], 1)
        fo_ref[:, 1, :] = ref["fin"][1]
        combined_send(1)
        solved3 = third_total()
        arrived(st_out[0][0], 1)
        fo_ref[:, 0, :] = ref["fin"][0]
        arrived(st_gr[0], 96)
        arrived(st_gr[1], 96)
        for c in range(2):
            ref["ga"][c, side] = (ref["gs"][chip_y, c] + ref["gr"][1, c]) + (ref["gr"][2, c] + ref["gr"][3, c])
        for k in (2, 1, 3):
            put(ref["ga"].at[:, side], ref["ga"].at[:, side], st_ga, side ^ k, "rhs")
        arrived(st_ga, 192)
        put(ref["ga"].at[1], ref["ga"].at[1], st_gd, front ^ 1)
        split_combined()
        finish_sends(0)
        for t in (0, 1):
            arrived(st_out[1][t], 1)
            so_ref[:, t, :] = ref["sin"][t]
        arrived(st_p3, 16)
        third_finish(solved3)
        arrived(st_out[1][2], 1)
        so_ref[:, 2, :] = ref["sin"][2]

    @on_one
    def _():
        arrived(st_tg, 7)
        targets_copy = pltpu.make_async_copy(ref["tgv"], tgs, load_sem.at[7])
        targets_copy.start()
        prepare_inverse(2, 0, 16)
        targets_copy.wait()
        arrived(st_u3, 14)
        for i in range(2):
            total = ref["up3"][chip_y, i]
            for k in range(1, 8):
                total = total + ref["ur3"][d ^ k, i]
            ref["us3"][i] = total
            ref["s3p"][0, 2 * chip_y + i] = total
        st_s3 = stage.take()
        for mask in (12, 10, 14, 8):
            put(ref["us3"], ref["s3p"].at[1, pair], st_s3, front ^ mask)
        for mask in (4, 2, 6):
            put(ref["us3"], ref["s3p"].at[0, pair], st_s3, front ^ mask)
        drains.append((st_s3, 0, 14))
        st_z3 = stage.take()
        for m in range(2, 8):
            put(ref["us3"], ref["uz3"].at[m], st_z3, front ^ (8 * m))
        drains.append((st_z3, 0, 12))
        plane_gather(1)
        prepare_panel(2)
        arrived(st_rp[2], 12)
        base2 = dense_forward(2)
        combined_partial()
        put(ref["gp"], ref["gx"], st_gx, front ^ 1)
        arrived(st_s3, 14)

        forward = base2
        for m in range(2):
            forward = forward - slots_forward(2, 2, m, lambda u, m=m: ref["s3p"][m, u])
        panel_forward(2, forward, ref["up2"])
        st = reduce_send(ref["up2"], ref["ur2"], 2)
        ref["fk"][2] = forward
        hand_over(0, 2, (forward[:, :128], forward[:, 128:]))
        plane_gather(0)
        arrived(st_z3, 12)
        for m in range(2, 8):
            into = ref["s3q"] if m < 4 else ref["s3r"]
            for i in range(2):
                into[m % 2 if m < 4 else m - 4, 2 * chip_y + i] = ref["uz3"][m, i]
        st_q3 = spread(ref["uz3"].at[pl.ds(2, 2)], ref["s3q"].at[:, pair], 4)
        prepare_inverse(1, 0, 32)
        arrived(st, 6)
        for i in range(2):
            ref["us2"][i] = reduced(ref["up2"], ref["ur2"], (i,))
        st_z2, st_z2b = stage.take(), stage.take()
        for m in (2, 3, 1):
            put(ref["us2"], ref["uz2"].at[m], st_z2, front ^ (8 * m))
        for m in range(4, 8):
            put(ref["us2"], ref["uz2b"].at[m - 4], st_z2b, front ^ (8 * m))
        drains.append((st_z2, 0, 6))
        drains.append((st_z2b, 0, 8))
        prepare_panel(1)
        arrived(st_rp[1], 24)
        base1 = dense_forward(1)
        arrived(st_z2, 6)
        for i in range(2):
            own = ref["us2"][i] + ref["uz2"][1, i]
            other = ref["uz2"][2, i] + ref["uz2"][3, i]
            for h, total in ((0, own), (1, other)):
                ref["st2"][h, i] = total
                ref["s2p"][h, 2 * chip_y + i] = total
        st_s2 = spread(ref["st2"], ref["s2p"].at[:, pair], 4)
        arrived(st_q3, 12)
        for m in range(4):
            src = ref["s3p"].at[m] if m < 2 else ref["s3q"].at[m - 2]
            base1 = base1 - slots_forward(1, 2, m, lambda u, src=src: src[u])
        prepare_inverse(0, 0, 24)
        arrived(st_s2, 12)

        forward = base1
        for h in range(2):
            forward = forward - slots_forward(1, 1, 2 * h, lambda u, h=h: ref["s2p"][h, u])
        panel_forward(1, forward, ref["up1"])
        st = reduce_send(ref["up1"], ref["ur1"], 2)
        ref["fk"][1] = forward
        hand_over(0, 1, (forward[:, :128], forward[:, 128:]))
        arrived(st_z2b, 8)
        for i in range(2):
            for h in range(2):
                total = ref["uz2b"][2 * h, i] + ref["uz2b"][2 * h + 1, i]
                ref["st2b"][h, i] = total
                ref["s2q"][h, 2 * chip_y + i] = total
        st_q2 = spread(ref["st2b"], ref["s2q"].at[:, pair], 4)
        st_r3x = spread(ref["uz3"].at[pl.ds(4, 4)], ref["s3r"].at[:, pair], 8)
        prepare_inverse(0, 24, 64)
        arrived(st, 6)
        for i in range(2):
            ref["us1"][i] = reduced(ref["up1"], ref["ur1"], (i,))
        st_z1 = stage.take()
        for m in (4, 5, 3, 6, 2, 7, 1):
            put(ref["us1"], ref["uz1"].at[m], st_z1, front ^ (8 * m))
        drains.append((st_z1, 0, 14))
        base0 = jnp.zeros((8, 256), F32)
        for h in range(2):
            base0 = base0 - slots_forward(0, 1, 2 * h, lambda u, h=h: ref["s2p"][h, u])
        for m in range(4):
            src = ref["s3p"].at[m] if m < 2 else ref["s3q"].at[m - 2]
            base0 = base0 - slots_forward(0, 2, m, lambda u, src=src: src[u])
        arrived(st_rp[0], 48)
        base0 = base0 + dense_forward(0)
        arrived(st_z1, 14)
        for i in range(2):
            own = ref["us1"][i]
            for m in range(1, 4):
                own = own + ref["uz1"][m, i]
            other = ref["uz1"][4, i]
            for m in range(5, 8):
                other = other + ref["uz1"][m, i]
            for h, total in ((0, own), (1, other)):
                ref["st1"][h, i] = total
                ref["s1p"][h, 2 * chip_y + i] = total
        st_s1 = spread(ref["st1"], ref["s1p"].at[:, pair], 4)
        arrived(st_r3x, 24)
        base0 = lax.fori_loop(
            0, 4, lambda m, total: total - slots_forward(0, 2, m + 4, lambda u: ref["s3r"][m, u]), base0
        )
        arrived(st_q2, 12)
        for h in range(2):
            base0 = base0 - slots_forward(0, 1, 4 + 2 * h, lambda u, h=h: ref["s2q"][h, u])
        arrived(st_s1, 12)

        forward = base0
        for h in range(2):
            forward = forward - slots_forward(0, 0, 4 * h, lambda u, h=h: ref["s1p"][h, u])

        value2 = doubled(forward)
        for h in range(2):
            slots_backward(0, 0, 4 * h, value2, ref["a1"], h)
        st = reduce_send(ref["a1"], ref["ar1"], 4)
        hand_over(0, 0, (forward[:, :128], forward[:, 128:]))
        dense_backward(0, value2, 0, 5)
        arrived(st, 12)
        for h in range(2):
            for i in range(2):
                ref["as1"][h, i] = reduced(ref["a1"], ref["ar1"], (h, i))
        st_z = stage.take()
        for m in (4, 5, 3, 6, 2, 7, 1):
            put(ref["as1"].at[m >> 2], ref["az1"].at[m], st_z, front ^ (8 * m))
        drains.append((st_z, 0, 14))
        dense_backward(0, value2, 5, 8)

        def pick(t, planes, out, place, m, k):
            for u in range(SLOTS):
                tag = target(m, k, u)
                live = jnp.where((tag >> 6) == t, 1.0, 0.0).astype(F32)
                block = sd[t][(tag >> 1) & 3, (tag >> 3) & (planes - 1), tag & 1]
                out[u // 2, place, u % 2] = block * live

        for j in range(12):
            pick(0, 8, ref["n0"], j, 2 * j if j < 4 else j - 4, 1 if j < 4 else 2)
        st_n0 = reduce_send(ref["n0"], ref["nr0"], 24)
        st_d0 = reduce_send(sd[0], ref["dr0"], 16)
        arrived(st_z, 14)
        for i in range(2):
            total = ref["as1"][0, i]
            for m in range(1, 8):
                total = total + ref["az1"][m, i]
            ref["pt1"][i] = total
            ref["pk1"][2 * chip_y + i] = total
        st_p = spread(ref["pt1"], ref["pk1"].at[pair], 2)
        arrived(st_p, 6)

        value2 = doubled(ref["fk"][1] - panel_backward(1, ref["pk1"]))
        for h in range(2):
            slots_backward(1, 1, 2 * h, value2, ref["a2"], h)
        st = reduce_send(ref["a2"], ref["ar2"], 4)
        arrived(st_n0, 72)

        def background_sums(m, carry):
            for i in range(2):
                ref["ns0"][m, 0, i] = reduced(ref["n0"], ref["nr0"], (m // 2, i))
                ref["ns0"][m, 1, i] = reduced(ref["n0"], ref["nr0"], (4 + m, i))
            return carry

        lax.fori_loop(0, 8, background_sums, 0)
        st_nz0 = stage.take()
        for m in (4, 5, 3, 6, 2, 7, 1):
            put(ref["ns0"].at[m], ref["nz0"].at[m], st_nz0, front ^ (8 * m))
        drains.append((st_nz0, 0, 28))
        dense_backward(1, value2, 0, 4)
        for m in range(4):
            pick(1, 4, ref["n1"], m, m, 2)
        st_n1 = reduce_send(ref["n1"], ref["nr1"], 8)
        arrived(st, 12)
        for h in range(2):
            for i in range(2):
                ref["as2"][h, i] = reduced(ref["a2"], ref["ar2"], (h, i))
        st_z = stage.take()
        for m in (2, 3, 1):
            put(ref["as2"].at[m >> 1], ref["az2"].at[m], st_z, front ^ (8 * m))
        drains.append((st_z, 0, 6))
        st_d1 = reduce_send(sd[1], ref["dr1"], 8)

        def plane_totals(st_d, t, into, final, st_f):
            arrived(st_d, 6 * PLANES[t])
            for w in range(PLANES[t]):
                for c in range(2):
                    final[w, c] = reduced(sd[t], into, (w, c))

        plane_totals(st_d0, 0, ref["dr0"], ref["ds0"], None)
        st_dz0 = stage.take()
        for m in (4, 5, 3, 6, 2, 7, 1):
            put(ref["ds0"].at[z ^ m], ref["dz0"].at[m], st_dz0, front ^ (8 * m))
        drains.append((st_dz0, 0, 14))
        arrived(st_nz0, 28)
        for q in range(2):
            for i in range(2):
                total = ref["ns0"][0, q, i]
                for m in range(1, 8):
                    total = total + ref["nz0"][m, q, i]
                ref["t0p"][q, i] = total
        arrived(st_z, 6)
        for i in range(2):
            total = ref["as2"][0, i] + ref["t0p"][0, i]
            for m in range(1, 4):
                total = total + ref["az2"][m, i]
            ref["pt2"][i] = total
            ref["pk2"][2 * chip_y + i] = total
        st_p = spread(ref["pt2"], ref["pk2"].at[pair], 2)
        arrived(st_n1, 24)
        for m in range(4):
            for i in range(2):
                ref["ns1"][m, i] = reduced(ref["n1"], ref["nr1"], (m, i))
        st_nz1 = stage.take()
        for m in (2, 3, 1):
            put(ref["ns1"].at[m], ref["nz1"].at[m], st_nz1, front ^ (8 * m))
        drains.append((st_nz1, 0, 6))
        plane_totals(st_d1, 1, ref["dr1"], ref["ds1"], None)
        st_dz1 = stage.take()
        for m in (2, 3, 1):
            put(ref["ds1"].at[(z ^ m) % 4], ref["dz1"].at[m], st_dz1, front ^ (8 * m))
        drains.append((st_dz1, 0, 6))
        arrived(st_p, 6)

        value2 = doubled(ref["fk"][2] - panel_backward(2, ref["pk2"]))
        for h in range(2):
            slots_backward(2, 2, h, value2, ref["a3"], h)
        st = reduce_send(ref["a3"], ref["ar3"], 4)
        dense_backward(2, value2, 0, 2)
        st_d2 = stage.take()
        for mask in (12, 14, 10, 8, 4, 6, 2):
            put(
                sd[2].at[chip_y ^ ((mask >> 1) & 3), (z ^ (mask >> 3)) % 2],
                ref["dr2"].at[mask >> 1], st_d2, front ^ mask,
            )
        drains.append((st_d2, 0, 14))
        arrived(st_nz1, 6)
        for i in range(2):
            total = ref["ns1"][0, i] + ref["t0p"][1, i]
            for m in range(1, 4):
                total = total + ref["nz1"][m, i]
            ref["t1p"][i] = total
        arrived(st, 12)
        for i in range(2):
            ref["as3"][1, i] = reduced(ref["a3"], ref["ar3"], (1, i))
            total = ref["t1p"][i] + reduced(ref["a3"], ref["ar3"], (0, i))
            ref["as3"][0, i] = total
            ref["pk3"][0, 2 * chip_y + i] = total
        for mask in (12, 13, 10, 11, 14, 15, 8, 9):
            put(ref["as3"].at[1], ref["pk3"].at[1, pair], st_p3, front ^ mask)
        for mask in (4, 5, 2, 3, 6, 7, 1):
            put(ref["as3"].at[0], ref["pk3"].at[0, pair], st_p3, front ^ mask)
        arrived(st_dz0, 14)
        totals = []
        for c in range(2):
            total = ref["ds0"][z, c]
            for m in range(1, 8):
                total = total + ref["dz0"][m, c]
            totals.append(total)
        hand_over(1, 0, totals)
        arrived(st_dz1, 6)
        totals = []
        for c in range(2):
            total = ref["ds1"][z % 4, c]
            for m in range(1, 4):
                total = total + ref["dz1"][m, c]
            totals.append(total)
        hand_over(1, 1, totals)
        arrived(st_d2, 14)
        totals = []
        for c in range(2):
            total = sd[2][chip_y, z % 2, c]
            for m in range(1, 8):
                total = total + ref["dr2"][m, c]
            totals.append(total)
        hand_over(1, 2, totals)
        solved3 = third_total()
        arrived(st_gd, 128)
        split_combined()
        finish_sends(1)
        arrived(st_p3, 14)
        third_finish(solved3)
        drain(send_sem.at[st_p3], 30)

    assert stage.count <= STAGE_COUNT


def shards(right_side, inverse_top, inverse_second, inverse_third, inverse_fourth, panels, targets):
    anywhere = pl.BlockSpec(memory_space=pl.ANY)
    results = pl.pallas_call(
        kernel,
        out_shape=pltpu.VMEM((2,) + right_side.shape, F32),
        in_specs=[anywhere] * 7,
        out_specs=pl.BlockSpec(memory_space=pltpu.VMEM),
        scratch_shapes=[pltpu.VMEM(shape, dtype) for shape, dtype in SCRATCH.values()]
        + [
            pltpu.SMEM((8, 8, 128), I32),
            pltpu.SMEM((3, 1, 8), I32),
            pltpu.SemaphoreType.DMA((STAGE_COUNT,)),
            pltpu.SemaphoreType.DMA((STAGE_COUNT,)),
            pltpu.SemaphoreType.DMA((12,)),
        ],
        compiler_params=pltpu.CompilerParams(
            collective_id=0, has_side_effects=True, vmem_limit_bytes=56 * 2**20
        ),
        name="tiers",
    )(right_side, inverse_top, inverse_second, inverse_third, inverse_fourth, panels, targets)
    return results[0], results[1]


def solution(mesh):
    placed = (
        P("rhs", None, "front"),
        P("front", None),
        P("front", None),
        P("front", None),
        P("front", None),
        P(None, None, "front"),
        P(None, "front", None),
    )
    return jax.shard_map(
        shards,
        mesh=mesh,
        in_specs=placed,
        out_specs=(P("rhs", None, "front"), P("rhs", None, "front")),
        check_vma=False,
    )
```

```python
import functools

import jax
import jax.numpy as jnp
from jax import lax
from jax.experimental import pallas as pl
from jax.experimental.pallas import tpu as pltpu
from jax.sharding import PartitionSpec as P

F32 = jnp.float32
BF16 = jnp.bfloat16
I32 = jnp.int32
MESH = pl.DeviceIdType.MESH
TIERS = 4
SLOTS = 8
BLOCKS = (64, 32, 16, 8)
PLANES = (8, 4, 2, 1)
TRANSPOSED = (((1,), (1,)), ((), ()))
NATURAL = (((1,), (0,)), ((), ()))


def split_rows(value):
    high = value.astype(BF16).astype(F32)
    return jnp.concatenate([high, value - high], axis=0).astype(BF16)


def fold_rows(value):
    return value[:8] + value[8:]


def fold_all(value):
    rows = fold_rows(value)
    sums = [
        rows[:, i : i + 128] + rows[:, i + 128 : i + 256] for i in range(0, rows.shape[1], 256)
    ]
    return sums[0] if len(sums) == 1 else jnp.concatenate(sums, axis=1)


def doubled(value):
    halves = split_rows(value)
    parts = [halves[:, i : i + 128] for i in range(0, halves.shape[1], 128)]
    return jnp.concatenate([part for part in parts for _ in range(2)], axis=1)


def matmul(left, right, dims):
    return lax.dot_general(left, right, dims, preferred_element_type=F32)


class Stage:
    def __init__(self):
        self.count = 0

    def take(self):
        self.count += 1
        return self.count - 1


STAGE_COUNT = 56

SCRATCH = dict(
    v0=((128, 8192), F32), v1=((128, 4096), F32), v2=((128, 2048), F32), v3=((128, 1024), F32),
    vp=((3, 1024, 128), F32),
    w0=((128, 8192), F32), w1=((128, 4096), F32), w2=((128, 2048), F32), wp=((2, 1024, 128), F32),
    c0=((64, 512, 128), BF16), c1=((32, 512, 128), BF16), c2=((16, 512, 128), BF16), c3=((8, 256, 128), BF16),
    pc3=((1024, 256), BF16), pc2=((1024, 512), BF16), pc1=((1024, 512), BF16),
    rb0=((8, 4, 2, 8, 128), F32), rb1=((4, 4, 2, 8, 128), F32), rb2=((2, 4, 2, 8, 128), F32), rb3=((1, 4, 2, 8, 128), F32),
    tgv=((8, 8, 128), I32),
    up3=((4, 2, 8, 128), F32), up2=((4, 2, 8, 128), F32), up1=((4, 2, 8, 128), F32),
    ur3=((8, 2, 8, 128), F32), ur2=((4, 2, 8, 128), F32), ur1=((4, 2, 8, 128), F32),
    us3=((2, 8, 128), F32), us2=((2, 8, 128), F32), us1=((2, 8, 128), F32),
    uz3=((8, 2, 8, 128), F32), uz2=((4, 2, 8, 128), F32), uz2b=((4, 2, 8, 128), F32), uz1=((8, 2, 8, 128), F32),
    s3p=((2, 8, 8, 128), F32), s3q=((2, 8, 8, 128), F32), s3r=((4, 8, 8, 128), F32),
    s2p=((2, 8, 8, 128), F32), s2q=((2, 8, 8, 128), F32), s1p=((2, 8, 8, 128), F32),
    st2=((2, 2, 8, 128), F32), st2b=((2, 2, 8, 128), F32), st1=((2, 2, 8, 128), F32),
    a1=((4, 2, 2, 8, 128), F32), a2=((4, 2, 2, 8, 128), F32), a3=((4, 2, 2, 8, 128), F32),
    ar1=((4, 2, 2, 8, 128), F32), ar2=((4, 2, 2, 8, 128), F32), ar3=((4, 2, 2, 8, 128), F32),
    as1=((2, 2, 8, 128), F32), as2=((2, 2, 8, 128), F32), as3=((2, 2, 8, 128), F32),
    az1=((8, 2, 8, 128), F32), az2=((4, 2, 8, 128), F32),
    pt1=((2, 8, 128), F32), pt2=((2, 8, 128), F32),
    pk1=((8, 8, 128), F32), pk2=((8, 8, 128), F32), pk3=((2, 8, 8, 128), F32),
    n0=((4, 12, 2, 8, 128), F32), nr0=((4, 12, 2, 8, 128), F32), ns0=((8, 2, 2, 8, 128), F32), nz0=((8, 2, 2, 8, 128), F32),
    n1=((4, 4, 2, 8, 128), F32), nr1=((4, 4, 2, 8, 128), F32), ns1=((4, 2, 8, 128), F32), nz1=((4, 2, 8, 128), F32),
    t0p=((2, 2, 8, 128), F32), t1p=((2, 8, 128), F32),
    sd0=((4, 8, 2, 8, 128), F32), sd1=((4, 4, 2, 8, 128), F32), sd2=((4, 2, 2, 8, 128), F32), sd3=((4, 1, 2, 8, 128), F32),
    dr0=((4, 8, 2, 8, 128), F32), dr1=((4, 4, 2, 8, 128), F32), dr2=((8, 2, 8, 128), F32), dr3=((8, 8, 128), F32),
    ds0=((8, 2, 8, 128), F32), ds1=((4, 2, 8, 128), F32),
    dz0=((8, 2, 8, 128), F32), dz1=((4, 2, 8, 128), F32),
    fk=((3, 8, 256), F32), fout=((3, 8, 128), F32), fin=((3, 8, 128), F32), sout=((3, 8, 128), F32), sin=((3, 8, 128), F32),
    gp=((2, 4, 256, 128), F32), gx=((2, 4, 256, 128), F32), gs=((4, 2, 256, 128), F32), gr=((4, 2, 256, 128), F32),
    ga=((2, 4, 256, 128), F32), gc=((1024, 256), BF16),
    rs=((8, 4, 128), F32),
    wt0=((2048, 512), BF16), wt1=((2048, 512), BF16), wt2=((2048, 512), BF16),
    dummy=((256, 8, 128), F32),
)


def kernel(rs_hbm, i0_ref, i1_ref, i2_ref, i3_ref, pn_ref, tg_hbm, out_ref, *scratch):
    names = list(SCRATCH)
    ref = dict(zip(names, scratch[: len(names)]))
    tgs, tg_ref, send_sem, recv_sem, load_sem = scratch[len(names) :]
    rs_ref, fo_ref, so_ref = ref["rs"], out_ref.at[0], out_ref.at[1]
    front = lax.axis_index("front")
    side = lax.axis_index("rhs")
    core = front % 2
    chip_y = (front // 2) % 4
    d = front % 8
    z = front // 8
    is_one = core == 1
    stage = Stage()
    drains = []
    cc = [ref["c0"], ref["c1"], ref["c2"], ref["c3"]]
    rb = [ref["rb0"], ref["rb1"], ref["rb2"], ref["rb3"]]
    sd = [ref["sd0"], ref["sd1"], ref["sd2"], ref["sd3"]]
    pc = [None, ref["pc1"], ref["pc2"], ref["pc3"]]
    zz = [z, z % 4, z % 2, 0]
    pair = pl.ds(2 * chip_y, 2)

    def on_one(body):
        pl.when(is_one)(body)

    def on_zero(body):
        pl.when(jnp.logical_not(is_one))(body)

    def put(src, dst, st, to, axis="front"):
        pltpu.make_async_remote_copy(
            src_ref=src, dst_ref=dst, send_sem=send_sem.at[st], recv_sem=recv_sem.at[st],
            device_id={axis: to}, device_id_type=MESH,
        ).start()

    def drain(sem, blocks):
        while blocks:
            some = min(blocks, 256)
            piece = ref["dummy"].at[pl.ds(0, some)]
            pltpu.make_async_copy(piece, piece, sem).wait()
            blocks -= some

    def arrived(st, blocks):
        drain(recv_sem.at[st], blocks)

    def finish_sends(core_number):
        for st_x, zero, one in drains:
            drain(send_sem.at[st_x], one if core_number else zero)

    barrier = pltpu.get_barrier_semaphore()
    masks = list(range(1, 16)) + [8 * m for m in range(2, 8)]
    for mask in masks:
        pl.semaphore_signal(barrier, inc=1, device_id={"front": front ^ mask}, device_id_type=MESH)
    for k in range(1, 4):
        pl.semaphore_signal(barrier, inc=1, device_id={"rhs": side ^ k}, device_id_type=MESH)

    inverse_refs = (i0_ref, i1_ref, i2_ref, i3_ref)

    def load(name):
        t = int(name[1])
        if name[0] == "p":
            return pltpu.make_async_copy(pn_ref.at[t - 1], ref["vp"].at[t - 1], load_sem.at[t + 3])
        return pltpu.make_async_copy(inverse_refs[t], ref[name], load_sem.at[t])

    rs_copy = pltpu.make_async_copy(rs_hbm, rs_ref, load_sem.at[8])
    rs_copy.start()
    tg_copy = pltpu.make_async_copy(tg_hbm, tg_ref, load_sem.at[9])
    tg_copy.start()
    load("v3").start()
    load("p3").start()

    @on_one
    def _():
        load("v2").start()
        load("p2").start()
        load("v1").start()
        load("p1").start()
        load("v0").start()

    rs_copy.wait()
    tg_copy.wait()
    for t in range(TIERS):
        rb[t][zz[t], chip_y, core] = rs_ref[:, t, :]
    lanes = lax.broadcasted_iota(I32, (8, 128), 1)
    own_targets = jnp.full((8, 128), -1, I32)
    for k in range(3):
        for u in range(SLOTS):
            own_targets = jnp.where(lanes == k * 8 + u, tg_ref[k, 0, u], own_targets)
    ref["tgv"][z] = own_targets

    pl.semaphore_wait(barrier, len(masks) + 3)

    st_r3 = stage.take()
    for mask in (4, 5, 2, 3, 6, 7, 1):
        put(rb[3].at[0, chip_y, core], rb[3].at[0, chip_y, core], st_r3, front ^ mask)
    drains.append((st_r3, 7, 7))
    st_tg = stage.take()
    st_rc = stage.take()
    st_rz = [stage.take() for t in range(3)]
    st_w = {name: stage.take() for name in ("w2", "p2", "w1", "p1", "w0")}

    @on_zero
    def _():
        for t in (2, 1, 0):
            put(rb[t].at[zz[t], chip_y, 0], rb[t].at[zz[t], chip_y, 0], st_rc, front ^ 1)
        put(i2_ref, ref["w2"], st_w["w2"], front ^ 1)
        put(pn_ref.at[1], ref["wp"].at[1], st_w["p2"], front ^ 1)
        put(i1_ref, ref["w1"], st_w["w1"], front ^ 1)
        put(pn_ref.at[0], ref["wp"].at[0], st_w["p1"], front ^ 1)
        put(i0_ref, ref["w0"], st_w["w0"], front ^ 1)

    drains.append((st_rc, 3, 0))
    drains.append((st_w["w2"], 256, 0))
    drains.append((st_w["p2"], 128, 0))
    drains.append((st_w["w1"], 512, 0))
    drains.append((st_w["p1"], 128, 0))
    drains.append((st_w["w0"], 1024, 0))

    def prepare_third():
        load("v3").wait()

        def body(e, carry):
            block = ref["v3"][:, pl.ds(pl.multiple_of(e * 128, 128), 128)]
            high = block.astype(BF16)
            cc[3][e, 0:128, :] = high
            cc[3][e, 128:256, :] = (block - high.astype(F32)).astype(BF16)
            return carry

        lax.fori_loop(0, 8, body, 0)
        load("p3").wait()

        def body_panel(u, carry):
            rows = pl.ds(pl.multiple_of(u * 128, 128), 128)
            block = ref["vp"][2, rows, :]
            high = block.astype(BF16)
            pc[3][rows, 0:128] = high
            pc[3][rows, 128:256] = (block - high.astype(F32)).astype(BF16)
            return carry

        lax.fori_loop(0, 8, body_panel, 0)

    def prepare_inverse(t, first, last):
        if first == 0:
            load("v" + str(t)).wait()
            arrived(st_w["w" + str(t)], 16 * BLOCKS[t])

        def body(e, carry):
            columns = pl.ds(pl.multiple_of(e * 128, 128), 128)
            for i, source in ((0, ref["w" + str(t)]), (1, ref["v" + str(t)])):
                block = source[:, columns]
                high = block.astype(BF16)
                cc[t][e, 256 * i : 256 * i + 128, :] = high
                cc[t][e, 256 * i + 128 : 256 * i + 256, :] = (block - high.astype(F32)).astype(BF16)
            return carry

        lax.fori_loop(first, last, body, 0)

    def prepare_panel(t):
        load("p" + str(t)).wait()
        arrived(st_w["p" + str(t)], 128)

        def body(u, carry):
            rows = pl.ds(pl.multiple_of(u * 128, 128), 128)
            for i, source in ((0, ref["wp"]), (1, ref["vp"])):
                block = source[t - 1, rows, :]
                high = block.astype(BF16)
                pc[t][rows, 256 * i : 256 * i + 128] = high
                pc[t][rows, 256 * i + 128 : 256 * i + 256] = (block - high.astype(F32)).astype(BF16)
            return carry

        lax.fori_loop(0, SLOTS, body, 0)

    def target(m, k, u):
        return tgs[z ^ m, 0, k * 8 + u]

    def dense_forward(t):
        def chunk(index):
            x = jnp.concatenate([rb[t][index, j // 2, j % 2] for j in range(8)], axis=1)
            w = jnp.concatenate([cc[t][index * 8 + j] for j in range(8)], axis=1)
            return fold_all(matmul(split_rows(x), w, TRANSPOSED))

        if PLANES[t] == 1:
            return chunk(0)
        return lax.fori_loop(0, PLANES[t], lambda i, total: total + chunk(i), jnp.zeros((8, 256), F32))

    def slots_forward(t, k, m, block_of):
        parts, weights = [], []
        for u in range(SLOTS):
            tag = target(m, k, u)
            live = jnp.where((tag >> 6) == t, 1.0, 0.0).astype(F32)
            parts.append(block_of(u) * live)
            weights.append(cc[t][tag & (BLOCKS[t] - 1)])
        x = jnp.concatenate(parts, axis=1)
        w = jnp.concatenate(weights, axis=1)
        return fold_all(matmul(split_rows(x), w, TRANSPOSED))

    def turn_slots(t, k, fronts):
        for h, m in fronts:
            for u in range(SLOTS):
                block = cc[t][target(m, k, u) & (BLOCKS[t] - 1)]
                first = (h * SLOTS + u) * 128
                ref["wt" + str(t)][first : first + 128, :] = block.T

    def turned_forward(t, k, fronts, sums):
        parts = []
        for h, m in fronts:
            for u in range(SLOTS):
                live = jnp.where((target(m, k, u) >> 6) == t, 1.0, 0.0).astype(F32)
                parts.append(sums[h, u] * live)
        x = jnp.concatenate(parts, axis=1)
        return fold_all(matmul(split_rows(x), ref["wt" + str(t)][...], NATURAL))

    def panel_forward(t, value, out):
        terms = fold_rows(matmul(doubled(value), pc[t][...], TRANSPOSED))
        for u in range(SLOTS):
            out[u // 2, u % 2] = terms[:, u * 128 : (u + 1) * 128]

    def panel_backward(t, picked):
        x = jnp.concatenate([picked[u] for u in range(SLOTS)], axis=1)
        return fold_all(matmul(split_rows(x), pc[t][...], NATURAL))

    def dense_backward(t, value2, first, last):
        def chunk(index, carry):
            w = jnp.concatenate([cc[t][index * 8 + j] for j in range(8)], axis=1)
            terms = fold_rows(matmul(value2, w, NATURAL))
            for j in range(8):
                sd[t][j // 2, index, j % 2] = terms[:, j * 128 : (j + 1) * 128]
            return carry

        if last - first == 1:
            chunk(first, 0)
        else:
            lax.fori_loop(first, last, chunk, 0)

    def slots_backward(t, k, m, value2, out, place):
        weights, lives = [], []
        for u in range(SLOTS):
            tag = target(m, k, u)
            lives.append(jnp.where((tag >> 6) == t, 1.0, 0.0).astype(F32))
            weights.append(cc[t][tag & (BLOCKS[t] - 1)])
        w = jnp.concatenate(weights, axis=1)
        terms = fold_rows(matmul(value2, w, NATURAL))
        for u in range(SLOTS):
            out[u // 2, place, u % 2] = terms[:, u * 128 : (u + 1) * 128] * lives[u]

    def reduce_send(out, into, blocks):
        st = stage.take()
        for k in (2, 1, 3):
            put(out.at[chip_y ^ k], into.at[k], st, front ^ (2 * k))
        drains.append((st, 0, 3 * blocks))
        return st

    def reduced(out, into, index):
        return (out[(chip_y,) + index] + into[(1,) + index]) + (into[(2,) + index] + into[(3,) + index])

    def spread(src, dst, blocks):
        st = stage.take()
        for mask in (4, 2, 6):
            put(src, dst, st, front ^ mask)
        drains.append((st, 0, 3 * blocks))
        return st

    def hand_over(kind, t, value):
        st = st_out[kind][t]
        out, into, own = (ref["fout"], ref["fin"], fo_ref) if kind == 0 else (ref["sout"], ref["sin"], so_ref)
        out[t] = value[0]
        put(out.at[t], into.at[t], st, front ^ 1)
        own[:, t, :] = value[1]

    st_out = [[stage.take() for t in range(3)] for kind in range(2)]
    for kind in range(2):
        for t in range(3):
            drains.append((st_out[kind][t], 0, 1))

    st_rp = [None] * 3

    def plane_gather(t):
        arrived(st_rz[t], 2 * PLANES[t] - 2)
        st_rp[t] = stage.take()
        for mask in (4, 2, 6):
            put(rb[t].at[:, chip_y], rb[t].at[:, chip_y], st_rp[t], front ^ mask)
        drains.append((st_rp[t], 0, 6 * PLANES[t]))

    @on_one
    def _():
        arrived(st_rc, 3)
        put(rb[2].at[z % 2, chip_y], rb[2].at[z % 2, chip_y], st_rz[2], front ^ 8)
        for m in range(1, 8):
            put(ref["tgv"].at[z], ref["tgv"].at[z], st_tg, front ^ (8 * m))
        for t, count in ((1, 4), (0, 8)):
            for m in range(1, count):
                put(rb[t].at[zz[t], chip_y], rb[t].at[zz[t], chip_y], st_rz[t], front ^ (8 * m))

    for t in range(3):
        drains.append((st_rz[t], 0, 2 * PLANES[t] - 2))
    drains.append((st_tg, 0, 7))
    prepare_third()

    @on_one
    def _():
        plane_gather(2)

    arrived(st_r3, 7)
    forward3 = dense_forward(3)
    panel_forward(3, forward3, ref["up3"])
    st_u3 = stage.take()
    for k in (2, 1, 3):
        put(ref["up3"].at[chip_y ^ k], ref["ur3"].at[d], st_u3, (front ^ (2 * k)) | 1)

    @on_zero
    def _():
        put(ref["up3"].at[chip_y], ref["ur3"].at[d], st_u3, front ^ 1)

    drains.append((st_u3, 8, 6))
    fo_ref[:, 3, :] = forward3
    dense_backward(3, doubled(forward3), 0, 1)
    st_d3 = stage.take()
    for mask in (4, 5, 2, 3, 6, 7, 1):
        put(sd[3].at[chip_y ^ (mask >> 1), 0, core ^ (mask & 1)], ref["dr3"].at[mask], st_d3, front ^ mask)
    drains.append((st_d3, 7, 7))

    def combined_partial():
        quarter = pl.ds(pl.multiple_of(side * 256, 256), 256)
        panel_rows = pc[3][quarter, :]
        swapped = jnp.concatenate([panel_rows[:, 128:], panel_rows[:, :128]], axis=1)
        for j in range(8):
            product = matmul(panel_rows, cc[3][j], NATURAL) + matmul(swapped, cc[3][j], NATURAL)
            ref["gp"][j % 2, j // 2] = product

    def split_combined():
        def body(x, carry):
            block = ref["ga"][core, x]
            high = block.astype(BF16)
            rows = pl.ds(pl.multiple_of(x * 256, 256), 256)
            ref["gc"][rows, 0:128] = high
            ref["gc"][rows, 128:256] = (block - high.astype(F32)).astype(BF16)
            return carry

        lax.fori_loop(0, 4, body, 0)

    def third_total():
        arrived(st_d3, 7)
        total = sd[3][chip_y, 0, core]
        for mask in range(1, 8):
            total = total + ref["dr3"][mask]
        return total

    def third_finish(solved3):
        x = jnp.concatenate([ref["pk3"][0, u] + ref["pk3"][1, u] for u in range(SLOTS)], axis=1)
        so_ref[:, 3, :] = solved3 - fold_all(matmul(split_rows(x), ref["gc"][...], NATURAL))

    st_gx = stage.take()
    drains.append((st_gx, 0, 256))
    st_gr = [stage.take(), stage.take()]
    drains.append((st_gr[0], 96, 0))
    drains.append((st_gr[1], 96, 0))
    st_ga = stage.take()
    drains.append((st_ga, 192, 0))
    st_gd = stage.take()
    drains.append((st_gd, 128, 0))
    st_p3 = stage.take()

    @on_zero
    def _():
        combined_partial()
        arrived(st_gx, 256)

        def add_cross(y, carry):
            for c in range(2):
                ref["gs"][y, c] = ref["gp"][c, y] + ref["gx"][c, y]
            return carry

        lax.fori_loop(0, 4, add_cross, 0)

        def combined_send(half):
            rows = pl.ds(128 * half, 128)
            for k in (2, 1, 3):
                put(ref["gs"].at[chip_y ^ k, :, rows], ref["gr"].at[k, :, rows], st_gr[half], front ^ (2 * k))

        arrived(st_out[0][2], 1)
        fo_ref[:, 2, :] = ref["fin"][2]
        combined_send(0)
        arrived(st_out[0][1], 1)
        fo_ref[:, 1, :] = ref["fin"][1]
        combined_send(1)
        solved3 = third_total()
        arrived(st_out[0][0], 1)
        fo_ref[:, 0, :] = ref["fin"][0]
        arrived(st_gr[0], 96)
        arrived(st_gr[1], 96)
        for c in range(2):
            ref["ga"][c, side] = (ref["gs"][chip_y, c] + ref["gr"][1, c]) + (ref["gr"][2, c] + ref["gr"][3, c])
        for k in (2, 1, 3):
            put(ref["ga"].at[:, side], ref["ga"].at[:, side], st_ga, side ^ k, "rhs")
        arrived(st_ga, 192)
        put(ref["ga"].at[1], ref["ga"].at[1], st_gd, front ^ 1)
        split_combined()
        finish_sends(0)
        for t in (0, 1):
            arrived(st_out[1][t], 1)
            so_ref[:, t, :] = ref["sin"][t]
        arrived(st_p3, 16)
        third_finish(solved3)
        arrived(st_out[1][2], 1)
        so_ref[:, 2, :] = ref["sin"][2]

    @on_one
    def _():
        arrived(st_tg, 7)
        targets_copy = pltpu.make_async_copy(ref["tgv"], tgs, load_sem.at[7])
        targets_copy.start()
        prepare_inverse(2, 0, 16)
        targets_copy.wait()
        arrived(st_u3, 14)
        for i in range(2):
            total = ref["up3"][chip_y, i]
            for k in range(1, 8):
                total = total + ref["ur3"][d ^ k, i]
            ref["us3"][i] = total
            ref["s3p"][0, 2 * chip_y + i] = total
        st_s3 = stage.take()
        for mask in (12, 10, 14, 8):
            put(ref["us3"], ref["s3p"].at[1, pair], st_s3, front ^ mask)
        for mask in (4, 2, 6):
            put(ref["us3"], ref["s3p"].at[0, pair], st_s3, front ^ mask)
        drains.append((st_s3, 0, 14))
        st_z3 = stage.take()
        for m in range(2, 8):
            put(ref["us3"], ref["uz3"].at[m], st_z3, front ^ (8 * m))
        drains.append((st_z3, 0, 12))
        plane_gather(1)
        prepare_panel(2)
        arrived(st_rp[2], 12)
        base2 = dense_forward(2)
        turn_slots(2, 2, ((0, 0), (1, 1)))
        combined_partial()
        put(ref["gp"], ref["gx"], st_gx, front ^ 1)
        arrived(st_s3, 14)

        forward = base2 - turned_forward(2, 2, ((0, 0), (1, 1)), ref["s3p"])
        panel_forward(2, forward, ref["up2"])
        st = reduce_send(ref["up2"], ref["ur2"], 2)
        ref["fk"][2] = forward
        hand_over(0, 2, (forward[:, :128], forward[:, 128:]))
        plane_gather(0)
        arrived(st_z3, 12)
        for m in range(2, 8):
            into = ref["s3q"] if m < 4 else ref["s3r"]
            for i in range(2):
                into[m % 2 if m < 4 else m - 4, 2 * chip_y + i] = ref["uz3"][m, i]
        st_q3 = spread(ref["uz3"].at[pl.ds(2, 2)], ref["s3q"].at[:, pair], 4)
        prepare_inverse(1, 0, 32)
        arrived(st, 6)
        for i in range(2):
            ref["us2"][i] = reduced(ref["up2"], ref["ur2"], (i,))
        st_z2, st_z2b = stage.take(), stage.take()
        for m in (2, 3, 1):
            put(ref["us2"], ref["uz2"].at[m], st_z2, front ^ (8 * m))
        for m in range(4, 8):
            put(ref["us2"], ref["uz2b"].at[m - 4], st_z2b, front ^ (8 * m))
        drains.append((st_z2, 0, 6))
        drains.append((st_z2b, 0, 8))
        prepare_panel(1)
        arrived(st_rp[1], 24)
        base1 = dense_forward(1)
        turn_slots(1, 1, ((0, 0), (1, 2)))
        prepare_inverse(0, 0, 20)
        arrived(st_z2, 6)
        for i in range(2):
            own = ref["us2"][i] + ref["uz2"][1, i]
            other = ref["uz2"][2, i] + ref["uz2"][3, i]
            for h, total in ((0, own), (1, other)):
                ref["st2"][h, i] = total
                ref["s2p"][h, 2 * chip_y + i] = total
        st_s2 = spread(ref["st2"], ref["s2p"].at[:, pair], 4)
        arrived(st_q3, 12)
        for m in range(4):
            src = ref["s3p"].at[m] if m < 2 else ref["s3q"].at[m - 2]
            base1 = base1 - slots_forward(1, 2, m, lambda u, src=src: src[u])
        prepare_inverse(0, 20, 44)
        arrived(st_s2, 12)

        forward = base1 - turned_forward(1, 1, ((0, 0), (1, 2)), ref["s2p"])
        panel_forward(1, forward, ref["up1"])
        st = reduce_send(ref["up1"], ref["ur1"], 2)
        ref["fk"][1] = forward
        hand_over(0, 1, (forward[:, :128], forward[:, 128:]))
        arrived(st_z2b, 8)
        for i in range(2):
            for h in range(2):
                total = ref["uz2b"][2 * h, i] + ref["uz2b"][2 * h + 1, i]
                ref["st2b"][h, i] = total
                ref["s2q"][h, 2 * chip_y + i] = total
        st_q2 = spread(ref["st2b"], ref["s2q"].at[:, pair], 4)
        st_r3x = spread(ref["uz3"].at[pl.ds(4, 4)], ref["s3r"].at[:, pair], 8)
        prepare_inverse(0, 44, 64)
        turn_slots(0, 0, ((0, 0), (1, 4)))
        base0 = jnp.zeros((8, 256), F32)
        for h in range(2):
            base0 = base0 - slots_forward(0, 1, 2 * h, lambda u, h=h: ref["s2p"][h, u])
            base0 = base0 - slots_forward(0, 2, h, lambda u, h=h: ref["s3p"][h, u])
        arrived(st, 6)
        for i in range(2):
            ref["us1"][i] = reduced(ref["up1"], ref["ur1"], (i,))
        st_z1 = stage.take()
        for m in (4, 5, 3, 6, 2, 7, 1):
            put(ref["us1"], ref["uz1"].at[m], st_z1, front ^ (8 * m))
        drains.append((st_z1, 0, 14))
        for m in range(2):
            base0 = base0 - slots_forward(0, 2, m + 2, lambda u, m=m: ref["s3q"][m, u])
        arrived(st_rp[0], 48)
        base0 = base0 + dense_forward(0)
        arrived(st_z1, 14)
        for i in range(2):
            own = ref["us1"][i]
            for m in range(1, 4):
                own = own + ref["uz1"][m, i]
            other = ref["uz1"][4, i]
            for m in range(5, 8):
                other = other + ref["uz1"][m, i]
            for h, total in ((0, own), (1, other)):
                ref["st1"][h, i] = total
                ref["s1p"][h, 2 * chip_y + i] = total
        st_s1 = spread(ref["st1"], ref["s1p"].at[:, pair], 4)
        arrived(st_r3x, 24)
        base0 = lax.fori_loop(
            0, 4, lambda m, total: total - slots_forward(0, 2, m + 4, lambda u: ref["s3r"][m, u]), base0
        )
        arrived(st_q2, 12)
        for h in range(2):
            base0 = base0 - slots_forward(0, 1, 4 + 2 * h, lambda u, h=h: ref["s2q"][h, u])
        arrived(st_s1, 12)

        forward = base0 - turned_forward(0, 0, ((0, 0), (1, 4)), ref["s1p"])

        value2 = doubled(forward)
        for h in range(2):
            slots_backward(0, 0, 4 * h, value2, ref["a1"], h)
        st = reduce_send(ref["a1"], ref["ar1"], 4)
        hand_over(0, 0, (forward[:, :128], forward[:, 128:]))
        dense_backward(0, value2, 0, 7)
        arrived(st, 12)
        for h in range(2):
            for i in range(2):
                ref["as1"][h, i] = reduced(ref["a1"], ref["ar1"], (h, i))
        st_z = stage.take()
        for m in (4, 5, 3, 6, 2, 7, 1):
            put(ref["as1"].at[m >> 2], ref["az1"].at[m], st_z, front ^ (8 * m))
        drains.append((st_z, 0, 14))
        dense_backward(0, value2, 7, 8)

        def pick(t, planes, out, place, m, k):
            for u in range(SLOTS):
                tag = target(m, k, u)
                live = jnp.where((tag >> 6) == t, 1.0, 0.0).astype(F32)
                block = sd[t][(tag >> 1) & 3, (tag >> 3) & (planes - 1), tag & 1]
                out[u // 2, place, u % 2] = block * live

        for j in range(12):
            pick(0, 8, ref["n0"], j, 2 * j if j < 4 else j - 4, 1 if j < 4 else 2)
        st_n0 = reduce_send(ref["n0"], ref["nr0"], 24)
        arrived(st_z, 14)
        for i in range(2):
            total = ref["as1"][0, i]
            for m in range(1, 8):
                total = total + ref["az1"][m, i]
            ref["pt1"][i] = total
            ref["pk1"][2 * chip_y + i] = total
        st_p = spread(ref["pt1"], ref["pk1"].at[pair], 2)
        arrived(st_p, 6)

        value2 = doubled(ref["fk"][1] - panel_backward(1, ref["pk1"]))
        for h in range(2):
            slots_backward(1, 1, 2 * h, value2, ref["a2"], h)
        st = reduce_send(ref["a2"], ref["ar2"], 4)
        arrived(st_n0, 72)

        def background_sums(m, carry):
            for i in range(2):
                ref["ns0"][m, 0, i] = reduced(ref["n0"], ref["nr0"], (m // 2, i))
                ref["ns0"][m, 1, i] = reduced(ref["n0"], ref["nr0"], (4 + m, i))
            return carry

        lax.fori_loop(0, 8, background_sums, 0)
        st_nz0 = stage.take()
        for m in (4, 5, 3, 6, 2, 7, 1):
            put(ref["ns0"].at[m], ref["nz0"].at[m], st_nz0, front ^ (8 * m))
        drains.append((st_nz0, 0, 28))
        st_d0 = reduce_send(sd[0], ref["dr0"], 16)
        dense_backward(1, value2, 0, 4)
        for m in range(4):
            pick(1, 4, ref["n1"], m, m, 2)
        st_n1 = reduce_send(ref["n1"], ref["nr1"], 8)
        arrived(st, 12)
        for h in range(2):
            for i in range(2):
                ref["as2"][h, i] = reduced(ref["a2"], ref["ar2"], (h, i))
        st_z = stage.take()
        for m in (2, 3, 1):
            put(ref["as2"].at[m >> 1], ref["az2"].at[m], st_z, front ^ (8 * m))
        drains.append((st_z, 0, 6))
        st_d1 = reduce_send(sd[1], ref["dr1"], 8)

        def plane_totals(st_d, t, into, final, st_f):
            arrived(st_d, 6 * PLANES[t])
            for w in range(PLANES[t]):
                for c in range(2):
                    final[w, c] = reduced(sd[t], into, (w, c))

        arrived(st_nz0, 28)
        for q in range(2):
            for i in range(2):
                total = ref["ns0"][0, q, i]
                for m in range(1, 8):
                    total = total + ref["nz0"][m, q, i]
                ref["t0p"][q, i] = total
        arrived(st_z, 6)
        for i in range(2):
            total = ref["as2"][0, i] + ref["t0p"][0, i]
            for m in range(1, 4):
                total = total + ref["az2"][m, i]
            ref["pt2"][i] = total
            ref["pk2"][2 * chip_y + i] = total
        st_p = spread(ref["pt2"], ref["pk2"].at[pair], 2)
        arrived(st_n1, 24)
        for m in range(4):
            for i in range(2):
                ref["ns1"][m, i] = reduced(ref["n1"], ref["nr1"], (m, i))
        st_nz1 = stage.take()
        for m in (2, 3, 1):
            put(ref["ns1"].at[m], ref["nz1"].at[m], st_nz1, front ^ (8 * m))
        drains.append((st_nz1, 0, 6))
        plane_totals(st_d0, 0, ref["dr0"], ref["ds0"], None)
        st_dz0 = stage.take()
        for m in (4, 5, 3, 6, 2, 7, 1):
            put(ref["ds0"].at[z ^ m], ref["dz0"].at[m], st_dz0, front ^ (8 * m))
        drains.append((st_dz0, 0, 14))
        plane_totals(st_d1, 1, ref["dr1"], ref["ds1"], None)
        st_dz1 = stage.take()
        for m in (2, 3, 1):
            put(ref["ds1"].at[(z ^ m) % 4], ref["dz1"].at[m], st_dz1, front ^ (8 * m))
        drains.append((st_dz1, 0, 6))
        arrived(st_p, 6)

        value2 = doubled(ref["fk"][2] - panel_backward(2, ref["pk2"]))
        for h in range(2):
            slots_backward(2, 2, h, value2, ref["a3"], h)
        st = reduce_send(ref["a3"], ref["ar3"], 4)
        dense_backward(2, value2, 0, 2)
        st_d2 = stage.take()
        for mask in (12, 14, 10, 8, 4, 6, 2):
            put(
                sd[2].at[chip_y ^ ((mask >> 1) & 3), (z ^ (mask >> 3)) % 2],
                ref["dr2"].at[mask >> 1], st_d2, front ^ mask,
            )
        drains.append((st_d2, 0, 14))
        arrived(st_nz1, 6)
        for i in range(2):
            total = ref["ns1"][0, i] + ref["t0p"][1, i]
            for m in range(1, 4):
                total = total + ref["nz1"][m, i]
            ref["t1p"][i] = total
        arrived(st, 12)
        for i in range(2):
            ref["as3"][1, i] = reduced(ref["a3"], ref["ar3"], (1, i))
            total = ref["t1p"][i] + reduced(ref["a3"], ref["ar3"], (0, i))
            ref["as3"][0, i] = total
            ref["pk3"][0, 2 * chip_y + i] = total
        for mask in (12, 13, 10, 11, 14, 15, 8, 9):
            put(ref["as3"].at[1], ref["pk3"].at[1, pair], st_p3, front ^ mask)
        for mask in (4, 5, 2, 3, 6, 7, 1):
            put(ref["as3"].at[0], ref["pk3"].at[0, pair], st_p3, front ^ mask)
        arrived(st_dz0, 14)
        totals = []
        for c in range(2):
            total = ref["ds0"][z, c]
            for m in range(1, 8):
                total = total + ref["dz0"][m, c]
            totals.append(total)
        hand_over(1, 0, totals)
        arrived(st_dz1, 6)
        totals = []
        for c in range(2):
            total = ref["ds1"][z % 4, c]
            for m in range(1, 4):
                total = total + ref["dz1"][m, c]
            totals.append(total)
        hand_over(1, 1, totals)
        arrived(st_d2, 14)
        totals = []
        for c in range(2):
            total = sd[2][chip_y, z % 2, c]
            for m in range(1, 8):
                total = total + ref["dr2"][m, c]
            totals.append(total)
        hand_over(1, 2, totals)
        solved3 = third_total()
        arrived(st_gd, 128)
        split_combined()
        finish_sends(1)
        arrived(st_p3, 14)
        third_finish(solved3)
        drain(send_sem.at[st_p3], 30)

    assert stage.count <= STAGE_COUNT


def shards(right_side, inverse_top, inverse_second, inverse_third, inverse_fourth, panels, targets):
    anywhere = pl.BlockSpec(memory_space=pl.ANY)
    results = pl.pallas_call(
        kernel,
        out_shape=pltpu.VMEM((2,) + right_side.shape, F32),
        in_specs=[anywhere] * 7,
        out_specs=pl.BlockSpec(memory_space=pltpu.VMEM),
        scratch_shapes=[pltpu.VMEM(shape, dtype) for shape, dtype in SCRATCH.values()]
        + [
            pltpu.SMEM((8, 8, 128), I32),
            pltpu.SMEM((3, 1, 8), I32),
            pltpu.SemaphoreType.DMA((STAGE_COUNT,)),
            pltpu.SemaphoreType.DMA((STAGE_COUNT,)),
            pltpu.SemaphoreType.DMA((12,)),
        ],
        compiler_params=pltpu.CompilerParams(
            collective_id=0, has_side_effects=True, vmem_limit_bytes=56 * 2**20
        ),
        name="tiers",
    )(right_side, inverse_top, inverse_second, inverse_third, inverse_fourth, panels, targets)
    return results[0], results[1]


def solution(mesh):
    placed = (
        P("rhs", None, "front"),
        P("front", None),
        P("front", None),
        P("front", None),
        P("front", None),
        P(None, None, "front"),
        P(None, "front", None),
    )
    return jax.shard_map(
        shards,
        mesh=mesh,
        in_specs=placed,
        out_specs=(P("rhs", None, "front"), P("rhs", None, "front")),
        check_vma=False,
    )
```

```python
import functools

import jax
import jax.numpy as jnp
from jax import lax
from jax.experimental import pallas as pl
from jax.experimental.pallas import tpu as pltpu
from jax.sharding import PartitionSpec as P

F32 = jnp.float32
BF16 = jnp.bfloat16
I32 = jnp.int32
MESH = pl.DeviceIdType.MESH
TIERS = 4
SLOTS = 8
BLOCKS = (64, 32, 16, 8)
PLANES = (8, 4, 2, 1)
TRANSPOSED = (((1,), (1,)), ((), ()))
NATURAL = (((1,), (0,)), ((), ()))


def split_rows(value):
    high = value.astype(BF16).astype(F32)
    return jnp.concatenate([high, value - high], axis=0).astype(BF16)


def fold_rows(value):
    return value[:8] + value[8:]


def fold_all(value):
    rows = fold_rows(value)
    sums = [
        rows[:, i : i + 128] + rows[:, i + 128 : i + 256] for i in range(0, rows.shape[1], 256)
    ]
    return sums[0] if len(sums) == 1 else jnp.concatenate(sums, axis=1)


def doubled(value):
    halves = split_rows(value)
    parts = [halves[:, i : i + 128] for i in range(0, halves.shape[1], 128)]
    return jnp.concatenate([part for part in parts for _ in range(2)], axis=1)


def matmul(left, right, dims):
    return lax.dot_general(left, right, dims, preferred_element_type=F32)


class Stage:
    def __init__(self):
        self.count = 0

    def take(self):
        self.count += 1
        return self.count - 1


STAGE_COUNT = 56

SCRATCH = dict(
    v0=((128, 8192), F32), v1=((128, 4096), F32), v2=((128, 2048), F32), v3=((128, 1024), F32),
    vp=((3, 1024, 128), F32),
    w0=((128, 8192), F32), w1=((128, 4096), F32), w2=((128, 2048), F32), wp=((2, 1024, 128), F32),
    c0=((64, 512, 128), BF16), c1=((32, 512, 128), BF16), c2=((16, 512, 128), BF16), c3=((8, 256, 128), BF16),
    pc3=((1024, 256), BF16), pc2=((1024, 512), BF16), pc1=((1024, 512), BF16),
    rb0=((8, 4, 2, 8, 128), F32), rb1=((4, 4, 2, 8, 128), F32), rb2=((2, 4, 2, 8, 128), F32), rb3=((1, 4, 2, 8, 128), F32),
    tgv=((8, 8, 128), I32),
    up3=((4, 2, 8, 128), F32), up2=((4, 2, 8, 128), F32), up1=((4, 2, 8, 128), F32),
    ur3=((8, 2, 8, 128), F32), ur2=((4, 2, 8, 128), F32), ur1=((4, 2, 8, 128), F32),
    us3=((2, 8, 128), F32), us2=((2, 8, 128), F32), us1=((2, 8, 128), F32),
    uz3=((8, 2, 8, 128), F32), uz2=((4, 2, 8, 128), F32), uz2b=((4, 2, 8, 128), F32), uz1=((8, 2, 8, 128), F32),
    s3p=((2, 8, 8, 128), F32), s3q=((2, 8, 8, 128), F32), s3r=((4, 8, 8, 128), F32),
    s2p=((2, 8, 8, 128), F32), s2q=((2, 8, 8, 128), F32), s1p=((2, 8, 8, 128), F32),
    st2=((2, 2, 8, 128), F32), st2b=((2, 2, 8, 128), F32), st1=((2, 2, 8, 128), F32),
    a1=((4, 2, 2, 8, 128), F32), a2=((4, 2, 2, 8, 128), F32), a3=((4, 2, 2, 8, 128), F32),
    ar1=((4, 2, 2, 8, 128), F32), ar2=((4, 2, 2, 8, 128), F32), ar3=((4, 2, 2, 8, 128), F32),
    as1=((2, 2, 8, 128), F32), as2=((2, 2, 8, 128), F32), as3=((2, 2, 8, 128), F32),
    az1=((8, 2, 8, 128), F32), az2=((4, 2, 8, 128), F32),
    pt1=((2, 8, 128), F32), pt2=((2, 8, 128), F32),
    pk1=((8, 8, 128), F32), pk2=((8, 8, 128), F32), pk3=((2, 8, 8, 128), F32),
    n0=((4, 12, 2, 8, 128), F32), nr0=((4, 12, 2, 8, 128), F32), ns0=((8, 2, 2, 8, 128), F32), nz0=((8, 2, 2, 8, 128), F32),
    n1=((4, 4, 2, 8, 128), F32), nr1=((4, 4, 2, 8, 128), F32), ns1=((4, 2, 8, 128), F32), nz1=((4, 2, 8, 128), F32),
    t0p=((2, 2, 8, 128), F32), t1p=((2, 8, 128), F32),
    sd0=((4, 8, 2, 8, 128), F32), sd1=((4, 4, 2, 8, 128), F32), sd2=((4, 2, 2, 8, 128), F32), sd3=((4, 1, 2, 8, 128), F32),
    dr0=((4, 8, 2, 8, 128), F32), dr1=((4, 4, 2, 8, 128), F32), dr2=((8, 2, 8, 128), F32), dr3=((8, 8, 128), F32),
    ds0=((8, 2, 8, 128), F32), ds1=((4, 2, 8, 128), F32),
    dz0=((8, 2, 8, 128), F32), dz1=((4, 2, 8, 128), F32),
    fk=((3, 8, 256), F32), fout=((3, 8, 128), F32), fin=((3, 8, 128), F32), sout=((3, 8, 128), F32), sin=((3, 8, 128), F32),
    gp=((2, 4, 256, 128), F32), gx=((2, 4, 256, 128), F32), gs=((4, 2, 256, 128), F32), gr=((4, 2, 256, 128), F32),
    ga=((2, 4, 256, 128), F32), gc=((1024, 256), BF16),
    rs=((8, 4, 128), F32),
    wt0=((2048, 512), BF16), wt1=((2048, 512), BF16), wt2=((2048, 512), BF16),
    dummy=((256, 8, 128), F32),
)


def kernel(rs_hbm, i0_ref, i1_ref, i2_ref, i3_ref, pn_ref, tg_hbm, out_ref, *scratch):
    names = list(SCRATCH)
    ref = dict(zip(names, scratch[: len(names)]))
    tgs, tg_ref, send_sem, recv_sem, load_sem = scratch[len(names) :]
    rs_ref, fo_ref, so_ref = ref["rs"], out_ref.at[0], out_ref.at[1]
    front = lax.axis_index("front")
    side = lax.axis_index("rhs")
    core = front % 2
    chip_y = (front // 2) % 4
    d = front % 8
    z = front // 8
    is_one = core == 1
    stage = Stage()
    drains = []
    cc = [ref["c0"], ref["c1"], ref["c2"], ref["c3"]]
    rb = [ref["rb0"], ref["rb1"], ref["rb2"], ref["rb3"]]
    sd = [ref["sd0"], ref["sd1"], ref["sd2"], ref["sd3"]]
    pc = [None, ref["pc1"], ref["pc2"], ref["pc3"]]
    zz = [z, z % 4, z % 2, 0]
    pair = pl.ds(2 * chip_y, 2)

    def on_one(body):
        pl.when(is_one)(body)

    def on_zero(body):
        pl.when(jnp.logical_not(is_one))(body)

    def put(src, dst, st, to, axis="front"):
        pltpu.make_async_remote_copy(
            src_ref=src, dst_ref=dst, send_sem=send_sem.at[st], recv_sem=recv_sem.at[st],
            device_id={axis: to}, device_id_type=MESH,
        ).start()

    def drain(sem, blocks):
        while blocks:
            some = min(blocks, 256)
            piece = ref["dummy"].at[pl.ds(0, some)]
            pltpu.make_async_copy(piece, piece, sem).wait()
            blocks -= some

    def arrived(st, blocks):
        drain(recv_sem.at[st], blocks)

    def finish_sends(core_number):
        for st_x, zero, one in drains:
            drain(send_sem.at[st_x], one if core_number else zero)

    barrier = pltpu.get_barrier_semaphore()
    masks = list(range(1, 16)) + [8 * m for m in range(2, 8)]
    for mask in masks:
        pl.semaphore_signal(barrier, inc=1, device_id={"front": front ^ mask}, device_id_type=MESH)
    for k in range(1, 4):
        pl.semaphore_signal(barrier, inc=1, device_id={"rhs": side ^ k}, device_id_type=MESH)

    inverse_refs = (i0_ref, i1_ref, i2_ref, i3_ref)

    def load(name):
        t = int(name[1])
        if name[0] == "p":
            return pltpu.make_async_copy(pn_ref.at[t - 1], ref["vp"].at[t - 1], load_sem.at[t + 3])
        return pltpu.make_async_copy(inverse_refs[t], ref[name], load_sem.at[t])

    rs_copy = pltpu.make_async_copy(rs_hbm, rs_ref, load_sem.at[8])
    rs_copy.start()
    tg_copy = pltpu.make_async_copy(tg_hbm, tg_ref, load_sem.at[9])
    tg_copy.start()
    load("v3").start()
    load("p3").start()

    @on_one
    def _():
        load("v2").start()
        load("p2").start()
        load("v1").start()
        load("p1").start()
        load("v0").start()

    rs_copy.wait()
    tg_copy.wait()
    for t in range(TIERS):
        rb[t][zz[t], chip_y, core] = rs_ref[:, t, :]
    lanes = lax.broadcasted_iota(I32, (8, 128), 1)
    own_targets = jnp.full((8, 128), -1, I32)
    for k in range(3):
        for u in range(SLOTS):
            own_targets = jnp.where(lanes == k * 8 + u, tg_ref[k, 0, u], own_targets)
    ref["tgv"][z] = own_targets

    pl.semaphore_wait(barrier, len(masks) + 3)

    st_r3 = stage.take()
    for mask in (4, 5, 2, 3, 6, 7, 1):
        put(rb[3].at[0, chip_y, core], rb[3].at[0, chip_y, core], st_r3, front ^ mask)
    drains.append((st_r3, 7, 7))
    st_tg = stage.take()
    st_rc = stage.take()
    st_rz = [stage.take() for t in range(3)]
    st_w = {name: stage.take() for name in ("w2", "p2", "w1", "p1", "w0")}

    @on_zero
    def _():
        for t in (2, 1, 0):
            put(rb[t].at[zz[t], chip_y, 0], rb[t].at[zz[t], chip_y, 0], st_rc, front ^ 1)
        put(i2_ref, ref["w2"], st_w["w2"], front ^ 1)
        put(pn_ref.at[1], ref["wp"].at[1], st_w["p2"], front ^ 1)
        put(i1_ref, ref["w1"], st_w["w1"], front ^ 1)
        put(pn_ref.at[0], ref["wp"].at[0], st_w["p1"], front ^ 1)
        put(i0_ref, ref["w0"], st_w["w0"], front ^ 1)

    drains.append((st_rc, 3, 0))
    drains.append((st_w["w2"], 256, 0))
    drains.append((st_w["p2"], 128, 0))
    drains.append((st_w["w1"], 512, 0))
    drains.append((st_w["p1"], 128, 0))
    drains.append((st_w["w0"], 1024, 0))

    def prepare_third():
        load("v3").wait()

        def body(e, carry):
            block = ref["v3"][:, pl.ds(pl.multiple_of(e * 128, 128), 128)]
            high = block.astype(BF16)
            cc[3][e, 0:128, :] = high
            cc[3][e, 128:256, :] = (block - high.astype(F32)).astype(BF16)
            return carry

        lax.fori_loop(0, 8, body, 0)
        load("p3").wait()

        def body_panel(u, carry):
            rows = pl.ds(pl.multiple_of(u * 128, 128), 128)
            block = ref["vp"][2, rows, :]
            high = block.astype(BF16)
            pc[3][rows, 0:128] = high
            pc[3][rows, 128:256] = (block - high.astype(F32)).astype(BF16)
            return carry

        lax.fori_loop(0, 8, body_panel, 0)

    def prepare_inverse(t, first, last):
        if first == 0:
            load("v" + str(t)).wait()
            arrived(st_w["w" + str(t)], 16 * BLOCKS[t])

        def body(e, carry):
            columns = pl.ds(pl.multiple_of(e * 128, 128), 128)
            for i, source in ((0, ref["w" + str(t)]), (1, ref["v" + str(t)])):
                block = source[:, columns]
                high = block.astype(BF16)
                cc[t][e, 256 * i : 256 * i + 128, :] = high
                cc[t][e, 256 * i + 128 : 256 * i + 256, :] = (block - high.astype(F32)).astype(BF16)
            return carry

        lax.fori_loop(first, last, body, 0)

    def prepare_panel(t):
        load("p" + str(t)).wait()
        arrived(st_w["p" + str(t)], 128)

        def body(u, carry):
            rows = pl.ds(pl.multiple_of(u * 128, 128), 128)
            for i, source in ((0, ref["wp"]), (1, ref["vp"])):
                block = source[t - 1, rows, :]
                high = block.astype(BF16)
                pc[t][rows, 256 * i : 256 * i + 128] = high
                pc[t][rows, 256 * i + 128 : 256 * i + 256] = (block - high.astype(F32)).astype(BF16)
            return carry

        lax.fori_loop(0, SLOTS, body, 0)

    def target(m, k, u):
        return tgs[z ^ m, 0, k * 8 + u]

    def dense_forward(t):
        def chunk(index):
            x = jnp.concatenate([rb[t][index, j // 2, j % 2] for j in range(8)], axis=1)
            w = jnp.concatenate([cc[t][index * 8 + j] for j in range(8)], axis=1)
            return fold_all(matmul(split_rows(x), w, TRANSPOSED))

        if PLANES[t] == 1:
            return chunk(0)
        return lax.fori_loop(0, PLANES[t], lambda i, total: total + chunk(i), jnp.zeros((8, 256), F32))

    def slots_forward(t, k, m, block_of):
        parts, weights = [], []
        for u in range(SLOTS):
            tag = target(m, k, u)
            live = jnp.where((tag >> 6) == t, 1.0, 0.0).astype(F32)
            parts.append(block_of(u) * live)
            weights.append(cc[t][tag & (BLOCKS[t] - 1)])
        x = jnp.concatenate(parts, axis=1)
        w = jnp.concatenate(weights, axis=1)
        return fold_all(matmul(split_rows(x), w, TRANSPOSED))

    def turn_slots(t, k, fronts):
        for h, m in fronts:
            for u in range(SLOTS):
                block = cc[t][target(m, k, u) & (BLOCKS[t] - 1)]
                first = (h * SLOTS + u) * 128
                ref["wt" + str(t)][first : first + 128, :] = block.T

    def turned_forward(t, k, fronts, sums):
        parts = []
        for h, m in fronts:
            for u in range(SLOTS):
                live = jnp.where((target(m, k, u) >> 6) == t, 1.0, 0.0).astype(F32)
                parts.append(sums[h, u] * live)
        x = jnp.concatenate(parts, axis=1)
        return fold_all(matmul(split_rows(x), ref["wt" + str(t)][...], NATURAL))

    def panel_forward(t, value, out):
        terms = fold_rows(matmul(doubled(value), pc[t][...], TRANSPOSED))
        for u in range(SLOTS):
            out[u // 2, u % 2] = terms[:, u * 128 : (u + 1) * 128]

    def panel_backward(t, picked):
        x = jnp.concatenate([picked[u] for u in range(SLOTS)], axis=1)
        return fold_all(matmul(split_rows(x), pc[t][...], NATURAL))

    def dense_backward(t, value2, first, last):
        def chunk(index, carry):
            w = jnp.concatenate([cc[t][index * 8 + j] for j in range(8)], axis=1)
            terms = fold_rows(matmul(value2, w, NATURAL))
            for j in range(8):
                sd[t][j // 2, index, j % 2] = terms[:, j * 128 : (j + 1) * 128]
            return carry

        if last - first == 1:
            chunk(first, 0)
        else:
            lax.fori_loop(first, last, chunk, 0)

    def slots_backward(t, k, m, value2, out, place):
        weights, lives = [], []
        for u in range(SLOTS):
            tag = target(m, k, u)
            lives.append(jnp.where((tag >> 6) == t, 1.0, 0.0).astype(F32))
            weights.append(cc[t][tag & (BLOCKS[t] - 1)])
        w = jnp.concatenate(weights, axis=1)
        terms = fold_rows(matmul(value2, w, NATURAL))
        for u in range(SLOTS):
            out[u // 2, place, u % 2] = terms[:, u * 128 : (u + 1) * 128] * lives[u]

    def reduce_send(out, into, blocks):
        st = stage.take()
        for k in (2, 1, 3):
            put(out.at[chip_y ^ k], into.at[k], st, front ^ (2 * k))
        drains.append((st, 0, 3 * blocks))
        return st

    def reduced(out, into, index):
        return (out[(chip_y,) + index] + into[(1,) + index]) + (into[(2,) + index] + into[(3,) + index])

    def spread(src, dst, blocks):
        st = stage.take()
        for mask in (4, 2, 6):
            put(src, dst, st, front ^ mask)
        drains.append((st, 0, 3 * blocks))
        return st

    def hand_over(kind, t, value):
        st = st_out[kind][t]
        out, into, own = (ref["fout"], ref["fin"], fo_ref) if kind == 0 else (ref["sout"], ref["sin"], so_ref)
        out[t] = value[0]
        put(out.at[t], into.at[t], st, front ^ 1)
        own[:, t, :] = value[1]

    st_out = [[stage.take() for t in range(3)] for kind in range(2)]
    for kind in range(2):
        for t in range(3):
            drains.append((st_out[kind][t], 0, 1))

    st_rp = [None] * 3

    def plane_gather(t):
        arrived(st_rz[t], 2 * PLANES[t] - 2)
        st_rp[t] = stage.take()
        for mask in (4, 2, 6):
            put(rb[t].at[:, chip_y], rb[t].at[:, chip_y], st_rp[t], front ^ mask)
        drains.append((st_rp[t], 0, 6 * PLANES[t]))

    @on_one
    def _():
        arrived(st_rc, 3)
        put(rb[2].at[z % 2, chip_y], rb[2].at[z % 2, chip_y], st_rz[2], front ^ 8)
        for m in range(1, 8):
            put(ref["tgv"].at[z], ref["tgv"].at[z], st_tg, front ^ (8 * m))
        for t, count in ((1, 4), (0, 8)):
            for m in range(1, count):
                put(rb[t].at[zz[t], chip_y], rb[t].at[zz[t], chip_y], st_rz[t], front ^ (8 * m))

    for t in range(3):
        drains.append((st_rz[t], 0, 2 * PLANES[t] - 2))
    drains.append((st_tg, 0, 7))
    prepare_third()

    @on_one
    def _():
        plane_gather(2)

    arrived(st_r3, 7)
    forward3 = dense_forward(3)
    panel_forward(3, forward3, ref["up3"])
    st_u3 = stage.take()
    for k in (2, 1, 3):
        put(ref["up3"].at[chip_y ^ k], ref["ur3"].at[d], st_u3, (front ^ (2 * k)) | 1)

    @on_zero
    def _():
        put(ref["up3"].at[chip_y], ref["ur3"].at[d], st_u3, front ^ 1)

    drains.append((st_u3, 8, 6))
    fo_ref[:, 3, :] = forward3
    dense_backward(3, doubled(forward3), 0, 1)
    st_d3 = stage.take()
    for mask in (4, 5, 2, 3, 6, 7, 1):
        put(sd[3].at[chip_y ^ (mask >> 1), 0, core ^ (mask & 1)], ref["dr3"].at[mask], st_d3, front ^ mask)
    drains.append((st_d3, 7, 7))

    def combined_partial():
        quarter = pl.ds(pl.multiple_of(side * 256, 256), 256)
        panel_rows = pc[3][quarter, :]
        swapped = jnp.concatenate([panel_rows[:, 128:], panel_rows[:, :128]], axis=1)
        for j in range(8):
            product = matmul(panel_rows, cc[3][j], NATURAL) + matmul(swapped, cc[3][j], NATURAL)
            ref["gp"][j % 2, j // 2] = product

    def split_combined():
        def body(x, carry):
            block = ref["ga"][core, x]
            high = block.astype(BF16)
            rows = pl.ds(pl.multiple_of(x * 256, 256), 256)
            ref["gc"][rows, 0:128] = high
            ref["gc"][rows, 128:256] = (block - high.astype(F32)).astype(BF16)
            return carry

        lax.fori_loop(0, 4, body, 0)

    def third_total():
        arrived(st_d3, 7)
        total = sd[3][chip_y, 0, core]
        for mask in range(1, 8):
            total = total + ref["dr3"][mask]
        return total

    def third_finish(solved3):
        x = jnp.concatenate([ref["pk3"][0, u] + ref["pk3"][1, u] for u in range(SLOTS)], axis=1)
        so_ref[:, 3, :] = solved3 - fold_all(matmul(split_rows(x), ref["gc"][...], NATURAL))

    st_gx = stage.take()
    drains.append((st_gx, 0, 256))
    st_gr = [stage.take(), stage.take()]
    drains.append((st_gr[0], 96, 0))
    drains.append((st_gr[1], 96, 0))
    st_ga = stage.take()
    drains.append((st_ga, 192, 0))
    st_gd = stage.take()
    drains.append((st_gd, 128, 0))
    st_p3 = stage.take()

    @on_zero
    def _():
        combined_partial()
        arrived(st_gx, 256)

        def add_cross(y, carry):
            for c in range(2):
                ref["gs"][y, c] = ref["gp"][c, y] + ref["gx"][c, y]
            return carry

        lax.fori_loop(0, 4, add_cross, 0)

        def combined_send(half):
            rows = pl.ds(128 * half, 128)
            for k in (2, 1, 3):
                put(ref["gs"].at[chip_y ^ k, :, rows], ref["gr"].at[k, :, rows], st_gr[half], front ^ (2 * k))

        arrived(st_out[0][2], 1)
        fo_ref[:, 2, :] = ref["fin"][2]
        combined_send(0)
        arrived(st_out[0][1], 1)
        fo_ref[:, 1, :] = ref["fin"][1]
        combined_send(1)
        solved3 = third_total()
        arrived(st_out[0][0], 1)
        fo_ref[:, 0, :] = ref["fin"][0]
        arrived(st_gr[0], 96)
        arrived(st_gr[1], 96)
        for c in range(2):
            ref["ga"][c, side] = (ref["gs"][chip_y, c] + ref["gr"][1, c]) + (ref["gr"][2, c] + ref["gr"][3, c])
        for k in (2, 1, 3):
            put(ref["ga"].at[:, side], ref["ga"].at[:, side], st_ga, side ^ k, "rhs")
        arrived(st_ga, 192)
        put(ref["ga"].at[1], ref["ga"].at[1], st_gd, front ^ 1)
        split_combined()
        finish_sends(0)
        for t in (0, 1):
            arrived(st_out[1][t], 1)
            so_ref[:, t, :] = ref["sin"][t]
        arrived(st_p3, 16)
        third_finish(solved3)
        arrived(st_out[1][2], 1)
        so_ref[:, 2, :] = ref["sin"][2]

    @on_one
    def _():
        arrived(st_tg, 7)
        targets_copy = pltpu.make_async_copy(ref["tgv"], tgs, load_sem.at[7])
        targets_copy.start()
        prepare_inverse(2, 0, 16)
        targets_copy.wait()
        arrived(st_u3, 14)
        for i in range(2):
            total = ref["up3"][chip_y, i]
            for k in range(1, 8):
                total = total + ref["ur3"][d ^ k, i]
            ref["us3"][i] = total
            ref["s3p"][0, 2 * chip_y + i] = total
        st_s3 = stage.take()
        for mask in (12, 10, 14, 8):
            put(ref["us3"], ref["s3p"].at[1, pair], st_s3, front ^ mask)
        for mask in (4, 2, 6):
            put(ref["us3"], ref["s3p"].at[0, pair], st_s3, front ^ mask)
        drains.append((st_s3, 0, 14))
        st_z3 = stage.take()
        for m in range(2, 8):
            put(ref["us3"], ref["uz3"].at[m], st_z3, front ^ (8 * m))
        drains.append((st_z3, 0, 12))
        plane_gather(1)
        combined_partial()
        put(ref["gp"], ref["gx"], st_gx, front ^ 1)
        prepare_panel(2)
        arrived(st_rp[2], 12)
        base2 = dense_forward(2)
        turn_slots(2, 2, ((0, 0), (1, 1)))
        arrived(st_s3, 14)

        forward = base2 - turned_forward(2, 2, ((0, 0), (1, 1)), ref["s3p"])
        panel_forward(2, forward, ref["up2"])
        st = reduce_send(ref["up2"], ref["ur2"], 2)
        ref["fk"][2] = forward
        hand_over(0, 2, (forward[:, :128], forward[:, 128:]))
        arrived(st_z3, 12)
        for m in range(2, 8):
            into = ref["s3q"] if m < 4 else ref["s3r"]
            for i in range(2):
                into[m % 2 if m < 4 else m - 4, 2 * chip_y + i] = ref["uz3"][m, i]
        st_q3 = spread(ref["uz3"].at[pl.ds(2, 2)], ref["s3q"].at[:, pair], 4)
        prepare_inverse(1, 0, 32)
        arrived(st, 6)
        for i in range(2):
            ref["us2"][i] = reduced(ref["up2"], ref["ur2"], (i,))
        st_z2, st_z2b = stage.take(), stage.take()
        for m in (2, 3, 1):
            put(ref["us2"], ref["uz2"].at[m], st_z2, front ^ (8 * m))
        for m in range(4, 8):
            put(ref["us2"], ref["uz2b"].at[m - 4], st_z2b, front ^ (8 * m))
        drains.append((st_z2, 0, 6))
        drains.append((st_z2b, 0, 8))
        plane_gather(0)
        prepare_panel(1)
        arrived(st_rp[1], 24)
        base1 = dense_forward(1)
        turn_slots(1, 1, ((0, 0), (1, 2)))
        prepare_inverse(0, 0, 20)
        arrived(st_z2, 6)
        for i in range(2):
            own = ref["us2"][i] + ref["uz2"][1, i]
            other = ref["uz2"][2, i] + ref["uz2"][3, i]
            for h, total in ((0, own), (1, other)):
                ref["st2"][h, i] = total
                ref["s2p"][h, 2 * chip_y + i] = total
        st_s2 = spread(ref["st2"], ref["s2p"].at[:, pair], 4)
        arrived(st_q3, 12)
        for m in range(4):
            src = ref["s3p"].at[m] if m < 2 else ref["s3q"].at[m - 2]
            base1 = base1 - slots_forward(1, 2, m, lambda u, src=src: src[u])
        prepare_inverse(0, 20, 44)
        arrived(st_s2, 12)

        forward = base1 - turned_forward(1, 1, ((0, 0), (1, 2)), ref["s2p"])
        panel_forward(1, forward, ref["up1"])
        st = reduce_send(ref["up1"], ref["ur1"], 2)
        ref["fk"][1] = forward
        hand_over(0, 1, (forward[:, :128], forward[:, 128:]))
        arrived(st_z2b, 8)
        for i in range(2):
            for h in range(2):
                total = ref["uz2b"][2 * h, i] + ref["uz2b"][2 * h + 1, i]
                ref["st2b"][h, i] = total
                ref["s2q"][h, 2 * chip_y + i] = total
        st_q2 = spread(ref["st2b"], ref["s2q"].at[:, pair], 4)
        st_r3x = spread(ref["uz3"].at[pl.ds(4, 4)], ref["s3r"].at[:, pair], 8)
        prepare_inverse(0, 44, 64)
        turn_slots(0, 0, ((0, 0), (1, 4)))
        base0 = jnp.zeros((8, 256), F32)
        for h in range(2):
            base0 = base0 - slots_forward(0, 1, 2 * h, lambda u, h=h: ref["s2p"][h, u])
            base0 = base0 - slots_forward(0, 2, h, lambda u, h=h: ref["s3p"][h, u])
        arrived(st, 6)
        for i in range(2):
            ref["us1"][i] = reduced(ref["up1"], ref["ur1"], (i,))
        st_z1 = stage.take()
        for m in (4, 5, 3, 6, 2, 7, 1):
            put(ref["us1"], ref["uz1"].at[m], st_z1, front ^ (8 * m))
        drains.append((st_z1, 0, 14))
        for m in range(2):
            base0 = base0 - slots_forward(0, 2, m + 2, lambda u, m=m: ref["s3q"][m, u])
        arrived(st_rp[0], 48)
        base0 = base0 + dense_forward(0)
        arrived(st_z1, 14)
        for i in range(2):
            own = ref["us1"][i]
            for m in range(1, 4):
                own = own + ref["uz1"][m, i]
            other = ref["uz1"][4, i]
            for m in range(5, 8):
                other = other + ref["uz1"][m, i]
            for h, total in ((0, own), (1, other)):
                ref["st1"][h, i] = total
                ref["s1p"][h, 2 * chip_y + i] = total
        st_s1 = spread(ref["st1"], ref["s1p"].at[:, pair], 4)
        arrived(st_r3x, 24)
        base0 = lax.fori_loop(
            0, 4, lambda m, total: total - slots_forward(0, 2, m + 4, lambda u: ref["s3r"][m, u]), base0
        )
        arrived(st_q2, 12)
        for h in range(2):
            base0 = base0 - slots_forward(0, 1, 4 + 2 * h, lambda u, h=h: ref["s2q"][h, u])
        arrived(st_s1, 12)

        forward = base0 - turned_forward(0, 0, ((0, 0), (1, 4)), ref["s1p"])

        value2 = doubled(forward)
        for h in range(2):
            slots_backward(0, 0, 4 * h, value2, ref["a1"], h)
        st = reduce_send(ref["a1"], ref["ar1"], 4)
        hand_over(0, 0, (forward[:, :128], forward[:, 128:]))
        dense_backward(0, value2, 0, 7)
        arrived(st, 12)
        for h in range(2):
            for i in range(2):
                ref["as1"][h, i] = reduced(ref["a1"], ref["ar1"], (h, i))
        st_z = stage.take()
        for m in (4, 5, 3, 6, 2, 7, 1):
            put(ref["as1"].at[m >> 2], ref["az1"].at[m], st_z, front ^ (8 * m))
        drains.append((st_z, 0, 14))
        dense_backward(0, value2, 7, 8)

        def pick(t, planes, out, place, m, k):
            for u in range(SLOTS):
                tag = target(m, k, u)
                live = jnp.where((tag >> 6) == t, 1.0, 0.0).astype(F32)
                block = sd[t][(tag >> 1) & 3, (tag >> 3) & (planes - 1), tag & 1]
                out[u // 2, place, u % 2] = block * live

        for j in range(12):
            pick(0, 8, ref["n0"], j, 2 * j if j < 4 else j - 4, 1 if j < 4 else 2)
        st_n0 = reduce_send(ref["n0"], ref["nr0"], 24)
        arrived(st_z, 14)
        for i in range(2):
            total = ref["as1"][0, i]
            for m in range(1, 8):
                total = total + ref["az1"][m, i]
            ref["pt1"][i] = total
            ref["pk1"][2 * chip_y + i] = total
        st_p = spread(ref["pt1"], ref["pk1"].at[pair], 2)
        arrived(st_p, 6)

        value2 = doubled(ref["fk"][1] - panel_backward(1, ref["pk1"]))
        for h in range(2):
            slots_backward(1, 1, 2 * h, value2, ref["a2"], h)
        st = reduce_send(ref["a2"], ref["ar2"], 4)
        arrived(st_n0, 72)

        def background_sums(m, carry):
            for i in range(2):
                ref["ns0"][m, 0, i] = reduced(ref["n0"], ref["nr0"], (m // 2, i))
                ref["ns0"][m, 1, i] = reduced(ref["n0"], ref["nr0"], (4 + m, i))
            return carry

        lax.fori_loop(0, 8, background_sums, 0)
        st_nz0 = stage.take()
        for m in (4, 5, 3, 6, 2, 7, 1):
            put(ref["ns0"].at[m], ref["nz0"].at[m], st_nz0, front ^ (8 * m))
        drains.append((st_nz0, 0, 28))
        st_d0 = reduce_send(sd[0], ref["dr0"], 16)
        dense_backward(1, value2, 0, 4)
        for m in range(4):
            pick(1, 4, ref["n1"], m, m, 2)
        st_n1 = reduce_send(ref["n1"], ref["nr1"], 8)
        arrived(st, 12)
        for h in range(2):
            for i in range(2):
                ref["as2"][h, i] = reduced(ref["a2"], ref["ar2"], (h, i))
        st_z = stage.take()
        for m in (2, 3, 1):
            put(ref["as2"].at[m >> 1], ref["az2"].at[m], st_z, front ^ (8 * m))
        drains.append((st_z, 0, 6))
        st_d1 = reduce_send(sd[1], ref["dr1"], 8)

        def plane_totals(st_d, t, into, final, st_f):
            arrived(st_d, 6 * PLANES[t])
            for w in range(PLANES[t]):
                for c in range(2):
                    final[w, c] = reduced(sd[t], into, (w, c))

        arrived(st_nz0, 28)
        for q in range(2):
            for i in range(2):
                total = ref["ns0"][0, q, i]
                for m in range(1, 8):
                    total = total + ref["nz0"][m, q, i]
                ref["t0p"][q, i] = total
        arrived(st_z, 6)
        for i in range(2):
            total = ref["as2"][0, i] + ref["t0p"][0, i]
            for m in range(1, 4):
                total = total + ref["az2"][m, i]
            ref["pt2"][i] = total
            ref["pk2"][2 * chip_y + i] = total
        st_p = spread(ref["pt2"], ref["pk2"].at[pair], 2)
        arrived(st_n1, 24)
        for m in range(4):
            for i in range(2):
                ref["ns1"][m, i] = reduced(ref["n1"], ref["nr1"], (m, i))
        st_nz1 = stage.take()
        for m in (2, 3, 1):
            put(ref["ns1"].at[m], ref["nz1"].at[m], st_nz1, front ^ (8 * m))
        drains.append((st_nz1, 0, 6))
        plane_totals(st_d0, 0, ref["dr0"], ref["ds0"], None)
        st_dz0 = stage.take()
        for m in (4, 5, 3, 6, 2, 7, 1):
            put(ref["ds0"].at[z ^ m], ref["dz0"].at[m], st_dz0, front ^ (8 * m))
        drains.append((st_dz0, 0, 14))
        plane_totals(st_d1, 1, ref["dr1"], ref["ds1"], None)
        st_dz1 = stage.take()
        for m in (2, 3, 1):
            put(ref["ds1"].at[(z ^ m) % 4], ref["dz1"].at[m], st_dz1, front ^ (8 * m))
        drains.append((st_dz1, 0, 6))
        arrived(st_p, 6)

        value2 = doubled(ref["fk"][2] - panel_backward(2, ref["pk2"]))
        for h in range(2):
            slots_backward(2, 2, h, value2, ref["a3"], h)
        st = reduce_send(ref["a3"], ref["ar3"], 4)
        dense_backward(2, value2, 0, 2)
        st_d2 = stage.take()
        for mask in (12, 14, 10, 8, 4, 6, 2):
            put(
                sd[2].at[chip_y ^ ((mask >> 1) & 3), (z ^ (mask >> 3)) % 2],
                ref["dr2"].at[mask >> 1], st_d2, front ^ mask,
            )
        drains.append((st_d2, 0, 14))
        arrived(st_nz1, 6)
        for i in range(2):
            total = ref["ns1"][0, i] + ref["t0p"][1, i]
            for m in range(1, 4):
                total = total + ref["nz1"][m, i]
            ref["t1p"][i] = total
        arrived(st, 12)
        for i in range(2):
            ref["as3"][1, i] = reduced(ref["a3"], ref["ar3"], (1, i))
            total = ref["t1p"][i] + reduced(ref["a3"], ref["ar3"], (0, i))
            ref["as3"][0, i] = total
            ref["pk3"][0, 2 * chip_y + i] = total
        for mask in (12, 13, 10, 11, 14, 15, 8, 9):
            put(ref["as3"].at[1], ref["pk3"].at[1, pair], st_p3, front ^ mask)
        for mask in (4, 5, 2, 3, 6, 7, 1):
            put(ref["as3"].at[0], ref["pk3"].at[0, pair], st_p3, front ^ mask)
        arrived(st_dz0, 14)
        totals = []
        for c in range(2):
            total = ref["ds0"][z, c]
            for m in range(1, 8):
                total = total + ref["dz0"][m, c]
            totals.append(total)
        hand_over(1, 0, totals)
        arrived(st_dz1, 6)
        totals = []
        for c in range(2):
            total = ref["ds1"][z % 4, c]
            for m in range(1, 4):
                total = total + ref["dz1"][m, c]
            totals.append(total)
        hand_over(1, 1, totals)
        arrived(st_d2, 14)
        totals = []
        for c in range(2):
            total = sd[2][chip_y, z % 2, c]
            for m in range(1, 8):
                total = total + ref["dr2"][m, c]
            totals.append(total)
        hand_over(1, 2, totals)
        solved3 = third_total()
        arrived(st_gd, 128)
        split_combined()
        finish_sends(1)
        arrived(st_p3, 14)
        third_finish(solved3)
        drain(send_sem.at[st_p3], 30)

    assert stage.count <= STAGE_COUNT


def shards(right_side, inverse_top, inverse_second, inverse_third, inverse_fourth, panels, targets):
    anywhere = pl.BlockSpec(memory_space=pl.ANY)
    results = pl.pallas_call(
        kernel,
        out_shape=pltpu.VMEM((2,) + right_side.shape, F32),
        in_specs=[anywhere] * 7,
        out_specs=pl.BlockSpec(memory_space=pltpu.VMEM),
        scratch_shapes=[pltpu.VMEM(shape, dtype) for shape, dtype in SCRATCH.values()]
        + [
            pltpu.SMEM((8, 8, 128), I32),
            pltpu.SMEM((3, 1, 8), I32),
            pltpu.SemaphoreType.DMA((STAGE_COUNT,)),
            pltpu.SemaphoreType.DMA((STAGE_COUNT,)),
            pltpu.SemaphoreType.DMA((12,)),
        ],
        compiler_params=pltpu.CompilerParams(
            collective_id=0, has_side_effects=True, vmem_limit_bytes=56 * 2**20
        ),
        name="tiers",
    )(right_side, inverse_top, inverse_second, inverse_third, inverse_fourth, panels, targets)
    return results[0], results[1]


def solution(mesh):
    placed = (
        P("rhs", None, "front"),
        P("front", None),
        P("front", None),
        P("front", None),
        P("front", None),
        P(None, None, "front"),
        P(None, "front", None),
    )
    return jax.shard_map(
        shards,
        mesh=mesh,
        in_specs=placed,
        out_specs=(P("rhs", None, "front"), P("rhs", None, "front")),
        check_vma=False,
    )
```
